32 devices in a mesh: freq: 2 (over x), tile: 16 (over z, y, core).
Axes of the slice: x: 2, y: 2, z: 4, core: 2. Of those that a mesh axis runs over, the one named last changes fastest.
Arguments:
- spectra: bfloat16 [2, 128, 256, 2048], P(None, None, 'freq', 'tile'), may hold values from -450 to 450
- seg_mask: int32 [128, 2048], P(None, 'tile'), may hold values 0 or 1
Outputs:
- coherence: bfloat16 [16, 2, 256, 128, 128], P('tile', None, None, 'freq')
The draws below stay inside these ranges and needn't reach their ends.
All inputs are finite; a program needn't handle non-finite values. No bound on the sum of `seg_mask` on one device may be relied on, other than what follows from the above.
Results may differ from the reference program's by a relative error of at most 0.012.
The reference program's roundings to bfloat16 on the way count: a program that leaves them out, or rounds other values in their place, can miss the bound.
Values may be sent and summed in bfloat16 or wider, within the bound.
No kernel may reach another device: no remote copies, remote signals or barrier semaphores. Data moves between devices by JAX's collectives and lax.ppermute only.
A program may use at most 128 MiB of HBM per device.

```python
import math
import jax
import jax.numpy as jnp
from jax import lax

BLK = 128
F = 256
SEG = 128
LAGS = 512
CH = 2048
N_TILE = 16


def draw_spectra(key, part):
    key_base = jax.random.fold_in(key, 0)
    key_rough = jax.random.fold_in(key, 2)
    key_chan = jax.random.fold_in(key, 3)
    freq_pos = jnp.arange(F, dtype=jnp.float32) / (F - 1)
    base = jax.random.truncated_normal(key_base, -4.0, 4.0, (2, SEG, F, CH), jnp.float32)
    rough = jnp.exp(jax.random.uniform(key_rough, (F,), jnp.float32, -0.5, 0.5))
    freq_scale = jnp.power(10.0, freq_pos) * rough
    chan_scale = jnp.exp(jax.random.uniform(key_chan, (CH,), jnp.float32, 0.0, math.log(3.0)))
    return (base * freq_scale[None, None, :, None] * chan_scale[None, None, None, :]).astype(jnp.bfloat16)


def place_ends(result, rng, least, largest):
    longest = result.shape.index(max(result.shape))
    spots = []
    for shift in (0, 1):
        where = [jax.random.randint(jax.random.fold_in(rng, axis), (), 0, length) for axis, length in enumerate(result.shape)]
        where[longest] = (where[longest] + shift) % result.shape[longest]
        spots.append(tuple(where))
    return result.at[spots[0]].set(least).at[spots[1]].set(largest)


def setup_inputs(seed: int = 0) -> dict:
    arg_keys = jax.random.split(jax.random.key(seed), 3)
    return {
        "spectra": draw_spectra(jax.random.fold_in(arg_keys[2], 71), 0),
        "seg_mask": place_ends((jax.random.randint(arg_keys[1], (SEG, CH), 0, 4) < 3).astype(jnp.int32), jax.random.fold_in(arg_keys[1], 1), 0, 1),
    }


WATER = 0.05

def dft_tables(lag_count, freq_count):
    lag_index = jnp.arange(lag_count, dtype=jnp.int32)[:, None]
    freq_index = jnp.arange(freq_count, dtype=jnp.int32)[None, :]
    phase = (lag_index * freq_index % lag_count).astype(jnp.float32) * (2.0 * math.pi / lag_count)
    return (jnp.cos(phase).astype(jnp.bfloat16), jnp.sin(phase).astype(jnp.bfloat16))

def cross_gram(first, second):
    real_part = jnp.einsum('sfa,sfb->fab', first[0], second[0]) + jnp.einsum('sfa,sfb->fab', first[1], second[1])
    imag_part = jnp.einsum('sfa,sfb->fab', first[0], second[1]) - jnp.einsum('sfa,sfb->fab', first[1], second[0])
    return (real_part / SEG, imag_part / SEG)

def reference(spectra, seg_mask):
    tile_count = N_TILE
    half_axis = tile_count // 2
    masked = spectra * seg_mask.astype(jnp.bfloat16)[None, :, None, :]
    power = lax.optimization_barrier(jnp.sum(jnp.square(masked.astype(jnp.float32)), axis=(0, 1))) / SEG + 1e-05
    weight = power + WATER * lax.optimization_barrier(jnp.mean(power, axis=0))[None, :]
    cos_tab, sin_tab = dft_tables(LAGS, F)
    cos_wide = cos_tab.astype(jnp.float32)
    sin_wide = sin_tab.astype(jnp.float32)
    norm_scale = 1.0 / math.sqrt(LAGS)

    def one_tile(tile_idx):
        first = (tile_idx * BLK).astype(jnp.int32)
        second = ((tile_idx + half_axis) % tile_count * BLK).astype(jnp.int32)
        src_block = lax.dynamic_slice_in_dim(masked, first, BLK, 3).astype(jnp.float32)
        rcv_block = lax.dynamic_slice_in_dim(masked, second, BLK, 3).astype(jnp.float32)
        src_weight = lax.dynamic_slice_in_dim(weight, first, BLK, 1)
        rcv_weight = lax.dynamic_slice_in_dim(weight, second, BLK, 1)
        cab_re, cab_im = cross_gram(src_block, rcv_block)
        cba_re, cba_im = cross_gram(rcv_block, src_block)
        dab_re = (cab_re / src_weight[:, :, None]).astype(jnp.bfloat16).astype(jnp.float32)
        dab_im = (cab_im / src_weight[:, :, None]).astype(jnp.bfloat16).astype(jnp.float32)
        dba_re = (cba_re / rcv_weight[:, :, None]).astype(jnp.bfloat16).astype(jnp.float32)
        dba_im = (cba_im / rcv_weight[:, :, None]).astype(jnp.bfloat16).astype(jnp.float32)
        sym_re = (0.5 * (dab_re + jnp.swapaxes(dba_re, 1, 2))).astype(jnp.bfloat16)
        sym_im = (0.5 * (dab_im - jnp.swapaxes(dba_im, 1, 2))).astype(jnp.bfloat16)
        real_flat = sym_re.reshape(F, BLK * BLK).astype(jnp.float32)
        imag_flat = sym_im.reshape(F, BLK * BLK).astype(jnp.float32)
        lag_re = jnp.dot(cos_wide, real_flat, preferred_element_type=jnp.float32) - jnp.dot(sin_wide, imag_flat, preferred_element_type=jnp.float32)
        lag_im = jnp.dot(sin_wide, real_flat, preferred_element_type=jnp.float32) + jnp.dot(cos_wide, imag_flat, preferred_element_type=jnp.float32)
        energy = lag_re * lag_re + lag_im * lag_im
        mean_energy = lax.optimization_barrier(jnp.mean(energy, axis=0, keepdims=True))
        phase_part = (lag_re / jnp.sqrt(energy + 0.25 * mean_energy + 1e-05)).astype(jnp.bfloat16).astype(jnp.float32)
        out_re = jnp.dot(cos_wide.T, phase_part, preferred_element_type=jnp.float32) * norm_scale
        out_im = -jnp.dot(sin_wide.T, phase_part, preferred_element_type=jnp.float32) * norm_scale
        return jnp.stack([out_re, out_im], axis=0).astype(jnp.bfloat16).reshape(2, F, BLK, BLK)
    return lax.map(one_tile, jnp.arange(tile_count, dtype=jnp.int32))
```

```python
import functools
import math

import jax
import jax.numpy as jnp
from jax import lax
from jax.experimental import pallas as pl
from jax.experimental.pallas import tpu as pltpu
from jax.sharding import PartitionSpec as P

F = 256
LAGS = 512
WATER = 0.05
SUB = 16
VMEM_BYTES = 48 * 2**20


def dft_tables(freq_index):
    lag_index = jnp.arange(LAGS, dtype=jnp.int32)[:, None]
    phase = (lag_index * freq_index[None, :] % LAGS).astype(jnp.float32) * (2.0 * math.pi / LAGS)
    return jnp.cos(phase).astype(jnp.bfloat16), jnp.sin(phase).astype(jnp.bfloat16)


def rounded(x):
    return x.astype(jnp.bfloat16).astype(jnp.float32)


def cross_kernel(piece, freq_count, rows, groups, held, me_ref, own_ref, far_ref, own_inv_ref, far_inv_ref, *refs):
    outs, (own_scr, far_scr) = refs[held:-2], refs[-2:]
    seg = own_ref.shape[2]
    block = own_ref.shape[3]
    for f in range(SUB):
        own = own_ref[f].reshape(2 * seg, block)
        far_re, far_im = far_ref[f, 0], far_ref[f, 1]
        cols = jnp.concatenate(
            [jnp.concatenate([far_re, far_im], axis=0), jnp.concatenate([far_im, -far_re], axis=0)], axis=1
        )
        cross = lax.dot_general(own, cols, (((0,), (0,)), ((), ())), preferred_element_type=jnp.float32)
        at = piece * SUB + f
        own_inv = own_inv_ref[:, at : at + 1]
        far_inv = far_inv_ref[at : at + 1, :]
        for part in range(2):
            val = cross[:, part * block : (part + 1) * block]
            sym = rounded(0.5 * (rounded(val * own_inv) + rounded(val * far_inv)))
            spot = pl.ds(part * SUB + f, block, stride=2 * SUB)
            own_scr[spot, :] = sym
            turned = jnp.transpose(sym)
            far_scr[spot, :] = turned if part == 0 else -turned
    me = me_ref[0]
    group_rows = rows * groups
    for which, scr in enumerate((own_scr, far_scr)):
        for d in range(freq_count):
            for j in range(groups):
                first = (lax.rem(me + d, freq_count) * group_rows + j * rows) * (2 * SUB)
                vals = scr[pl.ds(pl.multiple_of(first, 2 * SUB), rows * 2 * SUB), :]
                outs[(which * freq_count + d) * groups + j][...] = vals.reshape(rows, 2, SUB, block).astype(jnp.bfloat16)


def cross_piece(piece, freq_count, rows, groups, me, own, far, own_inv, far_inv, before):
    half, _, seg, block = own.shape
    n_out = 2 * freq_count * groups
    out_shape = [jax.ShapeDtypeStruct((rows, 2, half, block), jnp.bfloat16)] * n_out
    held = len(before)
    return pl.pallas_call(
        functools.partial(cross_kernel, piece, freq_count, rows, groups, held),
        grid=(1,),
        in_specs=[
            pl.BlockSpec(memory_space=pltpu.SMEM),
            pl.BlockSpec((SUB, 2, seg, block), lambda i: (piece, 0, 0, 0)),
            pl.BlockSpec((SUB, 2, seg, block), lambda i: (0, 0, 0, 0)),
            pl.BlockSpec((block, half), lambda i: (0, 0)),
            pl.BlockSpec((half, block), lambda i: (0, 0)),
        ]
        + [pl.BlockSpec(memory_space=pl.ANY)] * held,
        out_specs=[pl.BlockSpec((rows, 2, SUB, block), lambda i: (0, 0, piece, 0))] * n_out,
        out_shape=out_shape,
        scratch_shapes=[pltpu.VMEM((block * 2 * SUB, block), jnp.float32)] * 2,
        input_output_aliases={5 + i: i for i in range(held)},
        compiler_params=pltpu.CompilerParams(vmem_limit_bytes=VMEM_BYTES),
        cost_estimate=pl.CostEstimate(
            flops=SUB * 8 * seg * block * block, bytes_accessed=SUB * 16 * seg * block, transcendentals=0
        ),
        name="cross_piece",
    )(me, own, far, own_inv, far_inv, *before)


def lag_kernel(n_pieces, rows, held, lag_ref, back_ref, *refs):
    pieces, out_ref, scr = refs[:n_pieces], refs[n_pieces + held], refs[-1]
    block = scr.shape[1]
    half = pieces[0].shape[2]
    bins = out_ref.shape[2]

    def two_rows(r, _):
        cols = jnp.concatenate(
            [
                jnp.concatenate([piece[2 * r + k].reshape(2 * half, block) for piece in pieces], axis=0)
                for k in range(2)
            ],
            axis=1,
        )
        lag = jnp.dot(lag_ref[...], cols, preferred_element_type=jnp.float32)
        lag_re, lag_im = lag[:LAGS], lag[LAGS:]
        energy = lag_re * lag_re + lag_im * lag_im
        floor = (0.25 / LAGS) * jnp.sum(energy, axis=0, keepdims=True) + 1e-05
        normalized = (lag_re * lax.rsqrt(energy + floor)).astype(jnp.bfloat16)
        back = jnp.dot(back_ref[...], normalized, preferred_element_type=jnp.float32) * (1.0 / math.sqrt(LAGS))
        for k in range(2):
            scr[pl.ds(2 * r + k, 2 * bins, stride=rows), :] = back[:, k * block : (k + 1) * block]
        return 0

    lax.fori_loop(0, rows // 2, two_rows, 0)
    out_ref[...] = scr[...].reshape(out_ref.shape).astype(jnp.bfloat16)


def lag_group(group, groups, lag_table, back_table, pieces, before):
    rows, _, half, block = pieces[0].shape
    held = len(before)
    bins = back_table.shape[0] // 2
    return pl.pallas_call(
        functools.partial(lag_kernel, len(pieces), rows, held),
        grid=(1,),
        in_specs=[pl.BlockSpec(lag_table.shape, lambda i: (0, 0)), pl.BlockSpec(back_table.shape, lambda i: (0, 0))]
        + [pl.BlockSpec((rows, 2, half, block), lambda i: (0, 0, 0, 0))] * len(pieces)
        + [pl.BlockSpec(memory_space=pl.ANY)] * held,
        out_specs=pl.BlockSpec((1, 2, bins, rows, block), lambda i: (0, 0, 0, group, 0)),
        out_shape=jax.ShapeDtypeStruct((1, 2, bins, rows * groups, block), jnp.bfloat16),
        scratch_shapes=[pltpu.VMEM((2 * bins * rows, block), jnp.float32)],
        input_output_aliases={2 + len(pieces): 0} if held else {},
        compiler_params=pltpu.CompilerParams(vmem_limit_bytes=VMEM_BYTES),
        cost_estimate=pl.CostEstimate(
            flops=rows * block * 2 * LAGS * 6 * F, bytes_accessed=rows * block * 16 * F, transcendentals=rows * block * LAGS
        ),
        name="lag_group",
    )(lag_table, back_table, *pieces, *before)


def shards(spectra, seg_mask):
    tile_count, freq_count = lax.axis_size("tile"), lax.axis_size("freq")
    half_axis = tile_count // 2
    _, seg, band, block = spectra.shape
    half = band // 2
    n_sub = half // SUB
    rows = min(SUB, block // freq_count)
    groups = block // freq_count // rows
    me = lax.axis_index("freq")
    side = lax.axis_index("tile") // half_axis
    keep_from, send_from = side * half, (1 - side) * half
    mask = seg_mask.astype(jnp.bfloat16)[None, :, None, :]

    across = [(t, (t + half_axis) % tile_count) for t in range(tile_count)]

    def along(block, d, cross):
        route = []
        for h in range(freq_count):
            for t in range(tile_count):
                there = (t + half_axis * cross) % tile_count
                route.append((h * tile_count + t, (h + d) % freq_count * tile_count + there))
        return lax.ppermute(block, ("freq", "tile"), route)

    def masked_part(first, count):
        part = lax.dynamic_slice_in_dim(spectra, first, count, 2) * mask
        return jnp.transpose(part, (2, 0, 1, 3))

    far = []
    for i in range(n_sub):
        piece = masked_part(send_from + i * SUB, SUB)
        if i >= 2:
            piece, far[i - 2] = lax.optimization_barrier((piece, far[i - 2]))
        far.append(lax.ppermute(piece, "tile", across))
    own = masked_part(keep_from, half)

    power = jnp.sum(jnp.square((spectra * mask).astype(jnp.float32)), axis=(0, 1)) / seg + 1e-05
    total = lax.psum(jnp.sum(power, axis=0), "freq")
    inverse = 1.0 / ((power + WATER * (total / F)[None, :]) * seg)
    own_inv = lax.dynamic_slice_in_dim(inverse, keep_from, half, 0).T
    far_inv = lax.ppermute(lax.dynamic_slice_in_dim(inverse, send_from, half, 0), "tile", across)

    me_arr = me.astype(jnp.int32).reshape(1)
    sym = []
    for i in range(n_sub):
        sym = cross_piece(i, freq_count, rows, groups, me_arr, own, far[i], own_inv, far_inv, sym)

    def own_sym(d, j):
        return sym[d * groups + j]

    def far_sym(d, j):
        return sym[(freq_count + d) * groups + j]

    local = jnp.arange(half, dtype=jnp.int32)
    order = []
    for mine in (True, False):
        for d in range(freq_count):
            order.append((me - d) % freq_count * band + (keep_from if mine else send_from) + local)
    lag_cols = []
    for freqs in order:
        cos_tab, sin_tab = dft_tables(freqs)
        lag_cols.append(jnp.concatenate([cos_tab, sin_tab], axis=0))
        lag_cols.append(jnp.concatenate([-sin_tab, cos_tab], axis=0))
    lag_table = jnp.concatenate(lag_cols, axis=1)
    cos_tab, sin_tab = dft_tables(jnp.arange(F, dtype=jnp.int32))
    back_table = jnp.concatenate([cos_tab, -sin_tab], axis=1).T

    arrived = []
    for j in range(groups):
        outgoing = [own_sym(d, j) for d in range(1, freq_count)] + [far_sym(d, j) for d in range(freq_count)]
        if j >= 2:
            outgoing, arrived[j - 2] = lax.optimization_barrier((outgoing, arrived[j - 2]))
        arrived.append(
            [along(outgoing[d - 1], d, 0) for d in range(1, freq_count)]
            + [along(outgoing[freq_count - 1 + d], d, 1) for d in range(freq_count)]
        )
    out = []
    for j in range(groups):
        out = [lag_group(j, groups, lag_table, back_table, [own_sym(0, j)] + arrived[j], out)]
    return out[0]


def solution(mesh):
    placed = (P(None, None, "freq", "tile"), P(None, "tile"))
    return jax.shard_map(
        shards,
        mesh=mesh,
        in_specs=placed,
        out_specs=P("tile", None, None, "freq", None),
        check_vma=False,
    )
```

```python
import functools
import math

import jax
import jax.numpy as jnp
from jax import lax
from jax.experimental import pallas as pl
from jax.experimental.pallas import tpu as pltpu
from jax.sharding import PartitionSpec as P

F = 256
LAGS = 512
WATER = 0.05
SUB = 16
PIECE = 8
DEPTH = 3
VMEM_BYTES = 48 * 2**20


def dft_tables(freq_index):
    lag_index = jnp.arange(LAGS, dtype=jnp.int32)[:, None]
    phase = (lag_index * freq_index[None, :] % LAGS).astype(jnp.float32) * (2.0 * math.pi / LAGS)
    return jnp.cos(phase).astype(jnp.bfloat16), jnp.sin(phase).astype(jnp.bfloat16)


def rounded(x):
    return x.astype(jnp.bfloat16).astype(jnp.float32)


def cross_kernel(piece, freq_count, rows, groups, held, n_far, me_ref, own_ref, own_inv_ref, far_inv_ref, *refs):
    far_refs, outs, (own_scr, far_scr) = refs[:n_far], refs[n_far + held : -2], refs[-2:]
    seg = own_ref.shape[2]
    block = own_ref.shape[3]
    per_far = SUB // n_far
    for f in range(SUB):
        own = own_ref[f].reshape(2 * seg, block)
        far_ref = far_refs[f // per_far]
        far_re, far_im = far_ref[f % per_far, 0], far_ref[f % per_far, 1]
        cols = jnp.concatenate(
            [jnp.concatenate([far_re, far_im], axis=0), jnp.concatenate([far_im, -far_re], axis=0)], axis=1
        )
        cross = lax.dot_general(own, cols, (((0,), (0,)), ((), ())), preferred_element_type=jnp.float32)
        at = piece * SUB + f
        own_inv = own_inv_ref[:, at : at + 1]
        far_inv = far_inv_ref[at : at + 1, :]
        for part in range(2):
            val = cross[:, part * block : (part + 1) * block]
            sym = rounded(0.5 * (rounded(val * own_inv) + rounded(val * far_inv)))
            spot = pl.ds(part * SUB + f, block, stride=2 * SUB)
            own_scr[spot, :] = sym
            turned = jnp.transpose(sym)
            far_scr[spot, :] = turned if part == 0 else -turned
    me = me_ref[0]
    group_rows = rows * groups
    for which, scr in enumerate((own_scr, far_scr)):
        for d in range(freq_count):
            for j in range(groups):
                first = (lax.rem(me + d, freq_count) * group_rows + j * rows) * (2 * SUB)
                vals = scr[pl.ds(pl.multiple_of(first, 2 * SUB), rows * 2 * SUB), :]
                outs[(which * freq_count + d) * groups + j][...] = vals.reshape(rows, 2, SUB, block).astype(jnp.bfloat16)


def cross_piece(piece, freq_count, rows, groups, places, me, own, far, own_inv, far_inv, before):
    half, _, seg, block = own.shape
    n_far = len(far)
    outputs = [(k, j) for k in range(2 * freq_count) for j in range(groups)]
    spots = [n for n, (_, j) in enumerate(outputs) if places[j][2]]
    held = [before[outputs[n][0]][outputs[n][1]] for n in spots]
    flat = pl.pallas_call(
        functools.partial(cross_kernel, piece, freq_count, rows, groups, len(held), n_far),
        grid=(1,),
        in_specs=[
            pl.BlockSpec(memory_space=pltpu.SMEM),
            pl.BlockSpec((SUB, 2, seg, block), lambda i: (piece, 0, 0, 0)),
            pl.BlockSpec((block, half), lambda i: (0, 0)),
            pl.BlockSpec((half, block), lambda i: (0, 0)),
        ]
        + [pl.BlockSpec((SUB // n_far, 2, seg, block), lambda i: (0, 0, 0, 0))] * n_far
        + [pl.BlockSpec(memory_space=pl.ANY)] * len(held),
        out_specs=[
            pl.BlockSpec((rows, 2, SUB, block), functools.partial(lambda at, i: (0, 0, at, 0), places[j][1]))
            for _, j in outputs
        ],
        out_shape=[jax.ShapeDtypeStruct((rows, 2, places[j][0], block), jnp.bfloat16) for _, j in outputs],
        scratch_shapes=[pltpu.VMEM((block * 2 * SUB, block), jnp.float32)] * 2,
        input_output_aliases={4 + n_far + i: n for i, n in enumerate(spots)},
        compiler_params=pltpu.CompilerParams(vmem_limit_bytes=VMEM_BYTES),
        cost_estimate=pl.CostEstimate(
            flops=SUB * 8 * seg * block * block, bytes_accessed=SUB * 16 * seg * block, transcendentals=0
        ),
        name="cross_piece",
    )(me, own, own_inv, far_inv, *far, *held)
    return [flat[k * groups : (k + 1) * groups] for k in range(2 * freq_count)]


def lag_kernel(sources, rows, held, lag_ref, back_ref, *refs):
    n_pieces = sum(sources)
    pieces, out_ref, scr = refs[:n_pieces], refs[n_pieces + held], refs[-1]
    block = scr.shape[1]
    bins = out_ref.shape[2]

    def column(r):
        parts, at = [], 0
        for count in sources:
            for part in range(2):
                parts += [piece[r, part] for piece in pieces[at : at + count]]
            at += count
        return jnp.concatenate(parts, axis=0)

    for r in range(0, rows, 2):
        cols = jnp.concatenate([column(r), column(r + 1)], axis=1)
        lag = jnp.dot(lag_ref[...], cols, preferred_element_type=jnp.float32)
        lag_re, lag_im = lag[:LAGS], lag[LAGS:]
        energy = lag_re * lag_re + lag_im * lag_im
        floor = (0.25 / LAGS) * jnp.sum(energy, axis=0, keepdims=True) + 1e-05
        normalized = (lag_re * lax.rsqrt(energy + floor)).astype(jnp.bfloat16)
        back = jnp.dot(back_ref[...], normalized, preferred_element_type=jnp.float32) * (1.0 / math.sqrt(LAGS))
        for k in range(2):
            scr[pl.ds(r + k, 2 * bins, stride=rows), :] = back[:, k * block : (k + 1) * block]
    out_ref[...] = scr[...].reshape(out_ref.shape).astype(jnp.bfloat16)


def lag_group(group, groups, lag_table, back_table, sources, before):
    pieces = [piece for source in sources for piece in source]
    rows, _, _, block = pieces[0].shape
    held = len(before)
    bins = back_table.shape[0] // 2
    return pl.pallas_call(
        functools.partial(lag_kernel, [len(source) for source in sources], rows, held),
        grid=(1,),
        in_specs=[pl.BlockSpec(lag_table.shape, lambda i: (0, 0)), pl.BlockSpec(back_table.shape, lambda i: (0, 0))]
        + [pl.BlockSpec(piece.shape, lambda i: (0, 0, 0, 0)) for piece in pieces]
        + [pl.BlockSpec(memory_space=pl.ANY)] * held,
        out_specs=pl.BlockSpec((1, 2, bins, rows, block), lambda i: (0, 0, 0, group, 0)),
        out_shape=jax.ShapeDtypeStruct((1, 2, bins, rows * groups, block), jnp.bfloat16),
        scratch_shapes=[pltpu.VMEM((2 * bins * rows, block), jnp.float32)],
        input_output_aliases={2 + len(pieces): 0} if held else {},
        compiler_params=pltpu.CompilerParams(vmem_limit_bytes=VMEM_BYTES),
        cost_estimate=pl.CostEstimate(
            flops=rows * block * 2 * LAGS * 6 * F, bytes_accessed=rows * block * 16 * F, transcendentals=rows * block * LAGS
        ),
        name="lag_group",
    )(lag_table, back_table, *pieces, *before)


def shards(spectra, seg_mask):
    tile_count, freq_count = lax.axis_size("tile"), lax.axis_size("freq")
    half_axis = tile_count // 2
    _, seg, band, block = spectra.shape
    half = band // 2
    n_sub = half // SUB
    rows = min(SUB, block // freq_count)
    groups = block // freq_count // rows
    me = lax.axis_index("freq")
    side = lax.axis_index("tile") // half_axis
    keep_from, send_from = side * half, (1 - side) * half
    mask = seg_mask.astype(jnp.bfloat16)[None, :, None, :]

    across = [(t, (t + half_axis) % tile_count) for t in range(tile_count)]

    def along(block, d, cross):
        route = []
        for h in range(freq_count):
            for t in range(tile_count):
                there = (t + half_axis * cross) % tile_count
                route.append((h * tile_count + t, (h + d) % freq_count * tile_count + there))
        return lax.ppermute(block, ("freq", "tile"), route)

    def masked_part(whole, first, count):
        part = lax.dynamic_slice_in_dim(whole, first, count, 2) * mask
        return jnp.transpose(part, (2, 0, 1, 3))

    n_far = half // PIECE
    first_piece = masked_part(spectra, send_from, PIECE)
    later, first_piece = lax.optimization_barrier((spectra, first_piece))
    pieces = [first_piece] + [masked_part(later, send_from + i * PIECE, PIECE) for i in range(1, n_far)]
    rest, pieces = lax.optimization_barrier((later, pieces))
    far = []
    for i in range(n_far):
        piece = pieces[i]
        if i >= DEPTH:
            piece, far[i - DEPTH] = lax.optimization_barrier((piece, far[i - DEPTH]))
        far.append(lax.ppermute(piece, "tile", across))
    rest, far[0] = lax.optimization_barrier((rest, far[0]))
    own = masked_part(rest, keep_from, half)

    power = jnp.sum(jnp.square((rest * mask).astype(jnp.float32)), axis=(0, 1)) / seg + 1e-05
    total = lax.psum(jnp.sum(power, axis=0), "freq")
    inverse = 1.0 / ((power + WATER * (total / F)[None, :]) * seg)
    own_inv = lax.dynamic_slice_in_dim(inverse, keep_from, half, 0).T
    far_inv = lax.ppermute(lax.dynamic_slice_in_dim(inverse, send_from, half, 0), "tile", across)

    n_split = groups // 2 if n_sub > 1 else 0
    me_arr = me.astype(jnp.int32).reshape(1)
    per_sub = SUB // PIECE
    early, sym = None, None
    for i in range(n_sub):
        last = i == n_sub - 1
        if last:
            early = sym
            split = (SUB, 0, False)
        else:
            split = (half - SUB, i, i > 0)
        places = [split if j < n_split else (half, i, i > 0) for j in range(groups)]
        sym = cross_piece(
            i, freq_count, rows, groups, places, me_arr, own, far[i * per_sub : (i + 1) * per_sub], own_inv, far_inv, sym
        )

    local = jnp.arange(half, dtype=jnp.int32)
    lag_cols = []
    for mine in (True, False):
        for d in range(freq_count):
            freqs = (me - d) % freq_count * band + (keep_from if mine else send_from) + local
            cos_tab, sin_tab = dft_tables(freqs)
            lag_cols.append(jnp.concatenate([cos_tab, sin_tab], axis=0))
            lag_cols.append(jnp.concatenate([-sin_tab, cos_tab], axis=0))
    lag_table = jnp.concatenate(lag_cols, axis=1)
    cos_tab, sin_tab = dft_tables(jnp.arange(F, dtype=jnp.int32))
    back_table = jnp.concatenate([cos_tab, -sin_tab], axis=1).T

    stages = [(j, True) for j in range(n_split)] + [(j, False) for j in range(groups)]
    ahead = 2 * n_split or 2
    arrived = {}
    for n, (j, is_early) in enumerate(stages):
        made = early if is_early else sym
        outgoing = [made[k][j] for k in range(1, 2 * freq_count)]
        if n >= ahead:
            waited = stages[n - ahead]
            outgoing, arrived[waited] = lax.optimization_barrier((outgoing, arrived[waited]))
        arrived[j, is_early] = [along(outgoing[k - 1], k % freq_count, k // freq_count) for k in range(1, 2 * freq_count)]
    out = []
    for j in range(groups):
        parts = ([(early, True)] if j < n_split else []) + [(sym, False)]
        sources = [
            [made[0][j] if k == 0 else arrived[j, is_early][k - 1] for made, is_early in parts]
            for k in range(2 * freq_count)
        ]
        out = [lag_group(j, groups, lag_table, back_table, sources, out)]
    return out[0]


def solution(mesh):
    placed = (P(None, None, "freq", "tile"), P(None, "tile"))
    return jax.shard_map(
        shards,
        mesh=mesh,
        in_specs=placed,
        out_specs=P("tile", None, None, "freq", None),
        check_vma=False,
    )
```

```python
import functools
import math

import jax
import jax.numpy as jnp
from jax import lax
from jax.experimental import pallas as pl
from jax.experimental.pallas import tpu as pltpu
from jax.sharding import PartitionSpec as P

F = 256
LAGS = 512
WATER = 0.05
SUB = 16
SHORT = 4
DEPTH = 3
VMEM_BYTES = 48 * 2**20


def dft_tables(freq_index):
    lag_index = jnp.arange(LAGS, dtype=jnp.int32)[:, None]
    phase = (lag_index * freq_index[None, :] % LAGS).astype(jnp.float32) * (2.0 * math.pi / LAGS)
    return jnp.cos(phase).astype(jnp.bfloat16), jnp.sin(phase).astype(jnp.bfloat16)


def rounded(x):
    return x.astype(jnp.bfloat16).astype(jnp.float32)


def interleave():
    row = lax.broadcasted_iota(jnp.int32, (SUB * SUB, SUB * SUB), 0)
    col = lax.broadcasted_iota(jnp.int32, (SUB * SUB, SUB * SUB), 1)
    return jnp.where(col == row % SUB * SUB + row // SUB, 1.0, 0.0).astype(jnp.bfloat16)


def turned_rows(matrix, left, right):
    lanes = left.shape[2]
    both = jnp.concatenate([left.reshape(SUB * SUB, lanes), right.reshape(SUB * SUB, lanes)], axis=1)
    return jnp.dot(matrix, both, preferred_element_type=jnp.float32).reshape(SUB, SUB, 2 * lanes)


def prepare_kernel(at_ref, x_ref, mask_ref, *outs):
    parts, power_ref = outs[:-1], outs[-1]
    seg, lanes = mask_ref.shape
    matrix = interleave()
    total = jnp.zeros((SUB, 8, lanes), jnp.float32)
    for s in range(0, seg, SUB):
        mask = mask_ref[s : s + SUB].astype(jnp.float32)[None]
        turned = turned_rows(matrix, x_ref[0, s : s + SUB], x_ref[1, s : s + SUB])
        for part in range(2):
            val = turned[:, :, part * lanes : (part + 1) * lanes] * mask
            square = val * val
            total += square[:, :8] + square[:, 8:]
            at = 0
            for out in parts:
                count = out.shape[0]
                out[:, part, s : s + SUB] = val[at : at + count].astype(jnp.bfloat16)
                at += count
    power_ref[...] = jnp.sum(total, axis=1) * (1.0 / seg) + 1e-05


def prepare(spectra, seg_mask, first, steps, counts):
    _, seg, _, block = spectra.shape
    assert sum(counts) == steps * SUB and (steps == 1 or len(counts) == 1)
    out_specs = [pl.BlockSpec((min(count, SUB), 2, seg, block), lambda i, at: (i, 0, 0, 0)) for count in counts]
    out_shape = [jax.ShapeDtypeStruct((count, 2, seg, block), jnp.bfloat16) for count in counts]
    return pl.pallas_call(
        prepare_kernel,
        grid_spec=pltpu.PrefetchScalarGridSpec(
            num_scalar_prefetch=1,
            grid=(steps,),
            in_specs=[
                pl.BlockSpec((2, seg, SUB, block), lambda i, at: (0, 0, at[0] + i, 0)),
                pl.BlockSpec((seg, block), lambda i, at: (0, 0)),
            ],
            out_specs=out_specs + [pl.BlockSpec((SUB, block), lambda i, at: (i, 0))],
        ),
        out_shape=out_shape + [jax.ShapeDtypeStruct((steps * SUB, block), jnp.float32)],
        compiler_params=pltpu.CompilerParams(vmem_limit_bytes=VMEM_BYTES),
        cost_estimate=pl.CostEstimate(
            flops=steps * SUB * seg * block * 8, bytes_accessed=steps * SUB * seg * block * 8, transcendentals=0
        ),
        name="prepare",
    )(first.astype(jnp.int32).reshape(1), spectra, seg_mask)


def cross_kernel(piece, freq_count, groups, held, n_far, me_ref, own_ref, own_inv_ref, far_inv_ref, *refs):
    far_refs, outs, (own_scr, far_scr) = refs[:n_far], refs[n_far + held : -2], refs[-2:]
    seg = own_ref.shape[2]
    block = own_ref.shape[3]
    far_rows = [(far_ref, k) for far_ref in far_refs for k in range(far_ref.shape[0])]
    for f in range(SUB):
        own = own_ref[f].reshape(2 * seg, block)
        far_ref, k = far_rows[f]
        far_re, far_im = far_ref[k, 0], far_ref[k, 1]
        cols = jnp.concatenate(
            [jnp.concatenate([far_re, far_im], axis=0), jnp.concatenate([far_im, -far_re], axis=0)], axis=1
        )
        cross = lax.dot_general(own, cols, (((0,), (0,)), ((), ())), preferred_element_type=jnp.float32)
        at = piece * SUB + f
        own_inv = own_inv_ref[:, at : at + 1]
        far_inv = far_inv_ref[at : at + 1, :]
        for part in range(2):
            val = cross[:, part * block : (part + 1) * block]
            sym = 0.5 * (rounded(val * own_inv) + rounded(val * far_inv))
            own_scr[part, f] = sym.astype(jnp.bfloat16)
            turned = jnp.transpose(sym if part == 0 else -sym)
            far_scr[part, f] = turned.astype(jnp.bfloat16)
    me = me_ref[0]
    matrix = interleave()
    for which, scr in enumerate((own_scr, far_scr)):
        for d in range(freq_count):
            for j in range(groups):
                first = (lax.rem(me + d, freq_count) * groups + j) * SUB
                rows = pl.ds(pl.multiple_of(first, SUB), SUB)
                turned = turned_rows(matrix, scr[0, :, rows, :], scr[1, :, rows, :])
                out = outs[(which * freq_count + d) * groups + j]
                for part in range(2):
                    out[:, part] = turned[:, :, part * block : (part + 1) * block].astype(jnp.bfloat16)


def cross_piece(piece, freq_count, groups, places, me, own, far, own_inv, far_inv, before):
    half, _, seg, block = own.shape
    n_far = len(far)
    outputs = [(k, j) for k in range(2 * freq_count) for j in range(groups)]
    spots = [n for n, (_, j) in enumerate(outputs) if places[j][2]]
    held = [before[outputs[n][0]][outputs[n][1]] for n in spots]
    flat = pl.pallas_call(
        functools.partial(cross_kernel, piece, freq_count, groups, len(held), n_far),
        grid=(1,),
        in_specs=[
            pl.BlockSpec(memory_space=pltpu.SMEM),
            pl.BlockSpec((SUB, 2, seg, block), lambda i: (piece, 0, 0, 0)),
            pl.BlockSpec((block, half), lambda i: (0, 0)),
            pl.BlockSpec((half, block), lambda i: (0, 0)),
        ]
        + [pl.BlockSpec(x.shape, lambda i: (0, 0, 0, 0)) for x in far]
        + [pl.BlockSpec(memory_space=pl.ANY)] * len(held),
        out_specs=[
            pl.BlockSpec((SUB, 2, SUB, block), functools.partial(lambda at, i: (0, 0, at, 0), places[j][1]))
            for _, j in outputs
        ],
        out_shape=[jax.ShapeDtypeStruct((SUB, 2, places[j][0], block), jnp.bfloat16) for _, j in outputs],
        scratch_shapes=[pltpu.VMEM((2, SUB, block, block), jnp.bfloat16)] * 2,
        input_output_aliases={4 + n_far + i: n for i, n in enumerate(spots)},
        compiler_params=pltpu.CompilerParams(vmem_limit_bytes=VMEM_BYTES),
        cost_estimate=pl.CostEstimate(
            flops=SUB * 8 * seg * block * block, bytes_accessed=SUB * 16 * seg * block, transcendentals=0
        ),
        name="cross_piece",
    )(me, own, own_inv, far_inv, *far, *held)
    return [flat[k * groups : (k + 1) * groups] for k in range(2 * freq_count)]


def lag_kernel(sources, rows, held, lag_ref, back_ref, *refs):
    n_pieces = sum(sources)
    pieces, out_ref, scr = refs[:n_pieces], refs[n_pieces + held], refs[-1]
    block = scr.shape[2]
    bins = out_ref.shape[2]

    def column(r):
        parts, at = [], 0
        for count in sources:
            for part in range(2):
                parts += [piece[r, part] for piece in pieces[at : at + count]]
            at += count
        return jnp.concatenate(parts, axis=0)

    for r in range(0, rows, 2):
        cols = jnp.concatenate([column(r), column(r + 1)], axis=1)
        lag = jnp.dot(lag_ref[...], cols, preferred_element_type=jnp.float32)
        lag_re, lag_im = lag[:LAGS], lag[LAGS:]
        energy = lag_re * lag_re + lag_im * lag_im
        floor = (0.25 / LAGS) * jnp.sum(energy, axis=0, keepdims=True) + 1e-05
        normalized = (lag_re * lax.rsqrt(energy + floor)).astype(jnp.bfloat16)
        back = jnp.dot(back_ref[...], normalized, preferred_element_type=jnp.float32) * (1.0 / math.sqrt(LAGS))
        for k in range(2):
            scr[r + k] = back[:, k * block : (k + 1) * block].astype(jnp.bfloat16)
    matrix = interleave()
    for part in range(2):
        for k in range(0, bins, 2 * SUB):
            at = part * bins + k
            turned = turned_rows(matrix, scr[:, at : at + SUB], scr[:, at + SUB : at + 2 * SUB])
            for n in range(2):
                rows = turned[:, :, n * block : (n + 1) * block]
                out_ref[0, part, k + n * SUB : k + (n + 1) * SUB] = rows.astype(jnp.bfloat16)


def lag_group(group, groups, lag_table, back_table, sources, before):
    pieces = [piece for source in sources for piece in source]
    rows, _, _, block = pieces[0].shape
    held = len(before)
    bins = back_table.shape[0] // 2
    return pl.pallas_call(
        functools.partial(lag_kernel, [len(source) for source in sources], rows, held),
        grid=(1,),
        in_specs=[pl.BlockSpec(lag_table.shape, lambda i: (0, 0)), pl.BlockSpec(back_table.shape, lambda i: (0, 0))]
        + [pl.BlockSpec(piece.shape, lambda i: (0, 0, 0, 0)) for piece in pieces]
        + [pl.BlockSpec(memory_space=pl.ANY)] * held,
        out_specs=pl.BlockSpec((1, 2, bins, rows, block), lambda i: (0, 0, 0, group, 0)),
        out_shape=jax.ShapeDtypeStruct((1, 2, bins, rows * groups, block), jnp.bfloat16),
        scratch_shapes=[pltpu.VMEM((rows, 2 * bins, block), jnp.bfloat16)],
        input_output_aliases={2 + len(pieces): 0} if held else {},
        compiler_params=pltpu.CompilerParams(vmem_limit_bytes=VMEM_BYTES),
        cost_estimate=pl.CostEstimate(
            flops=rows * block * 2 * LAGS * 6 * F, bytes_accessed=rows * block * 16 * F, transcendentals=rows * block * LAGS
        ),
        name="lag_group",
    )(lag_table, back_table, *pieces, *before)


def shards(spectra, seg_mask):
    tile_count, freq_count = lax.axis_size("tile"), lax.axis_size("freq")
    half_axis = tile_count // 2
    _, seg, band, block = spectra.shape
    half = band // 2
    n_sub = half // SUB
    groups = block // freq_count // SUB
    me = lax.axis_index("freq")
    side = lax.axis_index("tile") // half_axis
    keep_from, send_from = side * half, (1 - side) * half

    across = [(t, (t + half_axis) % tile_count) for t in range(tile_count)]

    def along(block, d, cross):
        route = []
        for h in range(freq_count):
            for t in range(tile_count):
                there = (t + half_axis * cross) % tile_count
                route.append((h * tile_count + t, (h + d) % freq_count * tile_count + there))
        return lax.ppermute(block, ("freq", "tile"), route)

    keep_sub, send_sub = side * n_sub, (1 - side) * n_sub
    *pieces, power = prepare(spectra, seg_mask, send_sub, 1, (SHORT, SUB - SHORT))
    send_power = [power]
    far = [lax.ppermute(piece, "tile", across) for piece in pieces]
    rest, far[0] = lax.optimization_barrier((spectra, far[0]))
    for i in range(1, n_sub):
        *pieces, power = prepare(rest, seg_mask, send_sub + i, 1, (SUB // 2, SUB // 2))
        rest, pieces = lax.optimization_barrier((rest, pieces))
        send_power.append(power)
        for piece in pieces:
            if len(far) >= 2 + DEPTH - 1:
                piece, far[-DEPTH] = lax.optimization_barrier((piece, far[-DEPTH]))
            far.append(lax.ppermute(piece, "tile", across))
    own, own_power = prepare(rest, seg_mask, keep_sub, n_sub, (half,))
    send_power = jnp.concatenate(send_power, axis=0)

    total = lax.psum(jnp.sum(own_power, axis=0) + jnp.sum(send_power, axis=0), "freq")
    lift = WATER * (total / F)[None, :]
    own_inv = (1.0 / ((own_power + lift) * seg)).T
    far_inv = lax.ppermute(1.0 / ((send_power + lift) * seg), "tile", across)

    local = jnp.arange(half, dtype=jnp.int32)
    lag_cols = []
    for mine in (True, False):
        for d in range(freq_count):
            freqs = (me - d) % freq_count * band + (keep_from if mine else send_from) + local
            cos_tab, sin_tab = dft_tables(freqs)
            lag_cols.append(jnp.concatenate([cos_tab, sin_tab], axis=0))
            lag_cols.append(jnp.concatenate([-sin_tab, cos_tab], axis=0))
    lag_table = jnp.concatenate(lag_cols, axis=1)
    cos_tab, sin_tab = dft_tables(jnp.arange(F, dtype=jnp.int32))
    back_table = jnp.concatenate([cos_tab, -sin_tab], axis=1).T

    n_split = groups // 2 if n_sub > 1 else 0
    me_arr = me.astype(jnp.int32).reshape(1)
    ready = max(2 * n_sub - 3, 0)
    far[ready], lag_table, back_table, own_inv, far_inv, own = lax.optimization_barrier(
        (far[ready], lag_table, back_table, own_inv, far_inv, own)
    )
    early, sym = None, None
    for i in range(n_sub):
        last = i == n_sub - 1
        if last:
            early = sym
            split = (SUB, 0, False)
        else:
            split = (half - SUB, i, i > 0)
        places = [split if j < n_split else (half, i, i > 0) for j in range(groups)]
        sym = cross_piece(i, freq_count, groups, places, me_arr, own, far[2 * i : 2 * i + 2], own_inv, far_inv, sym)

    stages = [(j, True) for j in range(n_split)] + [(j, False) for j in range(groups)]
    ahead = 2 * n_split or 2
    arrived = {}
    for n, (j, is_early) in enumerate(stages):
        made = early if is_early else sym
        outgoing = [made[k][j] for k in range(1, 2 * freq_count)]
        if n >= ahead:
            waited = stages[n - ahead]
            outgoing, arrived[waited] = lax.optimization_barrier((outgoing, arrived[waited]))
        arrived[j, is_early] = [along(outgoing[k - 1], k % freq_count, k // freq_count) for k in range(1, 2 * freq_count)]
    out = []
    for j in range(groups):
        parts = ([(early, True)] if j < n_split else []) + [(sym, False)]
        sources = [
            [made[0][j] if k == 0 else arrived[j, is_early][k - 1] for made, is_early in parts]
            for k in range(2 * freq_count)
        ]
        out = [lag_group(j, groups, lag_table, back_table, sources, out)]
    return out[0]


def solution(mesh):
    placed = (P(None, None, "freq", "tile"), P(None, "tile"))
    return jax.shard_map(
        shards,
        mesh=mesh,
        in_specs=placed,
        out_specs=P("tile", None, None, "freq", None),
        check_vma=False,
    )
```

```python
import functools
import math

import jax
import jax.numpy as jnp
from jax import lax
from jax.experimental import pallas as pl
from jax.experimental.pallas import tpu as pltpu
from jax.sharding import PartitionSpec as P

F = 256
LAGS = 512
WATER = 0.05
SUB = 16
SHORT = 4
DEPTH = 4
VMEM_BYTES = 48 * 2**20


def dft_tables(freq_index):
    lag_index = jnp.arange(LAGS, dtype=jnp.int32)[:, None]
    phase = (lag_index * freq_index[None, :] % LAGS).astype(jnp.float32) * (2.0 * math.pi / LAGS)
    return jnp.cos(phase).astype(jnp.bfloat16), jnp.sin(phase).astype(jnp.bfloat16)


def rounded(x):
    return x.astype(jnp.bfloat16).astype(jnp.float32)


def interleave():
    row = lax.broadcasted_iota(jnp.int32, (SUB * SUB, SUB * SUB), 0)
    col = lax.broadcasted_iota(jnp.int32, (SUB * SUB, SUB * SUB), 1)
    return jnp.where(col == row % SUB * SUB + row // SUB, 1.0, 0.0).astype(jnp.bfloat16)


def turned_rows(matrix, left, right):
    lanes = left.shape[2]
    both = jnp.concatenate([left.reshape(SUB * SUB, lanes), right.reshape(SUB * SUB, lanes)], axis=1)
    return jnp.dot(matrix, both, preferred_element_type=jnp.float32).reshape(SUB, SUB, 2 * lanes)


def prepare_kernel(at_ref, x_ref, mask_ref, *outs):
    parts, power_ref = outs[:-1], outs[-1]
    seg, lanes = mask_ref.shape
    matrix = interleave()
    total = jnp.zeros((SUB, 8, lanes), jnp.float32)
    for s in range(0, seg, SUB):
        mask = mask_ref[s : s + SUB].astype(jnp.float32)[None]
        turned = turned_rows(matrix, x_ref[0, s : s + SUB], x_ref[1, s : s + SUB])
        for part in range(2):
            val = turned[:, :, part * lanes : (part + 1) * lanes] * mask
            square = val * val
            total += square[:, :8] + square[:, 8:]
            at = 0
            for out in parts:
                count = out.shape[0]
                out[:, part, s : s + SUB] = val[at : at + count].astype(jnp.bfloat16)
                at += count
    power_ref[...] = jnp.sum(total, axis=1) * (1.0 / seg) + 1e-05


def prepare(spectra, seg_mask, first, steps, counts):
    _, seg, _, block = spectra.shape
    assert sum(counts) == steps * SUB and (steps == 1 or len(counts) == 1)
    out_specs = [pl.BlockSpec((min(count, SUB), 2, seg, block), lambda i, at: (i, 0, 0, 0)) for count in counts]
    out_shape = [jax.ShapeDtypeStruct((count, 2, seg, block), jnp.bfloat16) for count in counts]
    return pl.pallas_call(
        prepare_kernel,
        grid_spec=pltpu.PrefetchScalarGridSpec(
            num_scalar_prefetch=1,
            grid=(steps,),
            in_specs=[
                pl.BlockSpec((2, seg, SUB, block), lambda i, at: (0, 0, at[0] + i, 0)),
                pl.BlockSpec((seg, block), lambda i, at: (0, 0)),
            ],
            out_specs=out_specs + [pl.BlockSpec((SUB, block), lambda i, at: (i, 0))],
        ),
        out_shape=out_shape + [jax.ShapeDtypeStruct((steps * SUB, block), jnp.float32)],
        compiler_params=pltpu.CompilerParams(vmem_limit_bytes=VMEM_BYTES),
        cost_estimate=pl.CostEstimate(
            flops=steps * SUB * seg * block * 8, bytes_accessed=steps * SUB * seg * block * 8, transcendentals=0
        ),
        name="prepare",
    )(first.astype(jnp.int32).reshape(1), spectra, seg_mask)


def cross_kernel(piece, freq_count, groups, held, n_far, me_ref, own_ref, own_inv_ref, far_inv_ref, *refs):
    far_refs, outs, (own_scr, far_scr) = refs[:n_far], refs[n_far + held : -2], refs[-2:]
    seg = own_ref.shape[2]
    block = own_ref.shape[3]
    far_rows = [(far_ref, k) for far_ref in far_refs for k in range(far_ref.shape[0])]
    for f in range(SUB):
        own = own_ref[f].reshape(2 * seg, block)
        far_ref, k = far_rows[f]
        far_re, far_im = far_ref[k, 0], far_ref[k, 1]
        cols = jnp.concatenate(
            [jnp.concatenate([far_re, far_im], axis=0), jnp.concatenate([far_im, -far_re], axis=0)], axis=1
        )
        cross = lax.dot_general(own, cols, (((0,), (0,)), ((), ())), preferred_element_type=jnp.float32)
        at = piece * SUB + f
        own_inv = own_inv_ref[:, at : at + 1]
        far_inv = far_inv_ref[at : at + 1, :]
        for part in range(2):
            val = cross[:, part * block : (part + 1) * block]
            sym = 0.5 * (rounded(val * own_inv) + rounded(val * far_inv))
            own_scr[part, f] = sym.astype(jnp.bfloat16)
            turned = jnp.transpose(sym if part == 0 else -sym)
            far_scr[part, f] = turned.astype(jnp.bfloat16)
    me = me_ref[0]
    matrix = interleave()
    for which, scr in enumerate((own_scr, far_scr)):
        for d in range(freq_count):
            for j in range(groups):
                first = (lax.rem(me + d, freq_count) * groups + j) * SUB
                rows = pl.ds(pl.multiple_of(first, SUB), SUB)
                turned = turned_rows(matrix, scr[0, :, rows, :], scr[1, :, rows, :])
                out = outs[(which * freq_count + d) * groups + j]
                for part in range(2):
                    out[:, part] = turned[:, :, part * block : (part + 1) * block].astype(jnp.bfloat16)


def cross_piece(piece, freq_count, groups, places, me, own, far, own_inv, far_inv, before):
    half, _, seg, block = own.shape
    n_far = len(far)
    outputs = [(k, j) for k in range(2 * freq_count) for j in range(groups)]
    spots = [n for n, (_, j) in enumerate(outputs) if places[j][2]]
    held = [before[outputs[n][0]][outputs[n][1]] for n in spots]
    flat = pl.pallas_call(
        functools.partial(cross_kernel, piece, freq_count, groups, len(held), n_far),
        grid=(1,),
        in_specs=[
            pl.BlockSpec(memory_space=pltpu.SMEM),
            pl.BlockSpec((SUB, 2, seg, block), lambda i: (piece, 0, 0, 0)),
            pl.BlockSpec((block, half), lambda i: (0, 0)),
            pl.BlockSpec((half, block), lambda i: (0, 0)),
        ]
        + [pl.BlockSpec(x.shape, lambda i: (0, 0, 0, 0)) for x in far]
        + [pl.BlockSpec(memory_space=pl.ANY)] * len(held),
        out_specs=[
            pl.BlockSpec((SUB, 2, SUB, block), functools.partial(lambda at, i: (0, 0, at, 0), places[j][1]))
            for _, j in outputs
        ],
        out_shape=[jax.ShapeDtypeStruct((SUB, 2, places[j][0], block), jnp.bfloat16) for _, j in outputs],
        scratch_shapes=[pltpu.VMEM((2, SUB, block, block), jnp.bfloat16)] * 2,
        input_output_aliases={4 + n_far + i: n for i, n in enumerate(spots)},
        compiler_params=pltpu.CompilerParams(vmem_limit_bytes=VMEM_BYTES),
        cost_estimate=pl.CostEstimate(
            flops=SUB * 8 * seg * block * block, bytes_accessed=SUB * 16 * seg * block, transcendentals=0
        ),
        name="cross_piece",
    )(me, own, own_inv, far_inv, *far, *held)
    return [flat[k * groups : (k + 1) * groups] for k in range(2 * freq_count)]


def lag_kernel(sources, rows, held, lag_ref, back_ref, *refs):
    n_pieces = sum(sources)
    pieces, out_ref, scr = refs[:n_pieces], refs[n_pieces + held], refs[-1]
    block = scr.shape[2]
    bins = out_ref.shape[2]

    def column(r):
        parts, at = [], 0
        for count in sources:
            for part in range(2):
                parts += [piece[r, part] for piece in pieces[at : at + count]]
            at += count
        return jnp.concatenate(parts, axis=0)

    for r in range(0, rows, 2):
        cols = jnp.concatenate([column(r), column(r + 1)], axis=1)
        lag = jnp.dot(lag_ref[...], cols, preferred_element_type=jnp.float32)
        lag_re, lag_im = lag[:LAGS], lag[LAGS:]
        energy = lag_re * lag_re + lag_im * lag_im
        floor = (0.25 / LAGS) * jnp.sum(energy, axis=0, keepdims=True) + 1e-05
        normalized = (lag_re * lax.rsqrt(energy + floor)).astype(jnp.bfloat16)
        back = jnp.dot(back_ref[...], normalized, preferred_element_type=jnp.float32) * (1.0 / math.sqrt(LAGS))
        for k in range(2):
            scr[r + k] = back[:, k * block : (k + 1) * block].astype(jnp.bfloat16)
    matrix = interleave()
    for part in range(2):
        for k in range(0, bins, 2 * SUB):
            at = part * bins + k
            turned = turned_rows(matrix, scr[:, at : at + SUB], scr[:, at + SUB : at + 2 * SUB])
            for n in range(2):
                rows = turned[:, :, n * block : (n + 1) * block]
                out_ref[0, part, k + n * SUB : k + (n + 1) * SUB] = rows.astype(jnp.bfloat16)


def lag_group(group, groups, lag_table, back_table, sources, before):
    pieces = [piece for source in sources for piece in source]
    rows, _, _, block = pieces[0].shape
    held = len(before)
    bins = back_table.shape[0] // 2
    return pl.pallas_call(
        functools.partial(lag_kernel, [len(source) for source in sources], rows, held),
        grid=(1,),
        in_specs=[pl.BlockSpec(lag_table.shape, lambda i: (0, 0)), pl.BlockSpec(back_table.shape, lambda i: (0, 0))]
        + [pl.BlockSpec(piece.shape, lambda i: (0, 0, 0, 0)) for piece in pieces]
        + [pl.BlockSpec(memory_space=pl.ANY)] * held,
        out_specs=pl.BlockSpec((1, 2, bins, rows, block), lambda i: (0, 0, 0, group, 0)),
        out_shape=jax.ShapeDtypeStruct((1, 2, bins, rows * groups, block), jnp.bfloat16),
        scratch_shapes=[pltpu.VMEM((rows, 2 * bins, block), jnp.bfloat16)],
        input_output_aliases={2 + len(pieces): 0} if held else {},
        compiler_params=pltpu.CompilerParams(vmem_limit_bytes=VMEM_BYTES),
        cost_estimate=pl.CostEstimate(
            flops=rows * block * 2 * LAGS * 6 * F, bytes_accessed=rows * block * 16 * F, transcendentals=rows * block * LAGS
        ),
        name="lag_group",
    )(lag_table, back_table, *pieces, *before)


def shards(spectra, seg_mask):
    tile_count, freq_count = lax.axis_size("tile"), lax.axis_size("freq")
    half_axis = tile_count // 2
    _, seg, band, block = spectra.shape
    half = band // 2
    n_sub = half // SUB
    groups = block // freq_count // SUB
    me = lax.axis_index("freq")
    side = lax.axis_index("tile") // half_axis
    keep_from, send_from = side * half, (1 - side) * half

    across = [(t, (t + half_axis) % tile_count) for t in range(tile_count)]

    def moved(block, d, distance):
        route = []
        for h in range(freq_count):
            for t in range(tile_count):
                route.append((h * tile_count + t, (h + d) % freq_count * tile_count + (t + distance) % tile_count))
        return lax.ppermute(block, ("freq", "tile"), route)

    def to_partner(block, d, way):
        if half_axis % 2:
            return moved(block, d, half_axis)
        hop = half_axis // 2 * (1 if way % 2 == 0 else -1)
        return moved(moved(block, 0, hop), d, hop)

    def along(block, d, cross, way):
        return to_partner(block, d, way) if cross else moved(block, d, 0)

    keep_sub, send_sub = side * n_sub, (1 - side) * n_sub
    *pieces, power = prepare(spectra, seg_mask, send_sub, 1, (SHORT, SUB - SHORT))
    send_power = [power]
    far = [to_partner(piece, 0, way) for way, piece in enumerate(pieces)]
    rest, far[0] = lax.optimization_barrier((spectra, far[0]))
    for i in range(1, n_sub):
        *pieces, power = prepare(rest, seg_mask, send_sub + i, 1, (SUB // 2, SUB // 2))
        rest, pieces = lax.optimization_barrier((rest, pieces))
        send_power.append(power)
        for piece in pieces:
            if len(far) >= 2 + DEPTH - 1:
                piece, far[-DEPTH] = lax.optimization_barrier((piece, far[-DEPTH]))
            far.append(to_partner(piece, 0, len(far)))
    own, own_power = prepare(rest, seg_mask, keep_sub, n_sub, (half,))
    send_power = jnp.concatenate(send_power, axis=0)

    total = lax.psum(jnp.sum(own_power, axis=0) + jnp.sum(send_power, axis=0), "freq")
    lift = WATER * (total / F)[None, :]
    own_inv = (1.0 / ((own_power + lift) * seg)).T
    far_inv = lax.ppermute(1.0 / ((send_power + lift) * seg), "tile", across)

    local = jnp.arange(half, dtype=jnp.int32)
    lag_cols = []
    for mine in (True, False):
        for d in range(freq_count):
            freqs = (me - d) % freq_count * band + (keep_from if mine else send_from) + local
            cos_tab, sin_tab = dft_tables(freqs)
            lag_cols.append(jnp.concatenate([cos_tab, sin_tab], axis=0))
            lag_cols.append(jnp.concatenate([-sin_tab, cos_tab], axis=0))
    lag_table = jnp.concatenate(lag_cols, axis=1)
    cos_tab, sin_tab = dft_tables(jnp.arange(F, dtype=jnp.int32))
    back_table = jnp.concatenate([cos_tab, -sin_tab], axis=1).T

    n_split = groups // 2 if n_sub > 1 else 0
    me_arr = me.astype(jnp.int32).reshape(1)
    ready = max(2 * n_sub - 3, 0)
    far[ready], lag_table, back_table, own_inv, far_inv, own = lax.optimization_barrier(
        (far[ready], lag_table, back_table, own_inv, far_inv, own)
    )
    early, sym = None, None
    for i in range(n_sub):
        last = i == n_sub - 1
        if last:
            early = sym
            split = (SUB, 0, False)
        else:
            split = (half - SUB, i, i > 0)
        places = [split if j < n_split else (half, i, i > 0) for j in range(groups)]
        sym = cross_piece(i, freq_count, groups, places, me_arr, own, far[2 * i : 2 * i + 2], own_inv, far_inv, sym)

    stages = [(j, True) for j in range(n_split)] + [(j, False) for j in range(groups)]
    ahead = 2 * n_split or 2
    arrived = {}
    for n, (j, is_early) in enumerate(stages):
        made = early if is_early else sym
        outgoing = [made[k][j] for k in range(1, 2 * freq_count)]
        if n >= ahead:
            waited = stages[n - ahead]
            outgoing, arrived[waited] = lax.optimization_barrier((outgoing, arrived[waited]))
        arrived[j, is_early] = [along(outgoing[k - 1], k % freq_count, k // freq_count, k) for k in range(1, 2 * freq_count)]
    out = []
    for j in range(groups):
        parts = ([(early, True)] if j < n_split else []) + [(sym, False)]
        sources = [
            [made[0][j] if k == 0 else arrived[j, is_early][k - 1] for made, is_early in parts]
            for k in range(2 * freq_count)
        ]
        out = [lag_group(j, groups, lag_table, back_table, sources, out)]
    return out[0]


def solution(mesh):
    placed = (P(None, None, "freq", "tile"), P(None, "tile"))
    return jax.shard_map(
        shards,
        mesh=mesh,
        in_specs=placed,
        out_specs=P("tile", None, None, "freq", None),
        check_vma=False,
    )
```

```python
import functools
import math

import jax
import jax.numpy as jnp
from jax import lax
from jax.experimental import pallas as pl
from jax.experimental.pallas import tpu as pltpu
from jax.sharding import PartitionSpec as P

F = 256
LAGS = 512
WATER = 0.05
SUB = 16
SHORT = 4
DEPTH = 3
AT_ONCE = 4
SLICE = 32
VMEM_BYTES = 48 * 2**20
NO_COST = pl.CostEstimate(flops=0, bytes_accessed=0, transcendentals=0)


def dft_tables(freq_index):
    lag_index = jnp.arange(LAGS, dtype=jnp.int32)[:, None]
    phase = (lag_index * freq_index[None, :] % LAGS).astype(jnp.float32) * (2.0 * math.pi / LAGS)
    return jnp.cos(phase).astype(jnp.bfloat16), jnp.sin(phase).astype(jnp.bfloat16)


def rounded(x):
    return x.astype(jnp.bfloat16).astype(jnp.float32)


def interleave():
    row = lax.broadcasted_iota(jnp.int32, (SUB * SUB, SUB * SUB), 0)
    col = lax.broadcasted_iota(jnp.int32, (SUB * SUB, SUB * SUB), 1)
    return jnp.where(col == row % SUB * SUB + row // SUB, 1.0, 0.0).astype(jnp.bfloat16)


def turned_rows(matrix, left, right):
    lanes = left.shape[2]
    both = jnp.concatenate([left.reshape(SUB * SUB, lanes), right.reshape(SUB * SUB, lanes)], axis=1)
    return jnp.dot(matrix, both, preferred_element_type=jnp.float32).reshape(SUB, SUB, 2 * lanes)


def prepare_kernel(at_ref, x_ref, mask_ref, *outs):
    parts, power_ref = outs[:-1], outs[-1]
    seg, lanes = mask_ref.shape
    matrix = interleave()
    total = jnp.zeros((SUB, 8, lanes), jnp.float32)
    for s in range(0, seg, SUB):
        mask = mask_ref[s : s + SUB].astype(jnp.float32)[None]
        turned = turned_rows(matrix, x_ref[0, s : s + SUB], x_ref[1, s : s + SUB])
        for part in range(2):
            val = turned[:, :, part * lanes : (part + 1) * lanes] * mask
            square = val * val
            total += square[:, :8] + square[:, 8:]
            at = 0
            for out in parts:
                count = out.shape[0]
                out[:, part, s : s + SUB] = val[at : at + count].astype(jnp.bfloat16)
                at += count
    power_ref[...] = jnp.sum(total, axis=1) * (1.0 / seg) + 1e-05


def prepare(spectra, seg_mask, first, steps, counts):
    _, seg, _, block = spectra.shape
    assert sum(counts) == steps * SUB and (steps == 1 or len(counts) == 1)
    out_specs = [pl.BlockSpec((min(count, SUB), 2, seg, block), lambda i, at: (i, 0, 0, 0)) for count in counts]
    out_shape = [jax.ShapeDtypeStruct((count, 2, seg, block), jnp.bfloat16) for count in counts]
    return pl.pallas_call(
        prepare_kernel,
        grid_spec=pltpu.PrefetchScalarGridSpec(
            num_scalar_prefetch=1,
            grid=(steps,),
            in_specs=[
                pl.BlockSpec((2, seg, SUB, block), lambda i, at: (0, 0, at[0] + i, 0)),
                pl.BlockSpec((seg, block), lambda i, at: (0, 0)),
            ],
            out_specs=out_specs + [pl.BlockSpec((SUB, block), lambda i, at: (i, 0))],
        ),
        out_shape=out_shape + [jax.ShapeDtypeStruct((steps * SUB, block), jnp.float32)],
        compiler_params=pltpu.CompilerParams(vmem_limit_bytes=VMEM_BYTES),
        cost_estimate=NO_COST,
        name="prepare",
    )(first.astype(jnp.int32).reshape(1), spectra, seg_mask)


def cross_kernel(piece, freq_count, groups, slots, held, n_far, me_ref, own_ref, own_inv_ref, far_inv_ref, *refs):
    far_refs, outs, (own_scr, far_scr) = refs[:n_far], refs[n_far + held : -2], refs[-2:]
    seg = own_ref.shape[2]
    block = own_ref.shape[3]
    far_rows = [(far_ref, k) for far_ref in far_refs for k in range(far_ref.shape[0])]
    for f in range(SUB):
        own = own_ref[f].reshape(2 * seg, block)
        far_ref, k = far_rows[f]
        far_re, far_im = far_ref[k, 0], far_ref[k, 1]
        cols = jnp.concatenate(
            [jnp.concatenate([far_re, far_im], axis=0), jnp.concatenate([far_im, -far_re], axis=0)], axis=1
        )
        cross = lax.dot_general(own, cols, (((0,), (0,)), ((), ())), preferred_element_type=jnp.float32)
        at = piece * SUB + f
        own_inv = own_inv_ref[:, at : at + 1]
        far_inv = far_inv_ref[at : at + 1, :]
        for part in range(2):
            val = cross[:, part * block : (part + 1) * block]
            sym = 0.5 * (rounded(val * own_inv) + rounded(val * far_inv))
            own_scr[part, f] = sym.astype(jnp.bfloat16)
            turned = jnp.transpose(sym if part == 0 else -sym)
            far_scr[part, f] = turned.astype(jnp.bfloat16)
    me = me_ref[0]
    matrix = interleave()
    for k in range(2 * freq_count):
        scr = own_scr if k < freq_count else far_scr
        for j in range(groups):
            first = (lax.rem(me + k % freq_count, freq_count) * groups + j) * SUB
            rows = pl.ds(pl.multiple_of(first, SUB), SUB)
            turned = turned_rows(matrix, scr[0, :, rows, :], scr[1, :, rows, :])
            for n, (group, first_row, count) in enumerate(slots):
                if group != j:
                    continue
                for part in range(2):
                    vals = turned[first_row : first_row + count, :, part * block : (part + 1) * block]
                    outs[k * len(slots) + n][:, part] = vals.astype(jnp.bfloat16)


def cross_piece(piece, freq_count, groups, slots, places, me, own, far, own_inv, far_inv, before):
    half, _, seg, block = own.shape
    n_far, n_slots = len(far), len(slots)
    outputs = [(k, n) for k in range(2 * freq_count) for n in range(n_slots)]
    spots = [m for m, (_, n) in enumerate(outputs) if places[n][2]]
    held = [before[outputs[m][0]][outputs[m][1]] for m in spots]
    flat = pl.pallas_call(
        functools.partial(cross_kernel, piece, freq_count, groups, slots, len(held), n_far),
        grid=(1,),
        in_specs=[
            pl.BlockSpec(memory_space=pltpu.SMEM),
            pl.BlockSpec((SUB, 2, seg, block), lambda i: (piece, 0, 0, 0)),
            pl.BlockSpec((block, half), lambda i: (0, 0)),
            pl.BlockSpec((half, block), lambda i: (0, 0)),
        ]
        + [pl.BlockSpec(x.shape, lambda i: (0, 0, 0, 0)) for x in far]
        + [pl.BlockSpec(memory_space=pl.ANY)] * len(held),
        out_specs=[
            pl.BlockSpec((slots[n][2], 2, SUB, block), functools.partial(lambda at, i: (0, 0, at, 0), places[n][1]))
            for _, n in outputs
        ],
        out_shape=[jax.ShapeDtypeStruct((slots[n][2], 2, places[n][0], block), jnp.bfloat16) for _, n in outputs],
        scratch_shapes=[pltpu.VMEM((2, SUB, block, block), jnp.bfloat16)] * 2,
        input_output_aliases={4 + n_far + i: m for i, m in enumerate(spots)},
        compiler_params=pltpu.CompilerParams(vmem_limit_bytes=VMEM_BYTES),
        cost_estimate=NO_COST,
        name="cross_piece",
    )(me, own, own_inv, far_inv, *far, *held)
    return [flat[k * n_slots : (k + 1) * n_slots] for k in range(2 * freq_count)]


def lag_kernel(sources, n_given, n_held, to_output, lag_ref, back_ref, *refs):
    n_pieces = sum(sources)
    pieces, given = refs[:n_pieces], refs[n_pieces : n_pieces + n_given]
    out_ref, lag_scr, norm_scr = refs[n_pieces + n_given + n_held :][:3]
    rows = pieces[0].shape[0]
    block = pieces[0].shape[3]
    width = AT_ONCE * block
    row_ref = refs[-1] if to_output else out_ref
    first = SUB - rows if to_output else 0

    def column(r):
        parts, at = [], 0
        for count in sources:
            for part in range(2):
                parts += [piece[r, part] for piece in pieces[at : at + count]]
            at += count
        return jnp.concatenate(parts, axis=0)

    for r in range(0, rows, AT_ONCE):
        cols = jnp.concatenate([column(r + k) for k in range(AT_ONCE)], axis=1)
        lag_scr[...] = jnp.dot(lag_ref[...], cols, preferred_element_type=jnp.float32)
        total = jnp.zeros((8, width), jnp.float32)
        for at in range(0, LAGS, SLICE):
            lag_re, lag_im = lag_scr[at : at + SLICE], lag_scr[LAGS + at : LAGS + at + SLICE]
            energy = lag_re * lag_re + lag_im * lag_im
            lag_scr[LAGS + at : LAGS + at + SLICE] = energy
            total += jnp.sum(energy.reshape(SLICE // 8, 8, width), axis=0)
        floor = (0.25 / LAGS) * jnp.sum(total, axis=0, keepdims=True) + 1e-05
        for at in range(0, LAGS, SLICE):
            scale = lax.rsqrt(lag_scr[LAGS + at : LAGS + at + SLICE] + floor)
            norm_scr[at : at + SLICE] = (lag_scr[at : at + SLICE] * scale).astype(jnp.bfloat16)
        lag_scr[: 2 * F] = jnp.dot(back_ref[...], norm_scr[...], preferred_element_type=jnp.float32)
        for at in range(0, 2 * F, SLICE):
            back = (lag_scr[at : at + SLICE] * (1.0 / math.sqrt(LAGS))).astype(jnp.bfloat16)
            for k in range(AT_ONCE):
                row_ref[first + r + k, at : at + SLICE] = back[:, k * block : (k + 1) * block]
    if to_output:
        matrix = interleave()
        for part in range(2):
            for k in range(0, F, 2 * SUB):
                at = part * F + k
                whole = [x[:, at : at + 2 * SUB] for x in given] + [row_ref[first:, at : at + 2 * SUB]]
                whole = jnp.concatenate(whole, axis=0)
                turned = turned_rows(matrix, whole[:, :SUB], whole[:, SUB:])
                for n in range(2):
                    bins = turned[:, :, n * block : (n + 1) * block]
                    out_ref[0, part, k + n * SUB : k + (n + 1) * SUB] = bins.astype(jnp.bfloat16)


def lag_group(group, groups, lag_table, back_table, sources, given, before, to_output=True):
    pieces = [piece for source in sources for piece in source]
    rows, _, _, block = pieces[0].shape
    if to_output:
        out_spec = pl.BlockSpec((1, 2, F, SUB, block), lambda i: (0, 0, 0, group, 0))
        out_shape = jax.ShapeDtypeStruct((1, 2, F, SUB * groups, block), jnp.bfloat16)
    else:
        out_spec = pl.BlockSpec((rows, 2 * F, block), lambda i: (0, 0, 0))
        out_shape = jax.ShapeDtypeStruct((rows, 2 * F, block), jnp.bfloat16)
    scratch = [
        pltpu.VMEM((2 * LAGS, AT_ONCE * block), jnp.float32),
        pltpu.VMEM((LAGS, AT_ONCE * block), jnp.bfloat16),
        pltpu.VMEM((SUB, 2 * F, block), jnp.bfloat16),
    ]
    return pl.pallas_call(
        functools.partial(lag_kernel, [len(source) for source in sources], len(given), len(before), to_output),
        grid=(1,),
        in_specs=[pl.BlockSpec(lag_table.shape, lambda i: (0, 0)), pl.BlockSpec(back_table.shape, lambda i: (0, 0))]
        + [pl.BlockSpec(piece.shape, lambda i: (0, 0, 0, 0)) for piece in pieces]
        + [pl.BlockSpec(x.shape, lambda i: (0, 0, 0)) for x in given]
        + [pl.BlockSpec(memory_space=pl.ANY)] * len(before),
        out_specs=out_spec,
        out_shape=out_shape,
        scratch_shapes=scratch,
        input_output_aliases={2 + len(pieces) + len(given): 0} if before else {},
        compiler_params=pltpu.CompilerParams(vmem_limit_bytes=VMEM_BYTES),
        cost_estimate=NO_COST,
        name="lag_group",
    )(lag_table, back_table, *pieces, *given, *before)


def shards(spectra, seg_mask):
    tile_count, freq_count = lax.axis_size("tile"), lax.axis_size("freq")
    half_axis = tile_count // 2
    _, seg, band, block = spectra.shape
    half = band // 2
    n_sub = half // SUB
    groups = block // freq_count // SUB
    me = lax.axis_index("freq")
    side = lax.axis_index("tile") // half_axis
    keep_from, send_from = side * half, (1 - side) * half

    across = [(t, (t + half_axis) % tile_count) for t in range(tile_count)]

    def along(block, d, cross):
        route = []
        for h in range(freq_count):
            for t in range(tile_count):
                there = (t + half_axis * cross) % tile_count
                route.append((h * tile_count + t, (h + d) % freq_count * tile_count + there))
        return lax.ppermute(block, ("freq", "tile"), route)

    keep_sub, send_sub = side * n_sub, (1 - side) * n_sub
    *pieces, power = prepare(spectra, seg_mask, send_sub, 1, (SHORT, SUB - SHORT))
    send_power = [power]
    far = [lax.ppermute(piece, "tile", across) for piece in pieces]
    rest, far[0] = lax.optimization_barrier((spectra, far[0]))
    for i in range(1, n_sub):
        *pieces, power = prepare(rest, seg_mask, send_sub + i, 1, (SUB // 2, SUB // 2))
        rest, pieces = lax.optimization_barrier((rest, pieces))
        send_power.append(power)
        for piece in pieces:
            if len(far) >= 2 + DEPTH - 1:
                piece, far[-DEPTH] = lax.optimization_barrier((piece, far[-DEPTH]))
            far.append(lax.ppermute(piece, "tile", across))
    own, own_power = prepare(rest, seg_mask, keep_sub, n_sub, (half,))
    send_power = jnp.concatenate(send_power, axis=0)

    total = lax.psum(jnp.sum(own_power, axis=0) + jnp.sum(send_power, axis=0), "freq")
    lift = WATER * (total / F)[None, :]
    own_inv = (1.0 / ((own_power + lift) * seg)).T
    far_inv = lax.ppermute(1.0 / ((send_power + lift) * seg), "tile", across)

    local = jnp.arange(half, dtype=jnp.int32)
    lag_cols = []
    for mine in (True, False):
        for d in range(freq_count):
            freqs = (me - d) % freq_count * band + (keep_from if mine else send_from) + local
            cos_tab, sin_tab = dft_tables(freqs)
            lag_cols.append(jnp.concatenate([cos_tab, sin_tab], axis=0))
            lag_cols.append(jnp.concatenate([-sin_tab, cos_tab], axis=0))
    lag_table = jnp.concatenate(lag_cols, axis=1)
    cos_tab, sin_tab = dft_tables(jnp.arange(F, dtype=jnp.int32))
    back_table = jnp.concatenate([cos_tab, -sin_tab], axis=1).T

    n_split = groups // 2 if n_sub > 1 else 0
    slots = [(j, 0, SUB) for j in range(groups if groups == 1 else n_split)]
    if groups > 1:
        slots += [(j, first_row, SUB // 2) for j in range(n_split, groups) for first_row in (0, SUB // 2)]
    me_arr = me.astype(jnp.int32).reshape(1)
    ready = max(2 * n_sub - 3, 0)
    far[ready], lag_table, back_table, own_inv, far_inv, own = lax.optimization_barrier(
        (far[ready], lag_table, back_table, own_inv, far_inv, own)
    )
    early, sym = None, None
    for i in range(n_sub):
        last = i == n_sub - 1
        if last:
            early = sym
            split = (SUB, 0, False)
        else:
            split = (half - SUB, i, i > 0)
        places = [split if n < n_split else (half, i, i > 0) for n in range(len(slots))]
        sym = cross_piece(i, freq_count, groups, slots, places, me_arr, own, far[2 * i : 2 * i + 2], own_inv, far_inv, sym)

    stages = [(n, True) for n in range(n_split)] + [(n, False) for n in range(len(slots))]
    arrived = {}
    for m, (n, is_early) in enumerate(stages):
        made = early if is_early else sym
        outgoing = [made[k][n] for k in range(1, 2 * freq_count)]
        place = m - 2 * n_split
        if place >= 2 or 0 <= place < n_split:
            waited = stages[m - 2 if place >= 2 else place]
            outgoing, arrived[waited] = lax.optimization_barrier((outgoing, arrived[waited]))
        arrived[n, is_early] = [along(outgoing[k - 1], k % freq_count, k // freq_count) for k in range(1, 2 * freq_count)]
    out, given = [], []
    for n, (group, first_row, count) in enumerate(slots):
        parts = ([(early, True)] if n < n_split else []) + [(sym, False)]
        sources = [
            [made[0][n] if k == 0 else arrived[n, is_early][k - 1] for made, is_early in parts]
            for k in range(2 * freq_count)
        ]
        if first_row + count < SUB:
            given = [lag_group(group, groups, lag_table, back_table, sources, [], [], to_output=False)]
        else:
            out = [lag_group(group, groups, lag_table, back_table, sources, given if first_row else [], out)]
    return out[0]


def solution(mesh):
    placed = (P(None, None, "freq", "tile"), P(None, "tile"))
    return jax.shard_map(
        shards,
        mesh=mesh,
        in_specs=placed,
        out_specs=P("tile", None, None, "freq", None),
        check_vma=False,
    )
```

```python
import functools
import math

import jax
import jax.numpy as jnp
from jax import lax
from jax.experimental import pallas as pl
from jax.experimental.pallas import tpu as pltpu
from jax.sharding import PartitionSpec as P

F = 256
LAGS = 512
WATER = 0.05
SUB = 16
SHORT = 4
DEPTH = 3
AT_ONCE = 4
SLICE = 32
VMEM_BYTES = 48 * 2**20
NO_COST = pl.CostEstimate(flops=0, bytes_accessed=0, transcendentals=0)


def dft_tables(freq_index):
    lag_index = jnp.arange(LAGS, dtype=jnp.int32)[:, None]
    phase = (lag_index * freq_index[None, :] % LAGS).astype(jnp.float32) * (2.0 * math.pi / LAGS)
    return jnp.cos(phase).astype(jnp.bfloat16), jnp.sin(phase).astype(jnp.bfloat16)


def rounded(x):
    return x.astype(jnp.bfloat16).astype(jnp.float32)


def interleave():
    row = lax.broadcasted_iota(jnp.int32, (SUB * SUB, SUB * SUB), 0)
    col = lax.broadcasted_iota(jnp.int32, (SUB * SUB, SUB * SUB), 1)
    return jnp.where(col == row % SUB * SUB + row // SUB, 1.0, 0.0).astype(jnp.bfloat16)


def turned_rows(matrix, left, right):
    lanes = left.shape[2]
    both = jnp.concatenate([left.reshape(SUB * SUB, lanes), right.reshape(SUB * SUB, lanes)], axis=1)
    return jnp.dot(matrix, both, preferred_element_type=jnp.float32).reshape(SUB, SUB, 2 * lanes)


def prepare_kernel(at_ref, x_ref, mask_ref, *outs):
    parts, power_ref = outs[:-1], outs[-1]
    seg, lanes = mask_ref.shape
    matrix = interleave()
    total = jnp.zeros((SUB, 8, lanes), jnp.float32)
    for s in range(0, seg, SUB):
        mask = mask_ref[s : s + SUB].astype(jnp.float32)[None]
        turned = turned_rows(matrix, x_ref[0, s : s + SUB], x_ref[1, s : s + SUB])
        for part in range(2):
            val = turned[:, :, part * lanes : (part + 1) * lanes] * mask
            square = val * val
            total += square[:, :8] + square[:, 8:]
            at = 0
            for out in parts:
                count = out.shape[0]
                out[:, part, s : s + SUB] = val[at : at + count].astype(jnp.bfloat16)
                at += count
    power_ref[...] = jnp.sum(total, axis=1) * (1.0 / seg) + 1e-05


def prepare(spectra, seg_mask, first, steps, counts):
    _, seg, _, block = spectra.shape
    assert sum(counts) == steps * SUB and (steps == 1 or len(counts) == 1)
    out_specs = [pl.BlockSpec((min(count, SUB), 2, seg, block), lambda i, at: (i, 0, 0, 0)) for count in counts]
    out_shape = [jax.ShapeDtypeStruct((count, 2, seg, block), jnp.bfloat16) for count in counts]
    return pl.pallas_call(
        prepare_kernel,
        grid_spec=pltpu.PrefetchScalarGridSpec(
            num_scalar_prefetch=1,
            grid=(steps,),
            in_specs=[
                pl.BlockSpec((2, seg, SUB, block), lambda i, at: (0, 0, at[0] + i, 0)),
                pl.BlockSpec((seg, block), lambda i, at: (0, 0)),
            ],
            out_specs=out_specs + [pl.BlockSpec((SUB, block), lambda i, at: (i, 0))],
        ),
        out_shape=out_shape + [jax.ShapeDtypeStruct((steps * SUB, block), jnp.float32)],
        compiler_params=pltpu.CompilerParams(vmem_limit_bytes=VMEM_BYTES),
        cost_estimate=pl.CostEstimate(
            flops=steps * SUB * seg * block * 8, bytes_accessed=steps * SUB * seg * block * 8, transcendentals=0
        ),
        name="prepare",
    )(first.astype(jnp.int32).reshape(1), spectra, seg_mask)


def exact_terms(x):
    terms, rest = [], x
    for _ in range(3):
        terms.append(lax.reduce_precision(rest, 8, 7))
        rest = rest - terms[-1]
    return jnp.pad(jnp.stack(terms).astype(jnp.bfloat16), ((0, SUB - 3), (0, 0)))


def cross_kernel(piece, freq_count, groups, slots, held, n_far, me_ref, own_ref, own_inv_ref, far_lift_ref, *refs):
    far_refs, outs, (own_scr, far_scr) = refs[:n_far], refs[n_far + held : -2], refs[-2:]
    seg = own_ref.shape[2]
    block = own_ref.shape[3]
    far_rows = [(far_ref, k) for far_ref in far_refs for k in range(far_ref.shape[0])]
    for f in range(SUB):
        own = own_ref[f].reshape(2 * seg, block)
        far_ref, k = far_rows[f]
        far_re, far_im = far_ref[k, 0], far_ref[k, 1]
        cols = jnp.concatenate(
            [jnp.concatenate([far_re, far_im], axis=0), jnp.concatenate([far_im, -far_re], axis=0)], axis=1
        )
        cross = lax.dot_general(own, cols, (((0,), (0,)), ((), ())), preferred_element_type=jnp.float32)
        at = piece * SUB + f
        own_inv = own_inv_ref[:, at : at + 1]
        square = jnp.square(far_re.astype(jnp.float32)) + jnp.square(far_im.astype(jnp.float32))
        far_power = jnp.sum(square, axis=0, keepdims=True) * (1.0 / seg) + 1e-05
        far_inv = 1.0 / ((far_power + far_lift_ref[...]) * seg)
        for part in range(2):
            val = cross[:, part * block : (part + 1) * block]
            sym = 0.5 * (rounded(val * own_inv) + rounded(val * far_inv))
            own_scr[part, f] = sym.astype(jnp.bfloat16)
            turned = jnp.transpose(sym if part == 0 else -sym)
            far_scr[part, f] = turned.astype(jnp.bfloat16)
    me = me_ref[0]
    matrix = interleave()
    for k in range(2 * freq_count):
        scr = own_scr if k < freq_count else far_scr
        for j in range(groups):
            first = (lax.rem(me + k % freq_count, freq_count) * groups + j) * SUB
            rows = pl.ds(pl.multiple_of(first, SUB), SUB)
            turned = turned_rows(matrix, scr[0, :, rows, :], scr[1, :, rows, :])
            for n, (group, first_row, count) in enumerate(slots):
                if group != j:
                    continue
                for part in range(2):
                    vals = turned[first_row : first_row + count, :, part * block : (part + 1) * block]
                    outs[k * len(slots) + n][:, part] = vals.astype(jnp.bfloat16)


def cross_piece(piece, freq_count, groups, slots, places, me, own, far, own_inv, far_lift, before):
    half, _, seg, block = own.shape
    n_far, n_slots = len(far), len(slots)
    outputs = [(k, n) for k in range(2 * freq_count) for n in range(n_slots)]
    spots = [m for m, (_, n) in enumerate(outputs) if places[n][2]]
    held = [before[outputs[m][0]][outputs[m][1]] for m in spots]
    flat = pl.pallas_call(
        functools.partial(cross_kernel, piece, freq_count, groups, slots, len(held), n_far),
        grid=(1,),
        in_specs=[
            pl.BlockSpec(memory_space=pltpu.SMEM),
            pl.BlockSpec((SUB, 2, seg, block), lambda i: (piece, 0, 0, 0)),
            pl.BlockSpec((block, half), lambda i: (0, 0)),
            pl.BlockSpec((1, block), lambda i: (0, 0)),
        ]
        + [pl.BlockSpec(x.shape, lambda i: (0, 0, 0, 0)) for x in far]
        + [pl.BlockSpec(memory_space=pl.ANY)] * len(held),
        out_specs=[
            pl.BlockSpec((slots[n][2], 2, SUB, block), functools.partial(lambda at, i: (0, 0, at, 0), places[n][1]))
            for _, n in outputs
        ],
        out_shape=[jax.ShapeDtypeStruct((slots[n][2], 2, places[n][0], block), jnp.bfloat16) for _, n in outputs],
        scratch_shapes=[pltpu.VMEM((2, SUB, block, block), jnp.bfloat16)] * 2,
        input_output_aliases={4 + n_far + i: m for i, m in enumerate(spots)},
        compiler_params=pltpu.CompilerParams(vmem_limit_bytes=VMEM_BYTES),
        cost_estimate=pl.CostEstimate(
            flops=SUB * 8 * seg * block * block, bytes_accessed=SUB * 16 * seg * block, transcendentals=0
        ),
        name="cross_piece",
    )(me, own, own_inv, far_lift, *far, *held)
    return [flat[k * n_slots : (k + 1) * n_slots] for k in range(2 * freq_count)]


def lag_kernel(sources, n_given, n_held, to_output, lag_ref, back_ref, *refs):
    n_pieces = sum(sources)
    pieces, given = refs[:n_pieces], refs[n_pieces : n_pieces + n_given]
    out_ref, lag_scr, norm_scr = refs[n_pieces + n_given + n_held :][:3]
    rows = pieces[0].shape[0]
    block = pieces[0].shape[3]
    width = AT_ONCE * block
    row_ref = refs[-1] if to_output else out_ref
    first = SUB - rows if to_output else 0

    def column(r):
        parts, at = [], 0
        for count in sources:
            for part in range(2):
                parts += [piece[r, part] for piece in pieces[at : at + count]]
            at += count
        return jnp.concatenate(parts, axis=0)

    for r in range(0, rows, AT_ONCE):
        cols = jnp.concatenate([column(r + k) for k in range(AT_ONCE)], axis=1)
        lag_scr[...] = jnp.dot(lag_ref[...], cols, preferred_element_type=jnp.float32)
        total = jnp.zeros((8, width), jnp.float32)
        for at in range(0, LAGS, SLICE):
            lag_re, lag_im = lag_scr[at : at + SLICE], lag_scr[LAGS + at : LAGS + at + SLICE]
            energy = lag_re * lag_re + lag_im * lag_im
            lag_scr[LAGS + at : LAGS + at + SLICE] = energy
            total += jnp.sum(energy.reshape(SLICE // 8, 8, width), axis=0)
        floor = (0.25 / LAGS) * jnp.sum(total, axis=0, keepdims=True) + 1e-05
        for at in range(0, LAGS, SLICE):
            scale = lax.rsqrt(lag_scr[LAGS + at : LAGS + at + SLICE] + floor)
            norm_scr[at : at + SLICE] = (lag_scr[at : at + SLICE] * scale).astype(jnp.bfloat16)
        lag_scr[: 2 * F] = jnp.dot(back_ref[...], norm_scr[...], preferred_element_type=jnp.float32)
        for at in range(0, 2 * F, SLICE):
            back = (lag_scr[at : at + SLICE] * (1.0 / math.sqrt(LAGS))).astype(jnp.bfloat16)
            for k in range(AT_ONCE):
                row_ref[first + r + k, at : at + SLICE] = back[:, k * block : (k + 1) * block]
    if to_output:
        matrix = interleave()
        for part in range(2):
            for k in range(0, F, 2 * SUB):
                at = part * F + k
                whole = [x[:, at : at + 2 * SUB] for x in given] + [row_ref[first:, at : at + 2 * SUB]]
                whole = jnp.concatenate(whole, axis=0)
                turned = turned_rows(matrix, whole[:, :SUB], whole[:, SUB:])
                for n in range(2):
                    bins = turned[:, :, n * block : (n + 1) * block]
                    out_ref[0, part, k + n * SUB : k + (n + 1) * SUB] = bins.astype(jnp.bfloat16)


def lag_group(group, groups, lag_table, back_table, sources, given, before, to_output=True):
    pieces = [piece for source in sources for piece in source]
    rows, _, _, block = pieces[0].shape
    if to_output:
        out_spec = pl.BlockSpec((1, 2, F, SUB, block), lambda i: (0, 0, 0, group, 0))
        out_shape = jax.ShapeDtypeStruct((1, 2, F, SUB * groups, block), jnp.bfloat16)
    else:
        out_spec = pl.BlockSpec((rows, 2 * F, block), lambda i: (0, 0, 0))
        out_shape = jax.ShapeDtypeStruct((rows, 2 * F, block), jnp.bfloat16)
    scratch = [
        pltpu.VMEM((2 * LAGS, AT_ONCE * block), jnp.float32),
        pltpu.VMEM((LAGS, AT_ONCE * block), jnp.bfloat16),
        pltpu.VMEM((SUB, 2 * F, block), jnp.bfloat16),
    ]
    return pl.pallas_call(
        functools.partial(lag_kernel, [len(source) for source in sources], len(given), len(before), to_output),
        grid=(1,),
        in_specs=[pl.BlockSpec(lag_table.shape, lambda i: (0, 0)), pl.BlockSpec(back_table.shape, lambda i: (0, 0))]
        + [pl.BlockSpec(piece.shape, lambda i: (0, 0, 0, 0)) for piece in pieces]
        + [pl.BlockSpec(x.shape, lambda i: (0, 0, 0)) for x in given]
        + [pl.BlockSpec(memory_space=pl.ANY)] * len(before),
        out_specs=out_spec,
        out_shape=out_shape,
        scratch_shapes=scratch,
        input_output_aliases={2 + len(pieces) + len(given): 0} if before else {},
        compiler_params=pltpu.CompilerParams(vmem_limit_bytes=VMEM_BYTES),
        cost_estimate=NO_COST,
        name="lag_group",
    )(lag_table, back_table, *pieces, *given, *before)


def shards(spectra, seg_mask):
    tile_count, freq_count = lax.axis_size("tile"), lax.axis_size("freq")
    half_axis = tile_count // 2
    _, seg, band, block = spectra.shape
    half = band // 2
    n_sub = half // SUB
    groups = block // freq_count // SUB
    me = lax.axis_index("freq")
    side = lax.axis_index("tile") // half_axis
    keep_from, send_from = side * half, (1 - side) * half

    across = [(t, (t + half_axis) % tile_count) for t in range(tile_count)]

    def along(block, d, cross):
        route = []
        for h in range(freq_count):
            for t in range(tile_count):
                there = (t + half_axis * cross) % tile_count
                route.append((h * tile_count + t, (h + d) % freq_count * tile_count + there))
        return lax.ppermute(block, ("freq", "tile"), route)

    keep_sub, send_sub = side * n_sub, (1 - side) * n_sub
    *pieces, power = prepare(spectra, seg_mask, send_sub, 1, (SHORT, SUB - SHORT))
    send_power = [power]
    far = [lax.ppermute(piece, "tile", across) for piece in pieces]
    rest, far[0] = lax.optimization_barrier((spectra, far[0]))
    pieces = []
    for i in range(1, n_sub):
        *both, power = prepare(rest, seg_mask, send_sub + i, 1, (SUB // 2, SUB // 2))
        rest, both = lax.optimization_barrier((rest, both))
        pieces += both
        send_power.append(power)
    own, own_power = prepare(rest, seg_mask, keep_sub, n_sub, (half,))
    send_power = jnp.concatenate(send_power, axis=0)

    total = lax.psum(jnp.sum(own_power, axis=0) + jnp.sum(send_power, axis=0), "freq")
    lift = WATER * (total / F)[None, :]
    own_inv = (1.0 / ((own_power + lift) * seg)).T
    local = jnp.arange(half, dtype=jnp.int32)
    lag_cols = []
    for mine in (True, False):
        for d in range(freq_count):
            freqs = (me - d) % freq_count * band + (keep_from if mine else send_from) + local
            cos_tab, sin_tab = dft_tables(freqs)
            lag_cols.append(jnp.concatenate([cos_tab, sin_tab], axis=0))
            lag_cols.append(jnp.concatenate([-sin_tab, cos_tab], axis=0))
    lag_table = jnp.concatenate(lag_cols, axis=1)
    cos_tab, sin_tab = dft_tables(jnp.arange(F, dtype=jnp.int32))
    back_table = jnp.concatenate([cos_tab, -sin_tab], axis=1).T

    far_total = None
    for i, piece in enumerate(pieces):
        if i == 2:
            shape = piece.shape
            piece, terms, own_inv, lag_table, back_table = lax.optimization_barrier(
                (piece, exact_terms(total), own_inv, lag_table, back_table)
            )
            piece = jnp.concatenate([piece.reshape(-1, block), terms], axis=0)
        if i >= 2:
            piece, far[-DEPTH] = lax.optimization_barrier((piece, far[-DEPTH]))
        got = lax.ppermute(piece, "tile", across)
        if i == 2:
            far_total = jnp.sum(got[-SUB:].astype(jnp.float32), axis=0)
            got = got[:-SUB].reshape(shape)
        far.append(got)
    if far_total is None:
        far_total = lax.ppermute(total, "tile", across)
    far_lift = WATER * (far_total / F)[None, :]

    n_split = groups // 2 if n_sub > 1 else 0
    slots = [(j, 0, SUB) for j in range(groups if groups == 1 else n_split)]
    if groups > 1:
        slots += [(j, first_row, SUB // 2) for j in range(n_split, groups) for first_row in (0, SUB // 2)]
    me_arr = me.astype(jnp.int32).reshape(1)
    ready = max(2 * n_sub - 3, 0)
    far[ready], lag_table, back_table, own_inv, far_lift, own = lax.optimization_barrier(
        (far[ready], lag_table, back_table, own_inv, far_lift, own)
    )
    early, sym = None, None
    for i in range(n_sub):
        last = i == n_sub - 1
        if last:
            early = sym
            split = (SUB, 0, False)
        else:
            split = (half - SUB, i, i > 0)
        places = [split if n < n_split else (half, i, i > 0) for n in range(len(slots))]
        sym = cross_piece(i, freq_count, groups, slots, places, me_arr, own, far[2 * i : 2 * i + 2], own_inv, far_lift, sym)

    stages = [(n, True) for n in range(n_split)] + [(n, False) for n in range(len(slots))]
    arrived = {}
    for m, (n, is_early) in enumerate(stages):
        made = early if is_early else sym
        outgoing = [made[k][n] for k in range(1, 2 * freq_count)]
        place = m - 2 * n_split
        if place >= 2 or 0 <= place < n_split:
            waited = stages[m - 2 if place >= 2 else place]
            outgoing, arrived[waited] = lax.optimization_barrier((outgoing, arrived[waited]))
        arrived[n, is_early] = [along(outgoing[k - 1], k % freq_count, k // freq_count) for k in range(1, 2 * freq_count)]
    out, given = [], []
    for n, (group, first_row, count) in enumerate(slots):
        parts = ([(early, True)] if n < n_split else []) + [(sym, False)]
        sources = [
            [made[0][n] if k == 0 else arrived[n, is_early][k - 1] for made, is_early in parts]
            for k in range(2 * freq_count)
        ]
        if first_row + count < SUB:
            given = [lag_group(group, groups, lag_table, back_table, sources, [], [], to_output=False)]
        else:
            out = [lag_group(group, groups, lag_table, back_table, sources, given if first_row else [], out)]
    return out[0]


def solution(mesh):
    placed = (P(None, None, "freq", "tile"), P(None, "tile"))
    return jax.shard_map(
        shards,
        mesh=mesh,
        in_specs=placed,
        out_specs=P("tile", None, None, "freq", None),
        check_vma=False,
    )
```

```python
import functools
import math

import jax
import jax.numpy as jnp
from jax import lax
from jax.experimental import pallas as pl
from jax.experimental.pallas import tpu as pltpu
from jax.sharding import PartitionSpec as P

F = 256
LAGS = 512
WATER = 0.05
SUB = 16
SHORT = 4
DEPTH = 3
AT_ONCE = 4
PARTS = 4
SLICE = 32
VMEM_BYTES = 48 * 2**20
NO_COST = pl.CostEstimate(flops=0, bytes_accessed=0, transcendentals=0)


def dft_tables(freq_index):
    lag_index = jnp.arange(LAGS, dtype=jnp.int32)[:, None]
    phase = (lag_index * freq_index[None, :] % LAGS).astype(jnp.float32) * (2.0 * math.pi / LAGS)
    return jnp.cos(phase).astype(jnp.bfloat16), jnp.sin(phase).astype(jnp.bfloat16)


def rounded(x):
    return x.astype(jnp.bfloat16).astype(jnp.float32)


def interleave():
    row = lax.broadcasted_iota(jnp.int32, (SUB * SUB, SUB * SUB), 0)
    col = lax.broadcasted_iota(jnp.int32, (SUB * SUB, SUB * SUB), 1)
    return jnp.where(col == row % SUB * SUB + row // SUB, 1.0, 0.0).astype(jnp.bfloat16)


def turned_rows(matrix, left, right):
    lanes = left.shape[2]
    both = jnp.concatenate([left.reshape(SUB * SUB, lanes), right.reshape(SUB * SUB, lanes)], axis=1)
    return jnp.dot(matrix, both, preferred_element_type=jnp.float32).reshape(SUB, SUB, 2 * lanes)


def prepare_rows(x_ref, mask_ref, s, matrix, parts):
    lanes = mask_ref.shape[1]
    mask = mask_ref[s : s + SUB].astype(jnp.float32)[None]
    turned = turned_rows(matrix, x_ref[0, s : s + SUB], x_ref[1, s : s + SUB])
    total = 0.0
    for part in range(2):
        val = turned[:, :, part * lanes : (part + 1) * lanes] * mask
        square = val * val
        total += square[:, :8] + square[:, 8:]
        at = 0
        for out in parts:
            count = out.shape[0]
            out[:, part, s : s + SUB] = val[at : at + count].astype(jnp.bfloat16)
            at += count
    return total


def prepare_kernel(at_ref, x_ref, mask_ref, out, power_ref):
    seg, lanes = mask_ref.shape
    matrix = interleave()
    total = jnp.zeros((SUB, 8, lanes), jnp.float32)
    for s in range(0, seg, SUB):
        total += prepare_rows(x_ref, mask_ref, s, matrix, [out])
    power_ref[...] = jnp.sum(total, axis=1) * (1.0 / seg) + 1e-05


def prepare_all(spectra, seg_mask, first, steps):
    _, seg, _, block = spectra.shape
    return pl.pallas_call(
        prepare_kernel,
        grid_spec=pltpu.PrefetchScalarGridSpec(
            num_scalar_prefetch=1,
            grid=(steps,),
            in_specs=[
                pl.BlockSpec((2, seg, SUB, block), lambda i, at: (0, 0, at[0] + i, 0)),
                pl.BlockSpec((seg, block), lambda i, at: (0, 0)),
            ],
            out_specs=[
                pl.BlockSpec((SUB, 2, seg, block), lambda i, at: (i, 0, 0, 0)),
                pl.BlockSpec((SUB, block), lambda i, at: (i, 0)),
            ],
        ),
        out_shape=[
            jax.ShapeDtypeStruct((steps * SUB, 2, seg, block), jnp.bfloat16),
            jax.ShapeDtypeStruct((steps * SUB, block), jnp.float32),
        ],
        compiler_params=pltpu.CompilerParams(vmem_limit_bytes=VMEM_BYTES),
        cost_estimate=pl.CostEstimate(
            flops=steps * SUB * seg * block * 8, bytes_accessed=steps * SUB * seg * block * 8, transcendentals=0
        ),
        name="prepare_all",
    )(first.astype(jnp.int32).reshape(1), spectra, seg_mask)


def prepare_piece_kernel(at_ref, x_hbm, mask_hbm, *refs):
    parts, power_ref, x_ref, mask_ref, sems = refs[:-4], refs[-4], refs[-3], refs[-2], refs[-1]
    seg, lanes = mask_ref.shape
    freqs = pl.ds(pl.multiple_of(at_ref[0] * SUB, SUB), SUB)
    chunk = seg // PARTS
    copies = []
    for n in range(PARTS):
        rows = pl.ds(n * chunk, chunk)
        copies.append(
            [
                pltpu.make_async_copy(mask_hbm.at[rows], mask_ref.at[rows], sems.at[2 * n]),
                pltpu.make_async_copy(x_hbm.at[:, rows, freqs], x_ref.at[:, rows], sems.at[2 * n + 1]),
            ]
        )
        for copy in copies[-1]:
            copy.start()
    matrix = interleave()
    total = jnp.zeros((SUB, 8, lanes), jnp.float32)
    for n in range(PARTS):
        for copy in copies[n]:
            copy.wait()
        for s in range(n * chunk, (n + 1) * chunk, SUB):
            total += prepare_rows(x_ref, mask_ref, s, matrix, parts)
    power_ref[...] = jnp.sum(total, axis=1) * (1.0 / seg) + 1e-05


def prepare(spectra, seg_mask, first, counts):
    _, seg, _, block = spectra.shape
    vmem = pl.BlockSpec(memory_space=pltpu.VMEM)
    return pl.pallas_call(
        prepare_piece_kernel,
        in_specs=[pl.BlockSpec(memory_space=pltpu.SMEM)] + [pl.BlockSpec(memory_space=pltpu.HBM)] * 2,
        out_specs=[vmem] * (len(counts) + 1),
        out_shape=[jax.ShapeDtypeStruct((count, 2, seg, block), jnp.bfloat16) for count in counts]
        + [jax.ShapeDtypeStruct((SUB, block), jnp.float32)],
        scratch_shapes=[
            pltpu.VMEM((2, seg, SUB, block), jnp.bfloat16),
            pltpu.VMEM((seg, block), jnp.int32),
            pltpu.SemaphoreType.DMA((2 * PARTS,)),
        ],
        compiler_params=pltpu.CompilerParams(vmem_limit_bytes=VMEM_BYTES),
        cost_estimate=pl.CostEstimate(
            flops=SUB * seg * block * 8, bytes_accessed=SUB * seg * block * 8, transcendentals=0
        ),
        name="prepare",
    )(first.astype(jnp.int32).reshape(1), spectra, seg_mask)


def exact_terms(x):
    terms, rest = [], x
    for _ in range(3):
        terms.append(lax.reduce_precision(rest, 8, 7))
        rest = rest - terms[-1]
    return jnp.pad(jnp.stack(terms).astype(jnp.bfloat16), ((0, SUB - 3), (0, 0)))


def cross_kernel(piece, freq_count, groups, slots, held, n_far, me_ref, own_ref, own_inv_ref, far_lift_ref, *refs):
    far_refs, outs, (own_scr, far_scr) = refs[:n_far], refs[n_far + held : -2], refs[-2:]
    seg = own_ref.shape[2]
    block = own_ref.shape[3]
    far_rows = [(far_ref, k) for far_ref in far_refs for k in range(far_ref.shape[0])]
    for f in range(SUB):
        own = own_ref[f].reshape(2 * seg, block)
        far_ref, k = far_rows[f]
        far_re, far_im = far_ref[k, 0], far_ref[k, 1]
        cols = jnp.concatenate(
            [jnp.concatenate([far_re, far_im], axis=0), jnp.concatenate([far_im, -far_re], axis=0)], axis=1
        )
        cross = lax.dot_general(own, cols, (((0,), (0,)), ((), ())), preferred_element_type=jnp.float32)
        at = piece * SUB + f
        own_inv = own_inv_ref[:, at : at + 1]
        square = jnp.square(far_re.astype(jnp.float32)) + jnp.square(far_im.astype(jnp.float32))
        far_power = jnp.sum(square, axis=0, keepdims=True) * (1.0 / seg) + 1e-05
        far_inv = 1.0 / ((far_power + far_lift_ref[...]) * seg)
        for part in range(2):
            val = cross[:, part * block : (part + 1) * block]
            sym = 0.5 * (rounded(val * own_inv) + rounded(val * far_inv))
            own_scr[part, f] = sym.astype(jnp.bfloat16)
            turned = jnp.transpose(sym if part == 0 else -sym)
            far_scr[part, f] = turned.astype(jnp.bfloat16)
    me = me_ref[0]
    matrix = interleave()
    for k in range(2 * freq_count):
        scr = own_scr if k < freq_count else far_scr
        for j in range(groups):
            first = (lax.rem(me + k % freq_count, freq_count) * groups + j) * SUB
            rows = pl.ds(pl.multiple_of(first, SUB), SUB)
            turned = turned_rows(matrix, scr[0, :, rows, :], scr[1, :, rows, :])
            for n, (group, first_row, count) in enumerate(slots):
                if group != j:
                    continue
                for part in range(2):
                    vals = turned[first_row : first_row + count, :, part * block : (part + 1) * block]
                    outs[k * len(slots) + n][:, part] = vals.astype(jnp.bfloat16)


def cross_piece(piece, freq_count, groups, slots, places, me, own, far, own_inv, far_lift, before):
    half, _, seg, block = own.shape
    n_far, n_slots = len(far), len(slots)
    outputs = [(k, n) for k in range(2 * freq_count) for n in range(n_slots)]
    spots = [m for m, (_, n) in enumerate(outputs) if places[n][2]]
    held = [before[outputs[m][0]][outputs[m][1]] for m in spots]
    flat = pl.pallas_call(
        functools.partial(cross_kernel, piece, freq_count, groups, slots, len(held), n_far),
        grid=(1,),
        in_specs=[
            pl.BlockSpec(memory_space=pltpu.SMEM),
            pl.BlockSpec((SUB, 2, seg, block), lambda i: (piece, 0, 0, 0)),
            pl.BlockSpec((block, half), lambda i: (0, 0)),
            pl.BlockSpec((1, block), lambda i: (0, 0)),
        ]
        + [pl.BlockSpec(x.shape, lambda i: (0, 0, 0, 0)) for x in far]
        + [pl.BlockSpec(memory_space=pl.ANY)] * len(held),
        out_specs=[
            pl.BlockSpec((slots[n][2], 2, SUB, block), functools.partial(lambda at, i: (0, 0, at, 0), places[n][1]))
            for _, n in outputs
        ],
        out_shape=[jax.ShapeDtypeStruct((slots[n][2], 2, places[n][0], block), jnp.bfloat16) for _, n in outputs],
        scratch_shapes=[pltpu.VMEM((2, SUB, block, block), jnp.bfloat16)] * 2,
        input_output_aliases={4 + n_far + i: m for i, m in enumerate(spots)},
        compiler_params=pltpu.CompilerParams(vmem_limit_bytes=VMEM_BYTES),
        cost_estimate=pl.CostEstimate(
            flops=SUB * 8 * seg * block * block, bytes_accessed=SUB * 16 * seg * block, transcendentals=0
        ),
        name="cross_piece",
    )(me, own, own_inv, far_lift, *far, *held)
    return [flat[k * n_slots : (k + 1) * n_slots] for k in range(2 * freq_count)]


def lag_kernel(sources, group, n_given, n_held, to_output, lag_ref, back_ref, *refs):
    n_pieces = sum(sources)
    pieces, given = refs[:n_pieces], refs[n_pieces : n_pieces + n_given]
    out_ref, lag_scr, norm_scr, *rest = refs[n_pieces + n_given + n_held :]
    rows = pieces[0].shape[0]
    block = pieces[0].shape[3]
    width = AT_ONCE * block
    row_ref = rest[0] if to_output else out_ref
    first = SUB - rows if to_output else 0

    def column(r):
        parts, at = [], 0
        for count in sources:
            for part in range(2):
                parts += [piece[r, part] for piece in pieces[at : at + count]]
            at += count
        return jnp.concatenate(parts, axis=0)

    for r in range(0, rows, AT_ONCE):
        cols = jnp.concatenate([column(r + k) for k in range(AT_ONCE)], axis=1)
        lag_scr[...] = jnp.dot(lag_ref[...], cols, preferred_element_type=jnp.float32)
        total = jnp.zeros((8, width), jnp.float32)
        for at in range(0, LAGS, SLICE):
            lag_re, lag_im = lag_scr[at : at + SLICE], lag_scr[LAGS + at : LAGS + at + SLICE]
            energy = lag_re * lag_re + lag_im * lag_im
            lag_scr[LAGS + at : LAGS + at + SLICE] = energy
            total += jnp.sum(energy.reshape(SLICE // 8, 8, width), axis=0)
        floor = (0.25 / LAGS) * jnp.sum(total, axis=0, keepdims=True) + 1e-05
        for at in range(0, LAGS, SLICE):
            scale = lax.rsqrt(lag_scr[LAGS + at : LAGS + at + SLICE] + floor)
            norm_scr[at : at + SLICE] = (lag_scr[at : at + SLICE] * scale).astype(jnp.bfloat16)
        lag_scr[: 2 * F] = jnp.dot(back_ref[...], norm_scr[...], preferred_element_type=jnp.float32)
        for at in range(0, 2 * F, SLICE):
            back = (lag_scr[at : at + SLICE] * (1.0 / math.sqrt(LAGS))).astype(jnp.bfloat16)
            for k in range(AT_ONCE):
                row_ref[first + r + k, at : at + SLICE] = back[:, k * block : (k + 1) * block]
    if to_output:
        _, bins_ref, sems = rest
        matrix = interleave()
        copies = []
        chunk = 2 * F // PARTS
        for at in range(0, 2 * F, 2 * SUB):
            whole = [x[:, at : at + 2 * SUB] for x in given] + [row_ref[first:, at : at + 2 * SUB]]
            whole = jnp.concatenate(whole, axis=0)
            turned = turned_rows(matrix, whole[:, :SUB], whole[:, SUB:])
            for n in range(2):
                bins = turned[:, :, n * block : (n + 1) * block]
                bins_ref[at + n * SUB : at + (n + 1) * SUB] = bins.astype(jnp.bfloat16)
            if (at + 2 * SUB) % chunk == 0:
                start = at + 2 * SUB - chunk
                there = out_ref.at[0, start // F, pl.ds(start % F, chunk), pl.ds(group * SUB, SUB)]
                copies.append(pltpu.make_async_copy(bins_ref.at[pl.ds(start, chunk)], there, sems.at[start // chunk]))
                copies[-1].start()
        for copy in copies:
            copy.wait()


def lag_group(group, groups, lag_table, back_table, sources, given, before, to_output=True):
    pieces = [piece for source in sources for piece in source]
    rows, _, _, block = pieces[0].shape
    vmem, scratch = pl.BlockSpec(memory_space=pltpu.VMEM), [
        pltpu.VMEM((2 * LAGS, AT_ONCE * block), jnp.float32),
        pltpu.VMEM((LAGS, AT_ONCE * block), jnp.bfloat16),
    ]
    if to_output:
        out_spec = pl.BlockSpec(memory_space=pltpu.HBM)
        out_shape = jax.ShapeDtypeStruct((1, 2, F, SUB * groups, block), jnp.bfloat16)
        scratch += [
            pltpu.VMEM((SUB, 2 * F, block), jnp.bfloat16),
            pltpu.VMEM((2 * F, SUB, block), jnp.bfloat16),
            pltpu.SemaphoreType.DMA((PARTS,)),
        ]
    else:
        out_spec = vmem
        out_shape = jax.ShapeDtypeStruct((rows, 2 * F, block), jnp.bfloat16)
    return pl.pallas_call(
        functools.partial(lag_kernel, [len(source) for source in sources], group, len(given), len(before), to_output),
        in_specs=[vmem] * (2 + len(pieces) + len(given)) + [pl.BlockSpec(memory_space=pltpu.HBM)] * len(before),
        out_specs=out_spec,
        out_shape=out_shape,
        scratch_shapes=scratch,
        input_output_aliases={2 + len(pieces) + len(given): 0} if before else {},
        compiler_params=pltpu.CompilerParams(vmem_limit_bytes=VMEM_BYTES),
        cost_estimate=NO_COST,
        name="lag_group",
    )(lag_table, back_table, *pieces, *given, *before)


def shards(spectra, seg_mask):
    tile_count, freq_count = lax.axis_size("tile"), lax.axis_size("freq")
    half_axis = tile_count // 2
    _, seg, band, block = spectra.shape
    half = band // 2
    n_sub = half // SUB
    groups = block // freq_count // SUB
    me = lax.axis_index("freq")
    side = lax.axis_index("tile") // half_axis
    keep_from, send_from = side * half, (1 - side) * half

    across = [(t, (t + half_axis) % tile_count) for t in range(tile_count)]

    def along(block, d, cross):
        route = []
        for h in range(freq_count):
            for t in range(tile_count):
                there = (t + half_axis * cross) % tile_count
                route.append((h * tile_count + t, (h + d) % freq_count * tile_count + there))
        return lax.ppermute(block, ("freq", "tile"), route)

    keep_sub, send_sub = side * n_sub, (1 - side) * n_sub
    *pieces, power = prepare(spectra, seg_mask, send_sub, (SHORT, SUB - SHORT))
    send_power = [power]
    far = [lax.ppermute(piece, "tile", across) for piece in pieces]
    rest, far[0] = lax.optimization_barrier((spectra, far[0]))
    pieces = []
    for i in range(1, n_sub):
        *both, power = prepare(rest, seg_mask, send_sub + i, (SUB // 2, SUB // 2))
        rest, both = lax.optimization_barrier((rest, both))
        pieces += both
        send_power.append(power)
    own, own_power = prepare_all(rest, seg_mask, keep_sub, n_sub)
    send_power = jnp.concatenate(send_power, axis=0)

    total = lax.psum(jnp.sum(own_power, axis=0) + jnp.sum(send_power, axis=0), "freq")
    lift = WATER * (total / F)[None, :]
    own_inv = (1.0 / ((own_power + lift) * seg)).T
    local = jnp.arange(half, dtype=jnp.int32)
    lag_cols = []
    for mine in (True, False):
        for d in range(freq_count):
            freqs = (me - d) % freq_count * band + (keep_from if mine else send_from) + local
            cos_tab, sin_tab = dft_tables(freqs)
            lag_cols.append(jnp.concatenate([cos_tab, sin_tab], axis=0))
            lag_cols.append(jnp.concatenate([-sin_tab, cos_tab], axis=0))
    lag_table = jnp.concatenate(lag_cols, axis=1)
    cos_tab, sin_tab = dft_tables(jnp.arange(F, dtype=jnp.int32))
    back_table = jnp.concatenate([cos_tab, -sin_tab], axis=1).T

    far_total = None
    for i, piece in enumerate(pieces):
        if i == 2:
            shape = piece.shape
            piece, terms, own_inv, lag_table, back_table = lax.optimization_barrier(
                (piece, exact_terms(total), own_inv, lag_table, back_table)
            )
            piece = jnp.concatenate([piece.reshape(-1, block), terms], axis=0)
        if i >= 2:
            piece, far[-DEPTH] = lax.optimization_barrier((piece, far[-DEPTH]))
        got = lax.ppermute(piece, "tile", across)
        if i == 2:
            far_total = jnp.sum(got[-SUB:].astype(jnp.float32), axis=0)
            got = got[:-SUB].reshape(shape)
        far.append(got)
    if far_total is None:
        far_total = lax.ppermute(total, "tile", across)
    far_lift = WATER * (far_total / F)[None, :]

    n_split = groups // 2 if n_sub > 1 else 0
    slots = [(j, 0, SUB) for j in range(groups if groups == 1 else n_split)]
    if groups > 1:
        slots += [(j, first_row, SUB // 2) for j in range(n_split, groups) for first_row in (0, SUB // 2)]
    me_arr = me.astype(jnp.int32).reshape(1)
    ready = max(2 * n_sub - 3, 0)
    far[ready], lag_table, back_table, own_inv, far_lift, own = lax.optimization_barrier(
        (far[ready], lag_table, back_table, own_inv, far_lift, own)
    )
    early, sym = None, None
    for i in range(n_sub):
        last = i == n_sub - 1
        if last:
            early = sym
            split = (SUB, 0, False)
        else:
            split = (half - SUB, i, i > 0)
        places = [split if n < n_split else (half, i, i > 0) for n in range(len(slots))]
        sym = cross_piece(i, freq_count, groups, slots, places, me_arr, own, far[2 * i : 2 * i + 2], own_inv, far_lift, sym)

    stages = [(n, True) for n in range(n_split)] + [(n, False) for n in range(len(slots))]
    arrived = {}
    for m, (n, is_early) in enumerate(stages):
        made = early if is_early else sym
        outgoing = [made[k][n] for k in range(1, 2 * freq_count)]
        place = m - 2 * n_split
        if place >= 2 or 0 <= place < n_split:
            waited = stages[m - 2 if place >= 2 else place]
            outgoing, arrived[waited] = lax.optimization_barrier((outgoing, arrived[waited]))
        arrived[n, is_early] = [along(outgoing[k - 1], k % freq_count, k // freq_count) for k in range(1, 2 * freq_count)]
    out, given = [], []
    for n, (group, first_row, count) in enumerate(slots):
        parts = ([(early, True)] if n < n_split else []) + [(sym, False)]
        sources = [
            [made[0][n] if k == 0 else arrived[n, is_early][k - 1] for made, is_early in parts]
            for k in range(2 * freq_count)
        ]
        if first_row + count < SUB:
            given = [lag_group(group, groups, lag_table, back_table, sources, [], [], to_output=False)]
        else:
            out = [lag_group(group, groups, lag_table, back_table, sources, given if first_row else [], out)]
    return out[0]


def solution(mesh):
    placed = (P(None, None, "freq", "tile"), P(None, "tile"))
    return jax.shard_map(
        shards,
        mesh=mesh,
        in_specs=placed,
        out_specs=P("tile", None, None, "freq", None),
        check_vma=False,
    )
```

```python
import functools
import math

import jax
import jax.numpy as jnp
from jax import lax
from jax.experimental import pallas as pl
from jax.experimental.pallas import tpu as pltpu
from jax.sharding import PartitionSpec as P

F = 256
LAGS = 512
WATER = 0.05
SUB = 16
SHORT = 4
DEPTH = 3
AT_ONCE = 4
PARTS = 4
SLICE = 32
VMEM_BYTES = 48 * 2**20
NO_COST = pl.CostEstimate(flops=0, bytes_accessed=0, transcendentals=0)


def dft_tables(freq_index):
    lag_index = jnp.arange(LAGS, dtype=jnp.int32)[:, None]
    phase = (lag_index * freq_index[None, :] % LAGS).astype(jnp.float32) * (2.0 * math.pi / LAGS)
    return jnp.cos(phase).astype(jnp.bfloat16), jnp.sin(phase).astype(jnp.bfloat16)


def rounded(x):
    return x.astype(jnp.bfloat16).astype(jnp.float32)


def interleave():
    row = lax.broadcasted_iota(jnp.int32, (SUB * SUB, SUB * SUB), 0)
    col = lax.broadcasted_iota(jnp.int32, (SUB * SUB, SUB * SUB), 1)
    return jnp.where(col == row % SUB * SUB + row // SUB, 1.0, 0.0).astype(jnp.bfloat16)


def turned_rows(matrix, left, right):
    lanes = left.shape[2]
    both = jnp.concatenate([left.reshape(SUB * SUB, lanes), right.reshape(SUB * SUB, lanes)], axis=1)
    return jnp.dot(matrix, both, preferred_element_type=jnp.float32).reshape(SUB, SUB, 2 * lanes)


def prepare_kernel(at_ref, x_ref, mask_ref, *outs):
    parts, power_ref = outs[:-1], outs[-1]
    seg, lanes = mask_ref.shape
    matrix = interleave()
    total = jnp.zeros((SUB, 8, lanes), jnp.float32)
    for s in range(0, seg, SUB):
        mask = mask_ref[s : s + SUB].astype(jnp.float32)[None]
        turned = turned_rows(matrix, x_ref[0, s : s + SUB], x_ref[1, s : s + SUB])
        for part in range(2):
            val = turned[:, :, part * lanes : (part + 1) * lanes] * mask
            square = val * val
            total += square[:, :8] + square[:, 8:]
            at = 0
            for out in parts:
                count = out.shape[0]
                out[:, part, s : s + SUB] = val[at : at + count].astype(jnp.bfloat16)
                at += count
    power_ref[...] = jnp.sum(total, axis=1) * (1.0 / seg) + 1e-05


def prepare(spectra, seg_mask, first, steps, counts):
    _, seg, _, block = spectra.shape
    assert sum(counts) == steps * SUB and (steps == 1 or len(counts) == 1)
    out_specs = [pl.BlockSpec((min(count, SUB), 2, seg, block), lambda i, at: (i, 0, 0, 0)) for count in counts]
    out_shape = [jax.ShapeDtypeStruct((count, 2, seg, block), jnp.bfloat16) for count in counts]
    return pl.pallas_call(
        prepare_kernel,
        grid_spec=pltpu.PrefetchScalarGridSpec(
            num_scalar_prefetch=1,
            grid=(steps,),
            in_specs=[
                pl.BlockSpec((2, seg, SUB, block), lambda i, at: (0, 0, at[0] + i, 0)),
                pl.BlockSpec((seg, block), lambda i, at: (0, 0)),
            ],
            out_specs=out_specs + [pl.BlockSpec((SUB, block), lambda i, at: (i, 0))],
        ),
        out_shape=out_shape + [jax.ShapeDtypeStruct((steps * SUB, block), jnp.float32)],
        compiler_params=pltpu.CompilerParams(vmem_limit_bytes=VMEM_BYTES),
        cost_estimate=pl.CostEstimate(
            flops=steps * SUB * seg * block * 8, bytes_accessed=steps * SUB * seg * block * 8, transcendentals=0
        ),
        name="prepare",
    )(first.astype(jnp.int32).reshape(1), spectra, seg_mask)


def exact_terms(x):
    terms, rest = [], x
    for _ in range(3):
        terms.append(lax.reduce_precision(rest, 8, 7))
        rest = rest - terms[-1]
    return jnp.pad(jnp.stack(terms).astype(jnp.bfloat16), ((0, SUB - 3), (0, 0)))


def cross_kernel(piece, freq_count, groups, slots, held, n_far, me_ref, own_ref, own_inv_ref, far_lift_ref, *refs):
    far_refs, outs, (own_scr, far_scr) = refs[:n_far], refs[n_far + held : -2], refs[-2:]
    seg = own_ref.shape[2]
    block = own_ref.shape[3]
    far_rows = [(far_ref, k) for far_ref in far_refs for k in range(far_ref.shape[0])]
    for f in range(SUB):
        own = own_ref[f].reshape(2 * seg, block)
        far_ref, k = far_rows[f]
        far_re, far_im = far_ref[k, 0], far_ref[k, 1]
        cols = jnp.concatenate(
            [jnp.concatenate([far_re, far_im], axis=0), jnp.concatenate([far_im, -far_re], axis=0)], axis=1
        )
        cross = lax.dot_general(own, cols, (((0,), (0,)), ((), ())), preferred_element_type=jnp.float32)
        at = piece * SUB + f
        own_inv = own_inv_ref[:, at : at + 1]
        square = jnp.square(far_re.astype(jnp.float32)) + jnp.square(far_im.astype(jnp.float32))
        far_power = jnp.sum(square, axis=0, keepdims=True) * (1.0 / seg) + 1e-05
        far_inv = 1.0 / ((far_power + far_lift_ref[...]) * seg)
        for part in range(2):
            val = cross[:, part * block : (part + 1) * block]
            sym = 0.5 * (rounded(val * own_inv) + rounded(val * far_inv))
            own_scr[part, f] = sym.astype(jnp.bfloat16)
            turned = jnp.transpose(sym if part == 0 else -sym)
            far_scr[part, f] = turned.astype(jnp.bfloat16)
    me = me_ref[0]
    matrix = interleave()
    for k in range(2 * freq_count):
        scr = own_scr if k < freq_count else far_scr
        for j in range(groups):
            first = (lax.rem(me + k % freq_count, freq_count) * groups + j) * SUB
            rows = pl.ds(pl.multiple_of(first, SUB), SUB)
            turned = turned_rows(matrix, scr[0, :, rows, :], scr[1, :, rows, :])
            for out, (kind, first_row, count, _) in zip(outs, slots):
                low, high = max(first_row, j * SUB), min(first_row + count, (j + 1) * SUB)
                if kind != k or low >= high:
                    continue
                for part in range(2):
                    vals = turned[low - j * SUB : high - j * SUB, :, part * block : (part + 1) * block]
                    out[low - first_row : high - first_row, part] = vals.astype(jnp.bfloat16)


def cross_piece(piece, freq_count, groups, slots, me, own, far, own_inv, far_lift, made):
    half, _, seg, block = own.shape
    n_far = len(far)
    last = (piece + 1) * SUB == half
    slots = [slot for slot in slots if slot[3] == "all" or (slot[3] == "late") == last]
    counts = {"all": half, "early": half - SUB, "late": SUB}
    places = [0 if slot[3] == "late" else piece for slot in slots]
    spots = [n for n, slot in enumerate(slots) if slot in made]
    flat = pl.pallas_call(
        functools.partial(cross_kernel, piece, freq_count, groups, slots, len(spots), n_far),
        grid=(1,),
        in_specs=[
            pl.BlockSpec(memory_space=pltpu.SMEM),
            pl.BlockSpec((SUB, 2, seg, block), lambda i: (piece, 0, 0, 0)),
            pl.BlockSpec((block, half), lambda i: (0, 0)),
            pl.BlockSpec((1, block), lambda i: (0, 0)),
        ]
        + [pl.BlockSpec(x.shape, lambda i: (0, 0, 0, 0)) for x in far]
        + [pl.BlockSpec(memory_space=pl.ANY)] * len(spots),
        out_specs=[
            pl.BlockSpec((slot[2], 2, SUB, block), functools.partial(lambda at, i: (0, 0, at, 0), at))
            for slot, at in zip(slots, places)
        ],
        out_shape=[jax.ShapeDtypeStruct((slot[2], 2, counts[slot[3]], block), jnp.bfloat16) for slot in slots],
        scratch_shapes=[pltpu.VMEM((2, SUB, block, block), jnp.bfloat16)] * 2,
        input_output_aliases={4 + n_far + i: n for i, n in enumerate(spots)},
        compiler_params=pltpu.CompilerParams(vmem_limit_bytes=VMEM_BYTES),
        cost_estimate=pl.CostEstimate(
            flops=SUB * 8 * seg * block * block, bytes_accessed=SUB * 16 * seg * block, transcendentals=0
        ),
        name="cross_piece",
    )(me, own, own_inv, far_lift, *far, *[made[slots[n]] for n in spots])
    return {**made, **dict(zip(slots, flat))}


def lag_kernel(sources, rows, group, n_given, n_held, to_output, lag_ref, back_ref, *refs):
    n_pieces = sum(len(places) for places in sources)
    pieces, given = refs[:n_pieces], refs[n_pieces : n_pieces + n_given]
    out_ref, lag_scr, norm_scr, *rest = refs[n_pieces + n_given + n_held :]
    block = pieces[0].shape[3]
    width = AT_ONCE * block
    row_ref = rest[0] if to_output else out_ref
    first = SUB - rows if to_output else 0

    def column(r):
        parts, at = [], 0
        for places in sources:
            for part in range(2):
                parts += [piece[place + r, part] for piece, place in zip(pieces[at:], places)]
            at += len(places)
        return jnp.concatenate(parts, axis=0)

    for r in range(0, rows, AT_ONCE):
        cols = jnp.concatenate([column(r + k) for k in range(AT_ONCE)], axis=1)
        lag_scr[...] = jnp.dot(lag_ref[...], cols, preferred_element_type=jnp.float32)
        total = jnp.zeros((8, width), jnp.float32)
        for at in range(0, LAGS, SLICE):
            lag_re, lag_im = lag_scr[at : at + SLICE], lag_scr[LAGS + at : LAGS + at + SLICE]
            energy = lag_re * lag_re + lag_im * lag_im
            lag_scr[LAGS + at : LAGS + at + SLICE] = energy
            total += jnp.sum(energy.reshape(SLICE // 8, 8, width), axis=0)
        floor = (0.25 / LAGS) * jnp.sum(total, axis=0, keepdims=True) + 1e-05
        for at in range(0, LAGS, SLICE):
            scale = lax.rsqrt(lag_scr[LAGS + at : LAGS + at + SLICE] + floor)
            norm_scr[at : at + SLICE] = (lag_scr[at : at + SLICE] * scale).astype(jnp.bfloat16)
        lag_scr[: 2 * F] = jnp.dot(back_ref[...], norm_scr[...], preferred_element_type=jnp.float32)
        for at in range(0, 2 * F, SLICE):
            back = (lag_scr[at : at + SLICE] * (1.0 / math.sqrt(LAGS))).astype(jnp.bfloat16)
            for k in range(AT_ONCE):
                row_ref[first + r + k, at : at + SLICE] = back[:, k * block : (k + 1) * block]
    if to_output:
        _, bins_ref, sems = rest
        matrix = interleave()
        copies = []
        chunk = 2 * F // PARTS
        for at in range(0, 2 * F, 2 * SUB):
            whole = [x[:, at : at + 2 * SUB] for x in given] + [row_ref[first:, at : at + 2 * SUB]]
            whole = jnp.concatenate(whole, axis=0)
            turned = turned_rows(matrix, whole[:, :SUB], whole[:, SUB:])
            for n in range(2):
                bins = turned[:, :, n * block : (n + 1) * block]
                bins_ref[at + n * SUB : at + (n + 1) * SUB] = bins.astype(jnp.bfloat16)
            if (at + 2 * SUB) % chunk == 0:
                start = at + 2 * SUB - chunk
                there = out_ref.at[0, start // F, pl.ds(start % F, chunk), pl.ds(group * SUB, SUB)]
                copies.append(pltpu.make_async_copy(bins_ref.at[pl.ds(start, chunk)], there, sems.at[start // chunk]))
                copies[-1].start()
        for copy in copies:
            copy.wait()


def lag_group(rows, group, groups, lag_table, back_table, sources, given, before, to_output=True):
    pieces = [piece for source in sources for piece, _ in source]
    places = [[place for _, place in source] for source in sources]
    block = pieces[0].shape[3]
    vmem, scratch = pl.BlockSpec(memory_space=pltpu.VMEM), [
        pltpu.VMEM((2 * LAGS, AT_ONCE * block), jnp.float32),
        pltpu.VMEM((LAGS, AT_ONCE * block), jnp.bfloat16),
    ]
    if to_output:
        out_spec = pl.BlockSpec(memory_space=pltpu.HBM)
        out_shape = jax.ShapeDtypeStruct((1, 2, F, SUB * groups, block), jnp.bfloat16)
        scratch += [
            pltpu.VMEM((SUB, 2 * F, block), jnp.bfloat16),
            pltpu.VMEM((2 * F, SUB, block), jnp.bfloat16),
            pltpu.SemaphoreType.DMA((PARTS,)),
        ]
    else:
        out_spec = vmem
        out_shape = jax.ShapeDtypeStruct((rows, 2 * F, block), jnp.bfloat16)
    return pl.pallas_call(
        functools.partial(lag_kernel, places, rows, group, len(given), len(before), to_output),
        in_specs=[vmem] * (2 + len(pieces) + len(given)) + [pl.BlockSpec(memory_space=pltpu.HBM)] * len(before),
        out_specs=out_spec,
        out_shape=out_shape,
        scratch_shapes=scratch,
        input_output_aliases={2 + len(pieces) + len(given): 0} if before else {},
        compiler_params=pltpu.CompilerParams(vmem_limit_bytes=VMEM_BYTES),
        cost_estimate=NO_COST,
        name="lag_group",
    )(lag_table, back_table, *pieces, *given, *before)


def shards(spectra, seg_mask):
    tile_count, freq_count = lax.axis_size("tile"), lax.axis_size("freq")
    half_axis = tile_count // 2
    _, seg, band, block = spectra.shape
    half = band // 2
    n_sub = half // SUB
    groups = block // freq_count // SUB
    me = lax.axis_index("freq")
    side = lax.axis_index("tile") // half_axis
    keep_from, send_from = side * half, (1 - side) * half

    across = [(t, (t + half_axis) % tile_count) for t in range(tile_count)]

    def moved(block, d, distance):
        route = []
        for h in range(freq_count):
            for t in range(tile_count):
                route.append((h * tile_count + t, (h + d) % freq_count * tile_count + (t + distance) % tile_count))
        return lax.ppermute(block, ("freq", "tile"), route)

    keep_sub, send_sub = side * n_sub, (1 - side) * n_sub
    *pieces, power = prepare(spectra, seg_mask, send_sub, 1, (SHORT, SUB - SHORT))
    send_power = [power]
    far = [lax.ppermute(piece, "tile", across) for piece in pieces]
    rest, far[0] = lax.optimization_barrier((spectra, far[0]))
    pieces = []
    for i in range(1, n_sub):
        *both, power = prepare(rest, seg_mask, send_sub + i, 1, (SUB // 2, SUB // 2))
        rest, both = lax.optimization_barrier((rest, both))
        pieces += both
        send_power.append(power)
    own, own_power = prepare(rest, seg_mask, keep_sub, n_sub, (half,))
    send_power = jnp.concatenate(send_power, axis=0)

    total = lax.psum(jnp.sum(own_power, axis=0) + jnp.sum(send_power, axis=0), "freq")
    lift = WATER * (total / F)[None, :]
    own_inv = (1.0 / ((own_power + lift) * seg)).T
    local = jnp.arange(half, dtype=jnp.int32)
    lag_cols = []
    for mine in (True, False):
        for d in range(freq_count):
            freqs = (me - d) % freq_count * band + (keep_from if mine else send_from) + local
            cos_tab, sin_tab = dft_tables(freqs)
            lag_cols.append(jnp.concatenate([cos_tab, sin_tab], axis=0))
            lag_cols.append(jnp.concatenate([-sin_tab, cos_tab], axis=0))
    lag_table = jnp.concatenate(lag_cols, axis=1)
    cos_tab, sin_tab = dft_tables(jnp.arange(F, dtype=jnp.int32))
    back_table = jnp.concatenate([cos_tab, -sin_tab], axis=1).T

    far_total = None
    for i, piece in enumerate(pieces):
        if i == 2:
            shape = piece.shape
            piece, terms, own_inv, lag_table, back_table = lax.optimization_barrier(
                (piece, exact_terms(total), own_inv, lag_table, back_table)
            )
            piece = jnp.concatenate([piece.reshape(-1, block), terms], axis=0)
        if i >= 2:
            piece, far[-DEPTH] = lax.optimization_barrier((piece, far[-DEPTH]))
        got = lax.ppermute(piece, "tile", across)
        if i == 2:
            far_total = jnp.sum(got[-SUB:].astype(jnp.float32), axis=0)
            got = got[:-SUB].reshape(shape)
        far.append(got)
    if far_total is None:
        far_total = lax.ppermute(total, "tile", across)
    far_lift = WATER * (far_total / F)[None, :]

    n_split = groups // 2 if n_sub > 1 else 0
    full = groups * SUB
    early_rows = n_split * SUB
    first_parts = [(j * SUB, SUB, "early") for j in range(n_split)]
    late_parts = [(0, early_rows, "late")] if n_split else []
    own_rest = [(early_rows, full - early_rows, "all")]
    halves = [(row, SUB // 2, "all") for row in range(early_rows, full, SUB // 2)] if groups > 1 else own_rest
    places = [first_parts + late_parts + (own_rest if k < freq_count else halves) for k in range(2 * freq_count)]
    slots = [(k, *place) for k in range(2 * freq_count) for place in places[k]]
    me_arr = me.astype(jnp.int32).reshape(1)
    ready = max(2 * n_sub - 3, 0)
    far[ready], lag_table, back_table, own_inv, far_lift, own = lax.optimization_barrier(
        (far[ready], lag_table, back_table, own_inv, far_lift, own)
    )
    made = {}
    for i in range(n_sub):
        made = cross_piece(i, freq_count, groups, slots, me_arr, own, far[2 * i : 2 * i + 2], own_inv, far_lift, made)

    arrived = {}

    def send(place, wait_for=None):
        kinds = [k for k in range(1, 2 * freq_count) if place in places[k]]
        outgoing = [made[(k, *place)] for k in kinds]
        if wait_for is not None:
            outgoing, arrived[wait_for] = lax.optimization_barrier((outgoing, arrived[wait_for]))
        moves = [moved(x, k % freq_count, half_axis * (k // freq_count)) for k, x in zip(kinds, outgoing)]
        arrived[place] = dict(zip(kinds, moves))

    for place in first_parts + late_parts:
        send(place)
    if own_rest != halves:
        send(own_rest[0])
    chain = first_parts + halves
    for n, place in enumerate(halves, start=len(first_parts)):
        send(place, chain[n - 2] if n >= 2 else None)

    out, given = [], []
    for place in first_parts + halves:
        first_row, rows, _ = place
        if place in halves[-2:-1]:
            arrived[place], out = lax.optimization_barrier((arrived[place], out))
        sources = []
        for k in range(2 * freq_count):
            holds = [hold for hold in places[k] if hold[0] <= first_row < hold[0] + hold[1]]
            sources.append([(arrived[hold][k] if k else made[(0, *hold)], first_row - hold[0]) for hold in holds])
        group, ends = first_row // SUB, (first_row + rows) % SUB == 0
        done = lag_group(rows, group, groups, lag_table, back_table, sources, given, out if ends else [], to_output=ends)
        if ends:
            given, out = [], [done]
        else:
            given = [done]
    return out[0]


def solution(mesh):
    placed = (P(None, None, "freq", "tile"), P(None, "tile"))
    return jax.shard_map(
        shards,
        mesh=mesh,
        in_specs=placed,
        out_specs=P("tile", None, None, "freq", None),
        check_vma=False,
    )
```

```python
import functools
import math

import jax
import jax.numpy as jnp
from jax import lax
from jax.experimental import pallas as pl
from jax.experimental.pallas import tpu as pltpu
from jax.sharding import PartitionSpec as P

F = 256
LAGS = 512
WATER = 0.05
SUB = 16
SHORT = 2
DEPTH = 3
AT_ONCE = 4
PARTS = 4
SLICE = 32
VMEM_BYTES = 48 * 2**20
NO_COST = pl.CostEstimate(flops=0, bytes_accessed=0, transcendentals=0)


def dft_tables(freq_index):
    lag_index = jnp.arange(LAGS, dtype=jnp.int32)[:, None]
    phase = (lag_index * freq_index[None, :] % LAGS).astype(jnp.float32) * (2.0 * math.pi / LAGS)
    return jnp.cos(phase).astype(jnp.bfloat16), jnp.sin(phase).astype(jnp.bfloat16)


def rounded(x):
    return x.astype(jnp.bfloat16).astype(jnp.float32)


def interleave():
    row = lax.broadcasted_iota(jnp.int32, (SUB * SUB, SUB * SUB), 0)
    col = lax.broadcasted_iota(jnp.int32, (SUB * SUB, SUB * SUB), 1)
    return jnp.where(col == row % SUB * SUB + row // SUB, 1.0, 0.0).astype(jnp.bfloat16)


def turned_rows(matrix, left, right):
    lanes = left.shape[2]
    both = jnp.concatenate([left.reshape(SUB * SUB, lanes), right.reshape(SUB * SUB, lanes)], axis=1)
    return jnp.dot(matrix, both, preferred_element_type=jnp.float32).reshape(SUB, SUB, 2 * lanes)


def prepare_kernel(at_ref, x_ref, mask_ref, *outs):
    parts, power_ref = outs[:-1], outs[-1]
    seg, lanes = mask_ref.shape
    matrix = interleave()
    total = jnp.zeros((SUB, 8, lanes), jnp.float32)
    for s in range(0, seg, SUB):
        mask = mask_ref[s : s + SUB].astype(jnp.float32)[None]
        turned = turned_rows(matrix, x_ref[0, s : s + SUB], x_ref[1, s : s + SUB])
        for part in range(2):
            val = turned[:, :, part * lanes : (part + 1) * lanes] * mask
            square = val * val
            total += square[:, :8] + square[:, 8:]
            at = 0
            for out in parts:
                count = out.shape[0]
                out[:, part, s : s + SUB] = val[at : at + count].astype(jnp.bfloat16)
                at += count
    power_ref[...] = jnp.sum(total, axis=1) * (1.0 / seg) + 1e-05


def prepare(spectra, seg_mask, first, steps, counts):
    _, seg, _, block = spectra.shape
    assert sum(counts) == steps * SUB and (steps == 1 or len(counts) == 1)
    out_specs = [pl.BlockSpec((min(count, SUB), 2, seg, block), lambda i, at: (i, 0, 0, 0)) for count in counts]
    out_shape = [jax.ShapeDtypeStruct((count, 2, seg, block), jnp.bfloat16) for count in counts]
    return pl.pallas_call(
        prepare_kernel,
        grid_spec=pltpu.PrefetchScalarGridSpec(
            num_scalar_prefetch=1,
            grid=(steps,),
            in_specs=[
                pl.BlockSpec((2, seg, SUB, block), lambda i, at: (0, 0, at[0] + i, 0)),
                pl.BlockSpec((seg, block), lambda i, at: (0, 0)),
            ],
            out_specs=out_specs + [pl.BlockSpec((SUB, block), lambda i, at: (i, 0))],
        ),
        out_shape=out_shape + [jax.ShapeDtypeStruct((steps * SUB, block), jnp.float32)],
        compiler_params=pltpu.CompilerParams(vmem_limit_bytes=VMEM_BYTES),
        cost_estimate=NO_COST,
        name="prepare",
    )(first.astype(jnp.int32).reshape(1), spectra, seg_mask)


def exact_terms(x):
    terms, rest = [], x
    for _ in range(3):
        terms.append(lax.reduce_precision(rest, 8, 7))
        rest = rest - terms[-1]
    return jnp.pad(jnp.stack(terms).astype(jnp.bfloat16), ((0, SUB - 3), (0, 0)))


def cross_kernel(piece, freq_count, groups, slots, held, n_far, me_ref, own_ref, own_inv_ref, far_lift_ref, *refs):
    far_refs, outs, (own_scr, far_scr) = refs[:n_far], refs[n_far + held : -2], refs[-2:]
    seg = own_ref.shape[2]
    block = own_ref.shape[3]
    far_rows = [(far_ref, k) for far_ref in far_refs for k in range(far_ref.shape[0])]
    for f in range(SUB):
        own = own_ref[f].reshape(2 * seg, block)
        far_ref, k = far_rows[f]
        far_re, far_im = far_ref[k, 0], far_ref[k, 1]
        cols = jnp.concatenate(
            [jnp.concatenate([far_re, far_im], axis=0), jnp.concatenate([far_im, -far_re], axis=0)], axis=1
        )
        cross = lax.dot_general(own, cols, (((0,), (0,)), ((), ())), preferred_element_type=jnp.float32)
        at = piece * SUB + f
        own_inv = own_inv_ref[:, at : at + 1]
        square = jnp.square(far_re.astype(jnp.float32)) + jnp.square(far_im.astype(jnp.float32))
        far_power = jnp.sum(square, axis=0, keepdims=True) * (1.0 / seg) + 1e-05
        far_inv = 1.0 / ((far_power + far_lift_ref[...]) * seg)
        for part in range(2):
            val = cross[:, part * block : (part + 1) * block]
            sym = 0.5 * (rounded(val * own_inv) + rounded(val * far_inv))
            own_scr[part, f] = sym.astype(jnp.bfloat16)
            turned = jnp.transpose(sym if part == 0 else -sym)
            far_scr[part, f] = turned.astype(jnp.bfloat16)
    me = me_ref[0]
    matrix = interleave()
    for k in range(2 * freq_count):
        scr = own_scr if k < freq_count else far_scr
        for j in range(groups):
            first = (lax.rem(me + k % freq_count, freq_count) * groups + j) * SUB
            rows = pl.ds(pl.multiple_of(first, SUB), SUB)
            turned = turned_rows(matrix, scr[0, :, rows, :], scr[1, :, rows, :])
            for out, (kind, first_row, count, _) in zip(outs, slots):
                low, high = max(first_row, j * SUB), min(first_row + count, (j + 1) * SUB)
                if kind != k or low >= high:
                    continue
                for part in range(2):
                    vals = turned[low - j * SUB : high - j * SUB, :, part * block : (part + 1) * block]
                    out[low - first_row : high - first_row, part] = vals.astype(jnp.bfloat16)


def cross_piece(piece, freq_count, groups, slots, me, own, far, own_inv, far_lift, made):
    half, _, seg, block = own.shape
    n_far = len(far)
    last = (piece + 1) * SUB == half
    slots = [slot for slot in slots if slot[3] == "all" or (slot[3] == "late") == last]
    counts = {"all": half, "early": half - SUB, "late": SUB}
    places = [0 if slot[3] == "late" else piece for slot in slots]
    spots = [n for n, slot in enumerate(slots) if slot in made]
    flat = pl.pallas_call(
        functools.partial(cross_kernel, piece, freq_count, groups, slots, len(spots), n_far),
        grid=(1,),
        in_specs=[
            pl.BlockSpec(memory_space=pltpu.SMEM),
            pl.BlockSpec((SUB, 2, seg, block), lambda i: (piece, 0, 0, 0)),
            pl.BlockSpec((block, half), lambda i: (0, 0)),
            pl.BlockSpec((1, block), lambda i: (0, 0)),
        ]
        + [pl.BlockSpec(x.shape, lambda i: (0, 0, 0, 0)) for x in far]
        + [pl.BlockSpec(memory_space=pl.ANY)] * len(spots),
        out_specs=[
            pl.BlockSpec((slot[2], 2, SUB, block), functools.partial(lambda at, i: (0, 0, at, 0), at))
            for slot, at in zip(slots, places)
        ],
        out_shape=[jax.ShapeDtypeStruct((slot[2], 2, counts[slot[3]], block), jnp.bfloat16) for slot in slots],
        scratch_shapes=[pltpu.VMEM((2, SUB, block, block), jnp.bfloat16)] * 2,
        input_output_aliases={4 + n_far + i: n for i, n in enumerate(spots)},
        compiler_params=pltpu.CompilerParams(vmem_limit_bytes=VMEM_BYTES),
        cost_estimate=pl.CostEstimate(
            flops=SUB * 8 * seg * block * block, bytes_accessed=SUB * 16 * seg * block, transcendentals=0
        ),
        name="cross_piece",
    )(me, own, own_inv, far_lift, *far, *[made[slots[n]] for n in spots])
    return {**made, **dict(zip(slots, flat))}


def lag_kernel(sources, rows, group, n_given, n_held, to_output, lag_ref, back_ref, *refs):
    n_pieces = sum(len(places) for places in sources)
    pieces, given = refs[:n_pieces], refs[n_pieces : n_pieces + n_given]
    out_ref, lag_scr, norm_scr, *rest = refs[n_pieces + n_given + n_held :]
    block = pieces[0].shape[3]
    width = AT_ONCE * block
    row_ref = rest[0] if to_output else out_ref
    first = SUB - rows if to_output else 0

    def column(r):
        parts, at = [], 0
        for places in sources:
            for part in range(2):
                parts += [piece[place + r, part] for piece, place in zip(pieces[at:], places)]
            at += len(places)
        return jnp.concatenate(parts, axis=0)

    for r in range(0, rows, AT_ONCE):
        cols = jnp.concatenate([column(r + k) for k in range(AT_ONCE)], axis=1)
        lag_scr[...] = jnp.dot(lag_ref[...], cols, preferred_element_type=jnp.float32)
        total = jnp.zeros((8, width), jnp.float32)
        for at in range(0, LAGS, SLICE):
            lag_re, lag_im = lag_scr[at : at + SLICE], lag_scr[LAGS + at : LAGS + at + SLICE]
            energy = lag_re * lag_re + lag_im * lag_im
            lag_scr[LAGS + at : LAGS + at + SLICE] = energy
            total += jnp.sum(energy.reshape(SLICE // 8, 8, width), axis=0)
        floor = (0.25 / LAGS) * jnp.sum(total, axis=0, keepdims=True) + 1e-05
        for at in range(0, LAGS, SLICE):
            scale = lax.rsqrt(lag_scr[LAGS + at : LAGS + at + SLICE] + floor)
            norm_scr[at : at + SLICE] = (lag_scr[at : at + SLICE] * scale).astype(jnp.bfloat16)
        lag_scr[: 2 * F] = jnp.dot(back_ref[...], norm_scr[...], preferred_element_type=jnp.float32)
        for at in range(0, 2 * F, SLICE):
            back = (lag_scr[at : at + SLICE] * (1.0 / math.sqrt(LAGS))).astype(jnp.bfloat16)
            for k in range(AT_ONCE):
                row_ref[first + r + k, at : at + SLICE] = back[:, k * block : (k + 1) * block]
    if to_output:
        _, bins_ref, sems = rest
        matrix = interleave()
        copies = []
        chunk = 2 * F // PARTS
        for at in range(0, 2 * F, 2 * SUB):
            whole = [x[:, at : at + 2 * SUB] for x in given] + [row_ref[first:, at : at + 2 * SUB]]
            whole = jnp.concatenate(whole, axis=0)
            turned = turned_rows(matrix, whole[:, :SUB], whole[:, SUB:])
            for n in range(2):
                bins = turned[:, :, n * block : (n + 1) * block]
                bins_ref[at + n * SUB : at + (n + 1) * SUB] = bins.astype(jnp.bfloat16)
            if (at + 2 * SUB) % chunk == 0:
                start = at + 2 * SUB - chunk
                there = out_ref.at[0, start // F, pl.ds(start % F, chunk), pl.ds(group * SUB, SUB)]
                copies.append(pltpu.make_async_copy(bins_ref.at[pl.ds(start, chunk)], there, sems.at[start // chunk]))
                copies[-1].start()
        for copy in copies:
            copy.wait()


def lag_group(rows, group, groups, lag_table, back_table, sources, given, before, to_output=True):
    pieces = [piece for source in sources for piece, _ in source]
    places = [[place for _, place in source] for source in sources]
    block = pieces[0].shape[3]
    vmem, scratch = pl.BlockSpec(memory_space=pltpu.VMEM), [
        pltpu.VMEM((2 * LAGS, AT_ONCE * block), jnp.float32),
        pltpu.VMEM((LAGS, AT_ONCE * block), jnp.bfloat16),
    ]
    if to_output:
        out_spec = pl.BlockSpec(memory_space=pltpu.HBM)
        out_shape = jax.ShapeDtypeStruct((1, 2, F, SUB * groups, block), jnp.bfloat16)
        scratch += [
            pltpu.VMEM((SUB, 2 * F, block), jnp.bfloat16),
            pltpu.VMEM((2 * F, SUB, block), jnp.bfloat16),
            pltpu.SemaphoreType.DMA((PARTS,)),
        ]
    else:
        out_spec = vmem
        out_shape = jax.ShapeDtypeStruct((rows, 2 * F, block), jnp.bfloat16)
    return pl.pallas_call(
        functools.partial(lag_kernel, places, rows, group, len(given), len(before), to_output),
        in_specs=[vmem] * (2 + len(pieces) + len(given)) + [pl.BlockSpec(memory_space=pltpu.HBM)] * len(before),
        out_specs=out_spec,
        out_shape=out_shape,
        scratch_shapes=scratch,
        input_output_aliases={2 + len(pieces) + len(given): 0} if before else {},
        compiler_params=pltpu.CompilerParams(vmem_limit_bytes=VMEM_BYTES),
        cost_estimate=NO_COST,
        name="lag_group",
    )(lag_table, back_table, *pieces, *given, *before)


def shards(spectra, seg_mask):
    tile_count, freq_count = lax.axis_size("tile"), lax.axis_size("freq")
    half_axis = tile_count // 2
    _, seg, band, block = spectra.shape
    half = band // 2
    n_sub = half // SUB
    groups = block // freq_count // SUB
    me = lax.axis_index("freq")
    side = lax.axis_index("tile") // half_axis
    keep_from, send_from = side * half, (1 - side) * half

    across = [(t, (t + half_axis) % tile_count) for t in range(tile_count)]

    def moved(block, d, distance):
        route = []
        for h in range(freq_count):
            for t in range(tile_count):
                route.append((h * tile_count + t, (h + d) % freq_count * tile_count + (t + distance) % tile_count))
        return lax.ppermute(block, ("freq", "tile"), route)

    keep_sub, send_sub = side * n_sub, (1 - side) * n_sub
    *pieces, power = prepare(spectra, seg_mask, send_sub, 1, (SHORT, SUB - SHORT))
    send_power = [power]
    far = [lax.ppermute(piece, "tile", across) for piece in pieces]
    rest, far[0] = lax.optimization_barrier((spectra, far[0]))
    pieces = []
    for i in range(1, n_sub):
        *both, power = prepare(rest, seg_mask, send_sub + i, 1, (SUB // 2, SUB // 2))
        rest, both = lax.optimization_barrier((rest, both))
        pieces += both
        send_power.append(power)
    own, own_power = prepare(rest, seg_mask, keep_sub, n_sub, (half,))
    send_power = jnp.concatenate(send_power, axis=0)

    total = lax.psum(jnp.sum(own_power, axis=0) + jnp.sum(send_power, axis=0), "freq")
    lift = WATER * (total / F)[None, :]
    own_inv = (1.0 / ((own_power + lift) * seg)).T
    local = jnp.arange(half, dtype=jnp.int32)
    lag_cols = []
    for mine in (True, False):
        for d in range(freq_count):
            freqs = (me - d) % freq_count * band + (keep_from if mine else send_from) + local
            cos_tab, sin_tab = dft_tables(freqs)
            lag_cols.append(jnp.concatenate([cos_tab, sin_tab], axis=0))
            lag_cols.append(jnp.concatenate([-sin_tab, cos_tab], axis=0))
    lag_table = jnp.concatenate(lag_cols, axis=1)
    cos_tab, sin_tab = dft_tables(jnp.arange(F, dtype=jnp.int32))
    back_table = jnp.concatenate([cos_tab, -sin_tab], axis=1).T

    far_total = None
    for i, piece in enumerate(pieces):
        if i == 2:
            shape = piece.shape
            piece, terms, own_inv, lag_table, back_table = lax.optimization_barrier(
                (piece, exact_terms(total), own_inv, lag_table, back_table)
            )
            piece = jnp.concatenate([piece.reshape(-1, block), terms], axis=0)
        if i >= 2:
            piece, far[-DEPTH] = lax.optimization_barrier((piece, far[-DEPTH]))
        got = lax.ppermute(piece, "tile", across)
        if i == 2:
            far_total = jnp.sum(got[-SUB:].astype(jnp.float32), axis=0)
            got = got[:-SUB].reshape(shape)
        far.append(got)
    if far_total is None:
        far_total = lax.ppermute(total, "tile", across)
    far_lift = WATER * (far_total / F)[None, :]

    n_split = groups // 2 if n_sub > 1 else 0
    full = groups * SUB
    early_rows = n_split * SUB
    first_parts = [(j * SUB, SUB, "early") for j in range(n_split)]
    late_parts = [(0, early_rows, "late")] if n_split else []
    own_rest = [(early_rows, full - early_rows, "all")]
    halves = [(row, SUB // 2, "all") for row in range(early_rows, full, SUB // 2)] if groups > 1 else own_rest
    places = [first_parts + late_parts + (own_rest if k < freq_count else halves) for k in range(2 * freq_count)]
    slots = [(k, *place) for k in range(2 * freq_count) for place in places[k]]
    me_arr = me.astype(jnp.int32).reshape(1)
    ready = max(2 * n_sub - 3, 0)
    far[ready], lag_table, back_table, own_inv, far_lift, own = lax.optimization_barrier(
        (far[ready], lag_table, back_table, own_inv, far_lift, own)
    )
    made = {}
    for i in range(n_sub):
        made = cross_piece(i, freq_count, groups, slots, me_arr, own, far[2 * i : 2 * i + 2], own_inv, far_lift, made)

    arrived = {}

    def send(place, wait_for=None):
        kinds = [k for k in range(1, 2 * freq_count) if place in places[k]]
        outgoing = [made[(k, *place)] for k in kinds]
        if wait_for is not None:
            outgoing, arrived[wait_for] = lax.optimization_barrier((outgoing, arrived[wait_for]))
        moves = [moved(x, k % freq_count, half_axis * (k // freq_count)) for k, x in zip(kinds, outgoing)]
        arrived[place] = dict(zip(kinds, moves))

    for place in first_parts + late_parts:
        send(place)
    if own_rest != halves:
        send(own_rest[0])
    chain = first_parts + halves
    for n, place in enumerate(halves, start=len(first_parts)):
        send(place, chain[n - 2] if n >= 2 else None)

    out, given = [], []
    for place in first_parts + halves:
        first_row, rows, _ = place
        if place in halves[-2:-1]:
            arrived[place], out = lax.optimization_barrier((arrived[place], out))
        sources = []
        for k in range(2 * freq_count):
            holds = [hold for hold in places[k] if hold[0] <= first_row < hold[0] + hold[1]]
            sources.append([(arrived[hold][k] if k else made[(0, *hold)], first_row - hold[0]) for hold in holds])
        group, ends = first_row // SUB, (first_row + rows) % SUB == 0
        done = lag_group(rows, group, groups, lag_table, back_table, sources, given, out if ends else [], to_output=ends)
        if ends:
            given, out = [], [done]
        else:
            given = [done]
    return out[0]


def solution(mesh):
    placed = (P(None, None, "freq", "tile"), P(None, "tile"))
    return jax.shard_map(
        shards,
        mesh=mesh,
        in_specs=placed,
        out_specs=P("tile", None, None, "freq", None),
        check_vma=False,
    )
```

```python
import functools
import math

import jax
import jax.numpy as jnp
from jax import lax
from jax.experimental import pallas as pl
from jax.experimental.pallas import tpu as pltpu
from jax.sharding import PartitionSpec as P

F = 256
LAGS = 512
WATER = 0.05
SUB = 16
SHORT = 4
AT_ONCE = 4
PARTS = 4
SLICE = 32
VMEM_BYTES = 48 * 2**20
NO_COST = pl.CostEstimate(flops=0, bytes_accessed=0, transcendentals=0)


def dft_tables(freq_index):
    lag_index = jnp.arange(LAGS, dtype=jnp.int32)[:, None]
    phase = (lag_index * freq_index[None, :] % LAGS).astype(jnp.float32) * (2.0 * math.pi / LAGS)
    return jnp.cos(phase).astype(jnp.bfloat16), jnp.sin(phase).astype(jnp.bfloat16)


def rounded(x):
    return x.astype(jnp.bfloat16).astype(jnp.float32)


def interleave():
    row = lax.broadcasted_iota(jnp.int32, (SUB * SUB, SUB * SUB), 0)
    col = lax.broadcasted_iota(jnp.int32, (SUB * SUB, SUB * SUB), 1)
    return jnp.where(col == row % SUB * SUB + row // SUB, 1.0, 0.0).astype(jnp.bfloat16)


def turned_rows(matrix, left, right):
    lanes = left.shape[2]
    both = jnp.concatenate([left.reshape(SUB * SUB, lanes), right.reshape(SUB * SUB, lanes)], axis=1)
    return jnp.dot(matrix, both, preferred_element_type=jnp.float32).reshape(SUB, SUB, 2 * lanes)


def prepare_kernel(at_ref, x_ref, mask_ref, *outs):
    parts, power_ref = outs[:-1], outs[-1]
    seg, lanes = mask_ref.shape
    matrix = interleave()
    total = jnp.zeros((SUB, 8, lanes), jnp.float32)
    for s in range(0, seg, SUB):
        mask = mask_ref[s : s + SUB].astype(jnp.float32)[None]
        turned = turned_rows(matrix, x_ref[0, s : s + SUB], x_ref[1, s : s + SUB])
        for part in range(2):
            val = turned[:, :, part * lanes : (part + 1) * lanes] * mask
            square = val * val
            total += square[:, :8] + square[:, 8:]
            at = 0
            for out in parts:
                count = out.shape[0]
                out[:, part, s : s + SUB] = val[at : at + count].astype(jnp.bfloat16)
                at += count
    power_ref[...] = jnp.sum(total, axis=1) * (1.0 / seg) + 1e-05


def prepare(spectra, seg_mask, first, steps, counts):
    _, seg, _, block = spectra.shape
    assert sum(counts) == steps * SUB and (steps == 1 or len(counts) == 1)
    out_specs = [pl.BlockSpec((min(count, SUB), 2, seg, block), lambda i, at: (i, 0, 0, 0)) for count in counts]
    out_shape = [jax.ShapeDtypeStruct((count, 2, seg, block), jnp.bfloat16) for count in counts]
    return pl.pallas_call(
        prepare_kernel,
        grid_spec=pltpu.PrefetchScalarGridSpec(
            num_scalar_prefetch=1,
            grid=(steps,),
            in_specs=[
                pl.BlockSpec((2, seg, SUB, block), lambda i, at: (0, 0, at[0] + i, 0)),
                pl.BlockSpec((seg, block), lambda i, at: (0, 0)),
            ],
            out_specs=out_specs + [pl.BlockSpec((SUB, block), lambda i, at: (i, 0))],
        ),
        out_shape=out_shape + [jax.ShapeDtypeStruct((steps * SUB, block), jnp.float32)],
        compiler_params=pltpu.CompilerParams(vmem_limit_bytes=VMEM_BYTES),
        cost_estimate=NO_COST,
        name="prepare",
    )(first.astype(jnp.int32).reshape(1), spectra, seg_mask)


def exact_terms(x):
    terms, rest = [], x
    for _ in range(3):
        terms.append(lax.reduce_precision(rest, 8, 7))
        rest = rest - terms[-1]
    return jnp.pad(jnp.stack(terms).astype(jnp.bfloat16), ((0, SUB - 3), (0, 0)))


def cross_kernel(piece, freq_count, groups, slots, held, n_far, me_ref, own_ref, own_inv_ref, far_lift_ref, *refs):
    far_refs, outs, (own_scr, far_scr) = refs[:n_far], refs[n_far + held : -2], refs[-2:]
    seg = own_ref.shape[2]
    block = own_ref.shape[3]
    far_rows = [(far_ref, k) for far_ref in far_refs for k in range(far_ref.shape[0])]
    for f in range(SUB):
        own = own_ref[f].reshape(2 * seg, block)
        far_ref, k = far_rows[f]
        far_re, far_im = far_ref[k, 0], far_ref[k, 1]
        cols = jnp.concatenate(
            [jnp.concatenate([far_re, far_im], axis=0), jnp.concatenate([far_im, -far_re], axis=0)], axis=1
        )
        cross = lax.dot_general(own, cols, (((0,), (0,)), ((), ())), preferred_element_type=jnp.float32)
        at = piece * SUB + f
        own_inv = own_inv_ref[:, at : at + 1]
        square = jnp.square(far_re.astype(jnp.float32)) + jnp.square(far_im.astype(jnp.float32))
        far_power = jnp.sum(square, axis=0, keepdims=True) * (1.0 / seg) + 1e-05
        far_inv = 1.0 / ((far_power + far_lift_ref[...]) * seg)
        for part in range(2):
            val = cross[:, part * block : (part + 1) * block]
            sym = 0.5 * (rounded(val * own_inv) + rounded(val * far_inv))
            own_scr[part, f] = sym.astype(jnp.bfloat16)
            turned = jnp.transpose(sym if part == 0 else -sym)
            far_scr[part, f] = turned.astype(jnp.bfloat16)
    me = me_ref[0]
    matrix = interleave()
    for k in range(2 * freq_count):
        scr = own_scr if k < freq_count else far_scr
        for j in range(groups):
            first = (lax.rem(me + k % freq_count, freq_count) * groups + j) * SUB
            rows = pl.ds(pl.multiple_of(first, SUB), SUB)
            turned = turned_rows(matrix, scr[0, :, rows, :], scr[1, :, rows, :])
            for out, (kind, first_row, count, _) in zip(outs, slots):
                low, high = max(first_row, j * SUB), min(first_row + count, (j + 1) * SUB)
                if kind != k or low >= high:
                    continue
                for part in range(2):
                    vals = turned[low - j * SUB : high - j * SUB, :, part * block : (part + 1) * block]
                    out[low - first_row : high - first_row, part] = vals.astype(jnp.bfloat16)


def cross_piece(piece, freq_count, groups, slots, me, own, far, own_inv, far_lift, made):
    half, _, seg, block = own.shape
    n_far = len(far)
    last = (piece + 1) * SUB == half
    slots = [slot for slot in slots if slot[3] == "all" or (slot[3] == "late") == last]
    counts = {"all": half, "early": half - SUB, "late": SUB}
    places = [0 if slot[3] == "late" else piece for slot in slots]
    spots = [n for n, slot in enumerate(slots) if slot in made]
    flat = pl.pallas_call(
        functools.partial(cross_kernel, piece, freq_count, groups, slots, len(spots), n_far),
        grid=(1,),
        in_specs=[
            pl.BlockSpec(memory_space=pltpu.SMEM),
            pl.BlockSpec((SUB, 2, seg, block), lambda i: (piece, 0, 0, 0)),
            pl.BlockSpec((block, half), lambda i: (0, 0)),
            pl.BlockSpec((1, block), lambda i: (0, 0)),
        ]
        + [pl.BlockSpec(x.shape, lambda i: (0, 0, 0, 0)) for x in far]
        + [pl.BlockSpec(memory_space=pl.ANY)] * len(spots),
        out_specs=[
            pl.BlockSpec((slot[2], 2, SUB, block), functools.partial(lambda at, i: (0, 0, at, 0), at))
            for slot, at in zip(slots, places)
        ],
        out_shape=[jax.ShapeDtypeStruct((slot[2], 2, counts[slot[3]], block), jnp.bfloat16) for slot in slots],
        scratch_shapes=[pltpu.VMEM((2, SUB, block, block), jnp.bfloat16)] * 2,
        input_output_aliases={4 + n_far + i: n for i, n in enumerate(spots)},
        compiler_params=pltpu.CompilerParams(vmem_limit_bytes=VMEM_BYTES),
        cost_estimate=pl.CostEstimate(
            flops=SUB * 8 * seg * block * block, bytes_accessed=SUB * 16 * seg * block, transcendentals=0
        ),
        name="cross_piece",
    )(me, own, own_inv, far_lift, *far, *[made[slots[n]] for n in spots])
    return {**made, **dict(zip(slots, flat))}


def lag_kernel(sources, rows, group, n_given, n_held, to_output, lag_ref, back_ref, *refs):
    n_pieces = sum(len(places) for places in sources)
    pieces, given = refs[:n_pieces], refs[n_pieces : n_pieces + n_given]
    out_ref, lag_scr, norm_scr, *rest = refs[n_pieces + n_given + n_held :]
    block = pieces[0].shape[3]
    width = AT_ONCE * block
    row_ref = rest[0] if to_output else out_ref
    first = SUB - rows if to_output else 0

    def column(r):
        parts, at = [], 0
        for places in sources:
            for part in range(2):
                parts += [piece[place + r, part] for piece, place in zip(pieces[at:], places)]
            at += len(places)
        return jnp.concatenate(parts, axis=0)

    for r in range(0, rows, AT_ONCE):
        cols = jnp.concatenate([column(r + k) for k in range(AT_ONCE)], axis=1)
        lag_scr[...] = jnp.dot(lag_ref[...], cols, preferred_element_type=jnp.float32)
        total = jnp.zeros((8, width), jnp.float32)
        for at in range(0, LAGS, SLICE):
            lag_re, lag_im = lag_scr[at : at + SLICE], lag_scr[LAGS + at : LAGS + at + SLICE]
            energy = lag_re * lag_re + lag_im * lag_im
            lag_scr[LAGS + at : LAGS + at + SLICE] = energy
            total += jnp.sum(energy.reshape(SLICE // 8, 8, width), axis=0)
        floor = (0.25 / LAGS) * jnp.sum(total, axis=0, keepdims=True) + 1e-05
        for at in range(0, LAGS, SLICE):
            scale = lax.rsqrt(lag_scr[LAGS + at : LAGS + at + SLICE] + floor)
            norm_scr[at : at + SLICE] = (lag_scr[at : at + SLICE] * scale).astype(jnp.bfloat16)
        lag_scr[: 2 * F] = jnp.dot(back_ref[...], norm_scr[...], preferred_element_type=jnp.float32)
        for at in range(0, 2 * F, SLICE):
            back = (lag_scr[at : at + SLICE] * (1.0 / math.sqrt(LAGS))).astype(jnp.bfloat16)
            for k in range(AT_ONCE):
                row_ref[first + r + k, at : at + SLICE] = back[:, k * block : (k + 1) * block]
    if to_output:
        _, bins_ref, sems = rest
        matrix = interleave()
        copies = []
        chunk = 2 * F // PARTS
        for at in range(0, 2 * F, 2 * SUB):
            whole = [x[:, at : at + 2 * SUB] for x in given] + [row_ref[first:, at : at + 2 * SUB]]
            whole = jnp.concatenate(whole, axis=0)
            turned = turned_rows(matrix, whole[:, :SUB], whole[:, SUB:])
            for n in range(2):
                bins = turned[:, :, n * block : (n + 1) * block]
                bins_ref[at + n * SUB : at + (n + 1) * SUB] = bins.astype(jnp.bfloat16)
            if (at + 2 * SUB) % chunk == 0:
                start = at + 2 * SUB - chunk
                there = out_ref.at[0, start // F, pl.ds(start % F, chunk), pl.ds(group * SUB, SUB)]
                copies.append(pltpu.make_async_copy(bins_ref.at[pl.ds(start, chunk)], there, sems.at[start // chunk]))
                copies[-1].start()
        for copy in copies:
            copy.wait()


def lag_group(rows, group, groups, lag_table, back_table, sources, given, before, to_output=True):
    pieces = [piece for source in sources for piece, _ in source]
    places = [[place for _, place in source] for source in sources]
    block = pieces[0].shape[3]
    vmem, scratch = pl.BlockSpec(memory_space=pltpu.VMEM), [
        pltpu.VMEM((2 * LAGS, AT_ONCE * block), jnp.float32),
        pltpu.VMEM((LAGS, AT_ONCE * block), jnp.bfloat16),
    ]
    if to_output:
        out_spec = pl.BlockSpec(memory_space=pltpu.HBM)
        out_shape = jax.ShapeDtypeStruct((1, 2, F, SUB * groups, block), jnp.bfloat16)
        scratch += [
            pltpu.VMEM((SUB, 2 * F, block), jnp.bfloat16),
            pltpu.VMEM((2 * F, SUB, block), jnp.bfloat16),
            pltpu.SemaphoreType.DMA((PARTS,)),
        ]
    else:
        out_spec = vmem
        out_shape = jax.ShapeDtypeStruct((rows, 2 * F, block), jnp.bfloat16)
    return pl.pallas_call(
        functools.partial(lag_kernel, places, rows, group, len(given), len(before), to_output),
        in_specs=[vmem] * (2 + len(pieces) + len(given)) + [pl.BlockSpec(memory_space=pltpu.HBM)] * len(before),
        out_specs=out_spec,
        out_shape=out_shape,
        scratch_shapes=scratch,
        input_output_aliases={2 + len(pieces) + len(given): 0} if before else {},
        compiler_params=pltpu.CompilerParams(vmem_limit_bytes=VMEM_BYTES),
        cost_estimate=NO_COST,
        name="lag_group",
    )(lag_table, back_table, *pieces, *given, *before)


def shards(spectra, seg_mask):
    tile_count, freq_count = lax.axis_size("tile"), lax.axis_size("freq")
    half_axis = tile_count // 2
    _, seg, band, block = spectra.shape
    half = band // 2
    n_sub = half // SUB
    groups = block // freq_count // SUB
    me = lax.axis_index("freq")
    side = lax.axis_index("tile") // half_axis
    keep_from, send_from = side * half, (1 - side) * half

    across = [(t, (t + half_axis) % tile_count) for t in range(tile_count)]

    def moved(block, d, distance):
        route = []
        for h in range(freq_count):
            for t in range(tile_count):
                route.append((h * tile_count + t, (h + d) % freq_count * tile_count + (t + distance) % tile_count))
        return lax.ppermute(block, ("freq", "tile"), route)

    keep_sub, send_sub = side * n_sub, (1 - side) * n_sub
    *pieces, power = prepare(spectra, seg_mask, send_sub, 1, (SHORT, SUB - SHORT))
    send_power, counts = [power], [2]
    if n_sub > 1:
        piece, power = prepare(spectra, seg_mask, send_sub + 1, 1, (SUB,))
        pieces.append(piece)
        send_power.append(power)
        counts.append(1)
    far = [lax.ppermute(piece, "tile", across) for piece in pieces]
    rest, far[0] = lax.optimization_barrier((spectra, far[0]))
    pieces = []
    for i in range(2, n_sub):
        *both, power = prepare(rest, seg_mask, send_sub + i, 1, (SUB // 2, SUB // 2))
        rest, both = lax.optimization_barrier((rest, both))
        pieces += both
        send_power.append(power)
        counts.append(2)
    own, own_power = prepare(rest, seg_mask, keep_sub, n_sub, (half,))
    send_power = jnp.concatenate(send_power, axis=0)

    total = lax.psum(jnp.sum(own_power, axis=0) + jnp.sum(send_power, axis=0), "freq")
    lift = WATER * (total / F)[None, :]
    own_inv = (1.0 / ((own_power + lift) * seg)).T
    local = jnp.arange(half, dtype=jnp.int32)
    lag_cols = []
    for mine in (True, False):
        for d in range(freq_count):
            freqs = (me - d) % freq_count * band + (keep_from if mine else send_from) + local
            cos_tab, sin_tab = dft_tables(freqs)
            lag_cols.append(jnp.concatenate([cos_tab, sin_tab], axis=0))
            lag_cols.append(jnp.concatenate([-sin_tab, cos_tab], axis=0))
    lag_table = jnp.concatenate(lag_cols, axis=1)
    cos_tab, sin_tab = dft_tables(jnp.arange(F, dtype=jnp.int32))
    back_table = jnp.concatenate([cos_tab, -sin_tab], axis=1).T

    far_total = None
    for i, piece in enumerate(pieces):
        if i == 0:
            shape = piece.shape
            piece, terms, own_inv, lag_table, back_table = lax.optimization_barrier(
                (piece, exact_terms(total), own_inv, lag_table, back_table)
            )
            piece = jnp.concatenate([piece.reshape(-1, block), terms], axis=0)
        if i >= 2:
            piece, far[i - 1] = lax.optimization_barrier((piece, far[i - 1]))
        got = lax.ppermute(piece, "tile", across)
        if i == 0:
            far_total = jnp.sum(got[-SUB:].astype(jnp.float32), axis=0)
            got = got[:-SUB].reshape(shape)
        far.append(got)
    if far_total is None:
        far_total = lax.ppermute(total, "tile", across)
    far_lift = WATER * (far_total / F)[None, :]

    n_split = groups // 2 if n_sub > 1 else 0
    full = groups * SUB
    early_rows = n_split * SUB
    first_parts = [(j * SUB, SUB, "early") for j in range(n_split)]
    late_parts = [(0, early_rows, "late")] if n_split else []
    own_rest = [(early_rows, full - early_rows, "all")]
    halves = [(row, SUB // 2, "all") for row in range(early_rows, full, SUB // 2)] if groups > 1 else own_rest
    places = [first_parts + late_parts + (own_rest if k < freq_count else halves) for k in range(2 * freq_count)]
    slots = [(k, *place) for k in range(2 * freq_count) for place in places[k]]
    me_arr = me.astype(jnp.int32).reshape(1)
    ready = max(sum(counts[:-1]) - 1, 0)
    far[ready], lag_table, back_table, own_inv, far_lift, own = lax.optimization_barrier(
        (far[ready], lag_table, back_table, own_inv, far_lift, own)
    )
    far = [far[sum(counts[:i]) : sum(counts[: i + 1])] for i in range(n_sub)]
    made = {}
    for i in range(n_sub):
        made = cross_piece(i, freq_count, groups, slots, me_arr, own, far[i], own_inv, far_lift, made)

    arrived = {}

    def send(place, wait_for=None):
        kinds = [k for k in range(1, 2 * freq_count) if place in places[k]]
        outgoing = [made[(k, *place)] for k in kinds]
        if wait_for is not None:
            outgoing, arrived[wait_for] = lax.optimization_barrier((outgoing, arrived[wait_for]))
        moves = [moved(x, k % freq_count, half_axis * (k // freq_count)) for k, x in zip(kinds, outgoing)]
        arrived[place] = dict(zip(kinds, moves))

    for place in first_parts + late_parts:
        send(place)
    if own_rest != halves:
        send(own_rest[0])
    chain = first_parts + halves
    for n, place in enumerate(halves, start=len(first_parts)):
        send(place, chain[n - 2] if n >= 2 else None)

    out, given = [], []
    for place in first_parts + halves:
        first_row, rows, _ = place
        if place in halves[-2:-1]:
            arrived[place], out = lax.optimization_barrier((arrived[place], out))
        sources = []
        for k in range(2 * freq_count):
            holds = [hold for hold in places[k] if hold[0] <= first_row < hold[0] + hold[1]]
            sources.append([(arrived[hold][k] if k else made[(0, *hold)], first_row - hold[0]) for hold in holds])
        group, ends = first_row // SUB, (first_row + rows) % SUB == 0
        done = lag_group(rows, group, groups, lag_table, back_table, sources, given, out if ends else [], to_output=ends)
        if ends:
            given, out = [], [done]
        else:
            given = [done]
    return out[0]


def solution(mesh):
    placed = (P(None, None, "freq", "tile"), P(None, "tile"))
    return jax.shard_map(
        shards,
        mesh=mesh,
        in_specs=placed,
        out_specs=P("tile", None, None, "freq", None),
        check_vma=False,
    )
```

```python
import functools
import math

import jax
import jax.numpy as jnp
from jax import lax
from jax.experimental import pallas as pl
from jax.experimental.pallas import tpu as pltpu
from jax.sharding import PartitionSpec as P

F = 256
LAGS = 512
WATER = 0.05
SUB = 16
SHORT = 4
AT_ONCE = 4
PARTS = 4
SLICE = 32
VMEM_BYTES = 48 * 2**20
NO_COST = pl.CostEstimate(flops=0, bytes_accessed=0, transcendentals=0)


def dft_tables(freq_index):
    lag_index = jnp.arange(LAGS, dtype=jnp.int32)[:, None]
    phase = (lag_index * freq_index[None, :] % LAGS).astype(jnp.float32) * (2.0 * math.pi / LAGS)
    return jnp.cos(phase).astype(jnp.bfloat16), jnp.sin(phase).astype(jnp.bfloat16)


def rounded(x):
    return x.astype(jnp.bfloat16).astype(jnp.float32)


def interleave():
    row = lax.broadcasted_iota(jnp.int32, (SUB * SUB, SUB * SUB), 0)
    col = lax.broadcasted_iota(jnp.int32, (SUB * SUB, SUB * SUB), 1)
    return jnp.where(col == row % SUB * SUB + row // SUB, 1.0, 0.0).astype(jnp.bfloat16)


def turned_rows(matrix, left, right):
    lanes = left.shape[2]
    both = jnp.concatenate([left.reshape(SUB * SUB, lanes), right.reshape(SUB * SUB, lanes)], axis=1)
    return jnp.dot(matrix, both, preferred_element_type=jnp.float32).reshape(SUB, SUB, 2 * lanes)


def prepare_kernel(at_ref, x_ref, mask_ref, *outs):
    parts, power_ref = outs[:-1], outs[-1]
    seg, lanes = mask_ref.shape
    matrix = interleave()
    total = jnp.zeros((SUB, 8, lanes), jnp.float32)
    for s in range(0, seg, SUB):
        mask = mask_ref[s : s + SUB].astype(jnp.float32)[None]
        turned = turned_rows(matrix, x_ref[0, s : s + SUB], x_ref[1, s : s + SUB])
        for part in range(2):
            val = turned[:, :, part * lanes : (part + 1) * lanes] * mask
            square = val * val
            total += square[:, :8] + square[:, 8:]
            at = 0
            for out in parts:
                count = out.shape[0]
                out[:, part, s : s + SUB] = val[at : at + count].astype(jnp.bfloat16)
                at += count
    power_ref[...] = jnp.sum(total, axis=1) * (1.0 / seg) + 1e-05


def prepare(spectra, seg_mask, first, steps, counts):
    _, seg, _, block = spectra.shape
    assert sum(counts) == steps * SUB and (steps == 1 or len(counts) == 1)
    out_specs = [pl.BlockSpec((min(count, SUB), 2, seg, block), lambda i, at: (i, 0, 0, 0)) for count in counts]
    out_shape = [jax.ShapeDtypeStruct((count, 2, seg, block), jnp.bfloat16) for count in counts]
    return pl.pallas_call(
        prepare_kernel,
        grid_spec=pltpu.PrefetchScalarGridSpec(
            num_scalar_prefetch=1,
            grid=(steps,),
            in_specs=[
                pl.BlockSpec((2, seg, SUB, block), lambda i, at: (0, 0, at[0] + i, 0)),
                pl.BlockSpec((seg, block), lambda i, at: (0, 0)),
            ],
            out_specs=out_specs + [pl.BlockSpec((SUB, block), lambda i, at: (i, 0))],
        ),
        out_shape=out_shape + [jax.ShapeDtypeStruct((steps * SUB, block), jnp.float32)],
        compiler_params=pltpu.CompilerParams(vmem_limit_bytes=VMEM_BYTES),
        cost_estimate=NO_COST,
        name="prepare",
    )(first.astype(jnp.int32).reshape(1), spectra, seg_mask)


def exact_terms(x):
    terms, rest = [], x
    for _ in range(3):
        terms.append(lax.reduce_precision(rest, 8, 7))
        rest = rest - terms[-1]
    return jnp.pad(jnp.stack(terms).astype(jnp.bfloat16), ((0, SUB - 3), (0, 0)))


def cross_kernel(piece, freq_count, groups, slots, held, n_far, me_ref, own_ref, own_inv_ref, far_lift_ref, *refs):
    far_refs, outs, (own_scr, far_scr) = refs[:n_far], refs[n_far + held : -2], refs[-2:]
    seg = own_ref.shape[2]
    block = own_ref.shape[3]
    far_rows = [(far_ref, k) for far_ref in far_refs for k in range(far_ref.shape[0])]
    for f in range(SUB):
        own = own_ref[f].reshape(2 * seg, block)
        far_ref, k = far_rows[f]
        far_re, far_im = far_ref[k, 0], far_ref[k, 1]
        cols = jnp.concatenate(
            [jnp.concatenate([far_re, far_im], axis=0), jnp.concatenate([far_im, -far_re], axis=0)], axis=1
        )
        cross = lax.dot_general(own, cols, (((0,), (0,)), ((), ())), preferred_element_type=jnp.float32)
        at = piece * SUB + f
        own_inv = own_inv_ref[:, at : at + 1]
        square = jnp.square(far_re.astype(jnp.float32)) + jnp.square(far_im.astype(jnp.float32))
        far_power = jnp.sum(square, axis=0, keepdims=True) * (1.0 / seg) + 1e-05
        far_inv = 1.0 / ((far_power + far_lift_ref[...]) * seg)
        for part in range(2):
            val = cross[:, part * block : (part + 1) * block]
            sym = 0.5 * (rounded(val * own_inv) + rounded(val * far_inv))
            own_scr[part, f] = sym.astype(jnp.bfloat16)
            turned = jnp.transpose(sym if part == 0 else -sym)
            far_scr[part, f] = turned.astype(jnp.bfloat16)
    me = me_ref[0]
    matrix = interleave()
    for k in range(2 * freq_count):
        scr = own_scr if k < freq_count else far_scr
        for j in range(groups):
            first = (lax.rem(me + k % freq_count, freq_count) * groups + j) * SUB
            rows = pl.ds(pl.multiple_of(first, SUB), SUB)
            turned = turned_rows(matrix, scr[0, :, rows, :], scr[1, :, rows, :])
            for out, (kind, first_row, count, _) in zip(outs, slots):
                low, high = max(first_row, j * SUB), min(first_row + count, (j + 1) * SUB)
                if kind != k or low >= high:
                    continue
                for part in range(2):
                    vals = turned[low - j * SUB : high - j * SUB, :, part * block : (part + 1) * block]
                    out[low - first_row : high - first_row, part] = vals.astype(jnp.bfloat16)


def cross_piece(piece, freq_count, groups, slots, me, own, far, own_inv, far_lift, made):
    half, _, seg, block = own.shape
    n_far = len(far)
    last = (piece + 1) * SUB == half
    slots = [slot for slot in slots if slot[3] == "all" or (slot[3] == "late") == last]
    counts = {"all": half, "early": half - SUB, "late": SUB}
    places = [0 if slot[3] == "late" else piece for slot in slots]
    spots = [n for n, slot in enumerate(slots) if slot in made]
    flat = pl.pallas_call(
        functools.partial(cross_kernel, piece, freq_count, groups, slots, len(spots), n_far),
        grid=(1,),
        in_specs=[
            pl.BlockSpec(memory_space=pltpu.SMEM),
            pl.BlockSpec((SUB, 2, seg, block), lambda i: (piece, 0, 0, 0)),
            pl.BlockSpec((block, half), lambda i: (0, 0)),
            pl.BlockSpec((1, block), lambda i: (0, 0)),
        ]
        + [pl.BlockSpec(x.shape, lambda i: (0, 0, 0, 0)) for x in far]
        + [pl.BlockSpec(memory_space=pl.ANY)] * len(spots),
        out_specs=[
            pl.BlockSpec((slot[2], 2, SUB, block), functools.partial(lambda at, i: (0, 0, at, 0), at))
            for slot, at in zip(slots, places)
        ],
        out_shape=[jax.ShapeDtypeStruct((slot[2], 2, counts[slot[3]], block), jnp.bfloat16) for slot in slots],
        scratch_shapes=[pltpu.VMEM((2, SUB, block, block), jnp.bfloat16)] * 2,
        input_output_aliases={4 + n_far + i: n for i, n in enumerate(spots)},
        compiler_params=pltpu.CompilerParams(vmem_limit_bytes=VMEM_BYTES),
        cost_estimate=pl.CostEstimate(
            flops=SUB * 8 * seg * block * block, bytes_accessed=SUB * 16 * seg * block, transcendentals=0
        ),
        name="cross_piece",
    )(me, own, own_inv, far_lift, *far, *[made[slots[n]] for n in spots])
    return {**made, **dict(zip(slots, flat))}


def lag_kernel(sources, rows, group, n_given, n_held, to_output, lag_ref, back_ref, *refs):
    n_pieces = sum(len(places) for places in sources)
    pieces, given = refs[:n_pieces], refs[n_pieces : n_pieces + n_given]
    out_ref, lag_scr, norm_scr, *rest = refs[n_pieces + n_given + n_held :]
    block = pieces[0].shape[3]
    width = AT_ONCE * block
    row_ref = rest[0] if to_output else out_ref
    first = SUB - rows if to_output else 0

    def column(r):
        parts, at = [], 0
        for places in sources:
            for part in range(2):
                parts += [piece[place + r, part] for piece, place in zip(pieces[at:], places)]
            at += len(places)
        return jnp.concatenate(parts, axis=0)

    for r in range(0, rows, AT_ONCE):
        cols = jnp.concatenate([column(r + k) for k in range(AT_ONCE)], axis=1)
        lag_scr[...] = jnp.dot(lag_ref[...], cols, preferred_element_type=jnp.float32)
        total = jnp.zeros((8, width), jnp.float32)
        for at in range(0, LAGS, SLICE):
            lag_re, lag_im = lag_scr[at : at + SLICE], lag_scr[LAGS + at : LAGS + at + SLICE]
            energy = lag_re * lag_re + lag_im * lag_im
            lag_scr[LAGS + at : LAGS + at + SLICE] = energy
            total += jnp.sum(energy.reshape(SLICE // 8, 8, width), axis=0)
        floor = (0.25 / LAGS) * jnp.sum(total, axis=0, keepdims=True) + 1e-05
        for at in range(0, LAGS, SLICE):
            scale = lax.rsqrt(lag_scr[LAGS + at : LAGS + at + SLICE] + floor)
            norm_scr[at : at + SLICE] = (lag_scr[at : at + SLICE] * scale).astype(jnp.bfloat16)
        lag_scr[: 2 * F] = jnp.dot(back_ref[...], norm_scr[...], preferred_element_type=jnp.float32)
        for at in range(0, 2 * F, SLICE):
            back = (lag_scr[at : at + SLICE] * (1.0 / math.sqrt(LAGS))).astype(jnp.bfloat16)
            for k in range(AT_ONCE):
                row_ref[first + r + k, at : at + SLICE] = back[:, k * block : (k + 1) * block]
    if to_output:
        _, bins_ref, sems = rest
        matrix = interleave()
        copies = []
        chunk = 2 * F // PARTS
        for at in range(0, 2 * F, 2 * SUB):
            whole = [x[:, at : at + 2 * SUB] for x in given] + [row_ref[first:, at : at + 2 * SUB]]
            whole = jnp.concatenate(whole, axis=0)
            turned = turned_rows(matrix, whole[:, :SUB], whole[:, SUB:])
            for n in range(2):
                bins = turned[:, :, n * block : (n + 1) * block]
                bins_ref[at + n * SUB : at + (n + 1) * SUB] = bins.astype(jnp.bfloat16)
            if (at + 2 * SUB) % chunk == 0:
                start = at + 2 * SUB - chunk
                there = out_ref.at[0, start // F, pl.ds(start % F, chunk), pl.ds(group * SUB, SUB)]
                copies.append(pltpu.make_async_copy(bins_ref.at[pl.ds(start, chunk)], there, sems.at[start // chunk]))
                copies[-1].start()
        for copy in copies:
            copy.wait()


def lag_group(rows, group, groups, lag_table, back_table, sources, given, before, to_output=True):
    pieces = [piece for source in sources for piece, _ in source]
    places = [[place for _, place in source] for source in sources]
    block = pieces[0].shape[3]
    vmem, scratch = pl.BlockSpec(memory_space=pltpu.VMEM), [
        pltpu.VMEM((2 * LAGS, AT_ONCE * block), jnp.float32),
        pltpu.VMEM((LAGS, AT_ONCE * block), jnp.bfloat16),
    ]
    if to_output:
        out_spec = pl.BlockSpec(memory_space=pltpu.HBM)
        out_shape = jax.ShapeDtypeStruct((1, 2, F, SUB * groups, block), jnp.bfloat16)
        scratch += [
            pltpu.VMEM((SUB, 2 * F, block), jnp.bfloat16),
            pltpu.VMEM((2 * F, SUB, block), jnp.bfloat16),
            pltpu.SemaphoreType.DMA((PARTS,)),
        ]
    else:
        out_spec = vmem
        out_shape = jax.ShapeDtypeStruct((rows, 2 * F, block), jnp.bfloat16)
    return pl.pallas_call(
        functools.partial(lag_kernel, places, rows, group, len(given), len(before), to_output),
        in_specs=[vmem] * (2 + len(pieces) + len(given)) + [pl.BlockSpec(memory_space=pltpu.HBM)] * len(before),
        out_specs=out_spec,
        out_shape=out_shape,
        scratch_shapes=scratch,
        input_output_aliases={2 + len(pieces) + len(given): 0} if before else {},
        compiler_params=pltpu.CompilerParams(vmem_limit_bytes=VMEM_BYTES),
        cost_estimate=NO_COST,
        name="lag_group",
    )(lag_table, back_table, *pieces, *given, *before)


def shards(spectra, seg_mask):
    tile_count, freq_count = lax.axis_size("tile"), lax.axis_size("freq")
    half_axis = tile_count // 2
    _, seg, band, block = spectra.shape
    half = band // 2
    n_sub = half // SUB
    groups = block // freq_count // SUB
    me = lax.axis_index("freq")
    side = lax.axis_index("tile") // half_axis
    keep_from, send_from = side * half, (1 - side) * half

    across = [(t, (t + half_axis) % tile_count) for t in range(tile_count)]

    def moved(block, d, distance):
        route = []
        for h in range(freq_count):
            for t in range(tile_count):
                route.append((h * tile_count + t, (h + d) % freq_count * tile_count + (t + distance) % tile_count))
        return lax.ppermute(block, ("freq", "tile"), route)

    keep_sub, send_sub = side * n_sub, (1 - side) * n_sub
    *pieces, power = prepare(spectra, seg_mask, send_sub, 1, (SHORT, SUB - SHORT))
    send_power, counts = [power], [2]
    if n_sub > 1:
        piece, power = prepare(spectra, seg_mask, send_sub + 1, 1, (SUB,))
        pieces.append(piece)
        send_power.append(power)
        counts.append(1)
    far = [lax.ppermute(piece, "tile", across) for piece in pieces]
    rest, far[0] = lax.optimization_barrier((spectra, far[0]))
    pieces = []
    for i in range(2, n_sub):
        *both, power = prepare(rest, seg_mask, send_sub + i, 1, (SUB // 2, SUB // 2))
        rest, both = lax.optimization_barrier((rest, both))
        pieces += both
        send_power.append(power)
        counts.append(2)
    own, own_power = prepare(rest, seg_mask, keep_sub, n_sub, (half,))
    send_power = jnp.concatenate(send_power, axis=0)

    total = lax.psum(jnp.sum(own_power, axis=0) + jnp.sum(send_power, axis=0), "freq")
    lift = WATER * (total / F)[None, :]
    own_inv = (1.0 / ((own_power + lift) * seg)).T
    local = jnp.arange(half, dtype=jnp.int32)
    lag_cols = []
    for mine in (True, False):
        for d in range(freq_count):
            freqs = (me - d) % freq_count * band + (keep_from if mine else send_from) + local
            cos_tab, sin_tab = dft_tables(freqs)
            lag_cols.append(jnp.concatenate([cos_tab, sin_tab], axis=0))
            lag_cols.append(jnp.concatenate([-sin_tab, cos_tab], axis=0))
    lag_table = jnp.concatenate(lag_cols, axis=1)
    cos_tab, sin_tab = dft_tables(jnp.arange(F, dtype=jnp.int32))
    back_table = jnp.concatenate([cos_tab, -sin_tab], axis=1).T

    far_total = None
    for i, piece in enumerate(pieces):
        if i == 0:
            shape = piece.shape
            piece, terms, own_inv, lag_table, back_table = lax.optimization_barrier(
                (piece, exact_terms(total), own_inv, lag_table, back_table)
            )
            piece = jnp.concatenate([piece.reshape(-1, block), terms], axis=0)
        if i >= 2:
            piece, far[i - 1] = lax.optimization_barrier((piece, far[i - 1]))
        got = lax.ppermute(piece, "tile", across)
        if i == 0:
            far_total = jnp.sum(got[-SUB:].astype(jnp.float32), axis=0)
            got = got[:-SUB].reshape(shape)
        far.append(got)
    if far_total is None:
        far_total = lax.ppermute(total, "tile", across)
    far_lift = WATER * (far_total / F)[None, :]

    n_split = groups // 2 if n_sub > 1 else 0
    full = groups * SUB
    early_rows = n_split * SUB
    first_parts = [(j * SUB, SUB, "early") for j in range(n_split)]
    late_parts = [(0, early_rows, "late")] if n_split else []
    own_rest = [(early_rows, full - early_rows, "all")]
    halves = [(row, SUB // 2, "all") for row in range(early_rows, full, SUB // 2)] if groups > 1 else own_rest
    places = [first_parts + late_parts + (own_rest if k < freq_count else halves) for k in range(2 * freq_count)]
    slots = [(k, *place) for k in range(2 * freq_count) for place in places[k]]
    me_arr = me.astype(jnp.int32).reshape(1)
    ready = max(sum(counts[:-1]) - 1, 0)
    far[ready], lag_table, back_table, own_inv, far_lift, own = lax.optimization_barrier(
        (far[ready], lag_table, back_table, own_inv, far_lift, own)
    )
    far = [far[sum(counts[:i]) : sum(counts[: i + 1])] for i in range(n_sub)]
    made = {}
    for i in range(n_sub):
        made = cross_piece(i, freq_count, groups, slots, me_arr, own, far[i], own_inv, far_lift, made)

    arrived = {}

    def send(place, wait_for=None):
        kinds = [k for k in range(1, 2 * freq_count) if place in places[k]]
        outgoing = [made[(k, *place)] for k in kinds]
        if wait_for is not None:
            outgoing, arrived[wait_for] = lax.optimization_barrier((outgoing, arrived[wait_for]))
        if wait_for is not None and place == halves[-1]:
            outgoing, state["out"] = lax.optimization_barrier((outgoing, state["out"]))
        moves = [moved(x, k % freq_count, half_axis * (k // freq_count)) for k, x in zip(kinds, outgoing)]
        arrived[place] = dict(zip(kinds, moves))

    def transform(place):
        first_row, rows, _ = place
        sources = []
        for k in range(2 * freq_count):
            holds = [hold for hold in places[k] if hold[0] <= first_row < hold[0] + hold[1]]
            sources.append([(arrived[hold][k] if k else made[(0, *hold)], first_row - hold[0]) for hold in holds])
        group, ends = first_row // SUB, (first_row + rows) % SUB == 0
        before = state["out"] if ends else []
        done = lag_group(rows, group, groups, lag_table, back_table, sources, state["given"], before, to_output=ends)
        state["given" if not ends else "out"] = [done]
        if ends:
            state["given"] = []

    state = {"given": [], "out": []}
    for place in first_parts + late_parts:
        send(place)
    if own_rest != halves:
        send(own_rest[0])
    chain = first_parts + late_parts + halves
    for n, place in enumerate(halves, start=len(chain) - len(halves)):
        if place == halves[-1]:
            for part in first_parts:
                transform(part)
        send(place, chain[n - 2] if n >= 2 else None)
    for place in halves:
        if place in halves[-2:-1]:
            arrived[place], state["out"] = lax.optimization_barrier((arrived[place], state["out"]))
        transform(place)
    out = state["out"]
    return out[0]


def solution(mesh):
    placed = (P(None, None, "freq", "tile"), P(None, "tile"))
    return jax.shard_map(
        shards,
        mesh=mesh,
        in_specs=placed,
        out_specs=P("tile", None, None, "freq", None),
        check_vma=False,
    )
```

```python
import functools
import math

import jax
import jax.numpy as jnp
from jax import lax
from jax.experimental import pallas as pl
from jax.experimental.pallas import tpu as pltpu
from jax.sharding import PartitionSpec as P

F = 256
LAGS = 512
WATER = 0.05
SUB = 16
SHORT = 4
AT_ONCE = 4
PARTS = 4
SLICE = 32
VMEM_BYTES = 28 * 2**20
PREPARE_BYTES = 48 * 2**20
NO_COST = pl.CostEstimate(flops=0, bytes_accessed=0, transcendentals=0)


def dft_tables(freq_index):
    lag_index = jnp.arange(LAGS, dtype=jnp.int32)[:, None]
    phase = (lag_index * freq_index[None, :] % LAGS).astype(jnp.float32) * (2.0 * math.pi / LAGS)
    return jnp.cos(phase).astype(jnp.bfloat16), jnp.sin(phase).astype(jnp.bfloat16)


def rounded(x):
    return x.astype(jnp.bfloat16).astype(jnp.float32)


def interleave():
    row = lax.broadcasted_iota(jnp.int32, (SUB * SUB, SUB * SUB), 0)
    col = lax.broadcasted_iota(jnp.int32, (SUB * SUB, SUB * SUB), 1)
    return jnp.where(col == row % SUB * SUB + row // SUB, 1.0, 0.0).astype(jnp.bfloat16)


def turned_rows(matrix, left, right):
    lanes = left.shape[2]
    both = jnp.concatenate([left.reshape(SUB * SUB, lanes), right.reshape(SUB * SUB, lanes)], axis=1)
    return jnp.dot(matrix, both, preferred_element_type=jnp.float32).reshape(SUB, SUB, 2 * lanes)


def prepare_kernel(at_ref, x_ref, mask_ref, *outs):
    parts, power_ref = outs[:-1], outs[-1]
    seg, lanes = mask_ref.shape
    matrix = interleave()
    total = jnp.zeros((SUB, 8, lanes), jnp.float32)
    for s in range(0, seg, SUB):
        mask = mask_ref[s : s + SUB].astype(jnp.float32)[None]
        turned = turned_rows(matrix, x_ref[0, s : s + SUB], x_ref[1, s : s + SUB])
        for part in range(2):
            val = turned[:, :, part * lanes : (part + 1) * lanes] * mask
            square = val * val
            total += square[:, :8] + square[:, 8:]
            at = 0
            for out in parts:
                count = out.shape[0]
                out[:, part, s : s + SUB] = val[at : at + count].astype(jnp.bfloat16)
                at += count
    power_ref[...] = jnp.sum(total, axis=1) * (1.0 / seg) + 1e-05


def prepare(spectra, seg_mask, first, steps, counts):
    _, seg, _, block = spectra.shape
    assert sum(counts) == steps * SUB and (steps == 1 or len(counts) == 1)
    out_specs = [pl.BlockSpec((min(count, SUB), 2, seg, block), lambda i, at: (i, 0, 0, 0)) for count in counts]
    out_shape = [jax.ShapeDtypeStruct((count, 2, seg, block), jnp.bfloat16) for count in counts]
    return pl.pallas_call(
        prepare_kernel,
        grid_spec=pltpu.PrefetchScalarGridSpec(
            num_scalar_prefetch=1,
            grid=(steps,),
            in_specs=[
                pl.BlockSpec((2, seg, SUB, block), lambda i, at: (0, 0, at[0] + i, 0)),
                pl.BlockSpec((seg, block), lambda i, at: (0, 0)),
            ],
            out_specs=out_specs + [pl.BlockSpec((SUB, block), lambda i, at: (i, 0))],
        ),
        out_shape=out_shape + [jax.ShapeDtypeStruct((steps * SUB, block), jnp.float32)],
        compiler_params=pltpu.CompilerParams(vmem_limit_bytes=PREPARE_BYTES),
        cost_estimate=NO_COST,
        name="prepare",
    )(first.astype(jnp.int32).reshape(1), spectra, seg_mask)


def exact_terms(x):
    terms, rest = [], x
    for _ in range(3):
        terms.append(lax.reduce_precision(rest, 8, 7))
        rest = rest - terms[-1]
    return jnp.pad(jnp.stack(terms).astype(jnp.bfloat16), ((0, SUB - 3), (0, 0)))


def cross_kernel(piece, freq_count, groups, slots, held, n_far, me_ref, own_ref, own_inv_ref, far_lift_ref, *refs):
    far_refs, outs, (own_scr, far_scr) = refs[:n_far], refs[n_far + held : -2], refs[-2:]
    seg = own_ref.shape[2]
    block = own_ref.shape[3]
    far_rows = [(far_ref, k) for far_ref in far_refs for k in range(far_ref.shape[0])]
    for f in range(SUB):
        own = own_ref[f].reshape(2 * seg, block)
        far_ref, k = far_rows[f]
        far_re, far_im = far_ref[k, 0], far_ref[k, 1]
        cols = jnp.concatenate(
            [jnp.concatenate([far_re, far_im], axis=0), jnp.concatenate([far_im, -far_re], axis=0)], axis=1
        )
        cross = lax.dot_general(own, cols, (((0,), (0,)), ((), ())), preferred_element_type=jnp.float32)
        at = piece * SUB + f
        own_inv = own_inv_ref[:, at : at + 1]
        square = jnp.square(far_re.astype(jnp.float32)) + jnp.square(far_im.astype(jnp.float32))
        far_power = jnp.sum(square, axis=0, keepdims=True) * (1.0 / seg) + 1e-05
        far_inv = 1.0 / ((far_power + far_lift_ref[...]) * seg)
        for part in range(2):
            val = cross[:, part * block : (part + 1) * block]
            sym = 0.5 * (rounded(val * own_inv) + rounded(val * far_inv))
            own_scr[part, f] = sym.astype(jnp.bfloat16)
            turned = jnp.transpose(sym if part == 0 else -sym)
            far_scr[part, f] = turned.astype(jnp.bfloat16)
    me = me_ref[0]
    matrix = interleave()
    for k in range(2 * freq_count):
        scr = own_scr if k < freq_count else far_scr
        for j in range(groups):
            first = (lax.rem(me + k % freq_count, freq_count) * groups + j) * SUB
            rows = pl.ds(pl.multiple_of(first, SUB), SUB)
            turned = turned_rows(matrix, scr[0, :, rows, :], scr[1, :, rows, :])
            for out, (kind, first_row, count, _) in zip(outs, slots):
                low, high = max(first_row, j * SUB), min(first_row + count, (j + 1) * SUB)
                if kind != k or low >= high:
                    continue
                for part in range(2):
                    vals = turned[low - j * SUB : high - j * SUB, :, part * block : (part + 1) * block]
                    out[low - first_row : high - first_row, part] = vals.astype(jnp.bfloat16)


def cross_piece(piece, freq_count, groups, slots, me, own, far, own_inv, far_lift, made):
    half, _, seg, block = own.shape
    n_far = len(far)
    last = (piece + 1) * SUB == half
    slots = [slot for slot in slots if slot[3] == "all" or (slot[3] == "late") == last]
    counts = {"all": half, "early": half - SUB, "late": SUB}
    places = [0 if slot[3] == "late" else piece for slot in slots]
    spots = [n for n, slot in enumerate(slots) if slot in made]
    flat = pl.pallas_call(
        functools.partial(cross_kernel, piece, freq_count, groups, slots, len(spots), n_far),
        grid=(1,),
        in_specs=[
            pl.BlockSpec(memory_space=pltpu.SMEM),
            pl.BlockSpec((SUB, 2, seg, block), lambda i: (piece, 0, 0, 0)),
            pl.BlockSpec((block, half), lambda i: (0, 0)),
            pl.BlockSpec((1, block), lambda i: (0, 0)),
        ]
        + [pl.BlockSpec(x.shape, lambda i: (0, 0, 0, 0)) for x in far]
        + [pl.BlockSpec(memory_space=pl.ANY)] * len(spots),
        out_specs=[
            pl.BlockSpec((slot[2], 2, SUB, block), functools.partial(lambda at, i: (0, 0, at, 0), at))
            for slot, at in zip(slots, places)
        ],
        out_shape=[jax.ShapeDtypeStruct((slot[2], 2, counts[slot[3]], block), jnp.bfloat16) for slot in slots],
        scratch_shapes=[pltpu.VMEM((2, SUB, block, block), jnp.bfloat16)] * 2,
        input_output_aliases={4 + n_far + i: n for i, n in enumerate(spots)},
        compiler_params=pltpu.CompilerParams(vmem_limit_bytes=VMEM_BYTES),
        cost_estimate=pl.CostEstimate(
            flops=SUB * 8 * seg * block * block, bytes_accessed=SUB * 16 * seg * block, transcendentals=0
        ),
        name="cross_piece",
    )(me, own, own_inv, far_lift, *far, *[made[slots[n]] for n in spots])
    return {**made, **dict(zip(slots, flat))}


def lag_kernel(sources, rows, group, n_given, n_held, to_output, lag_ref, back_ref, *refs):
    n_pieces = sum(len(places) for places in sources)
    pieces, given = refs[:n_pieces], refs[n_pieces : n_pieces + n_given]
    out_ref, lag_scr, norm_scr, *rest = refs[n_pieces + n_given + n_held :]
    block = pieces[0].shape[3]
    width = AT_ONCE * block
    row_ref = rest[0] if to_output else out_ref
    first = SUB - rows if to_output else 0

    def column(r):
        parts, at = [], 0
        for places in sources:
            for part in range(2):
                parts += [piece[place + r, part] for piece, place in zip(pieces[at:], places)]
            at += len(places)
        return jnp.concatenate(parts, axis=0)

    for r in range(0, rows, AT_ONCE):
        cols = jnp.concatenate([column(r + k) for k in range(AT_ONCE)], axis=1)
        lag_scr[...] = jnp.dot(lag_ref[...], cols, preferred_element_type=jnp.float32)
        total = jnp.zeros((8, width), jnp.float32)
        for at in range(0, LAGS, SLICE):
            lag_re, lag_im = lag_scr[at : at + SLICE], lag_scr[LAGS + at : LAGS + at + SLICE]
            energy = lag_re * lag_re + lag_im * lag_im
            lag_scr[LAGS + at : LAGS + at + SLICE] = energy
            total += jnp.sum(energy.reshape(SLICE // 8, 8, width), axis=0)
        floor = (0.25 / LAGS) * jnp.sum(total, axis=0, keepdims=True) + 1e-05
        for at in range(0, LAGS, SLICE):
            scale = lax.rsqrt(lag_scr[LAGS + at : LAGS + at + SLICE] + floor)
            norm_scr[at : at + SLICE] = (lag_scr[at : at + SLICE] * scale).astype(jnp.bfloat16)
        lag_scr[: 2 * F] = jnp.dot(back_ref[...], norm_scr[...], preferred_element_type=jnp.float32)
        for at in range(0, 2 * F, SLICE):
            back = (lag_scr[at : at + SLICE] * (1.0 / math.sqrt(LAGS))).astype(jnp.bfloat16)
            for k in range(AT_ONCE):
                row_ref[first + r + k, at : at + SLICE] = back[:, k * block : (k + 1) * block]
    if to_output:
        _, bins_ref, sems = rest
        matrix = interleave()
        copies = []
        chunk = 2 * F // PARTS
        for at in range(0, 2 * F, 2 * SUB):
            whole = [x[:, at : at + 2 * SUB] for x in given] + [row_ref[first:, at : at + 2 * SUB]]
            whole = jnp.concatenate(whole, axis=0)
            turned = turned_rows(matrix, whole[:, :SUB], whole[:, SUB:])
            for n in range(2):
                bins = turned[:, :, n * block : (n + 1) * block]
                bins_ref[at + n * SUB : at + (n + 1) * SUB] = bins.astype(jnp.bfloat16)
            if (at + 2 * SUB) % chunk == 0:
                start = at + 2 * SUB - chunk
                there = out_ref.at[0, start // F, pl.ds(start % F, chunk), pl.ds(group * SUB, SUB)]
                copies.append(pltpu.make_async_copy(bins_ref.at[pl.ds(start, chunk)], there, sems.at[start // chunk]))
                copies[-1].start()
        for copy in copies:
            copy.wait()


def lag_group(rows, group, groups, lag_table, back_table, sources, given, before, to_output=True):
    pieces = [piece for source in sources for piece, _ in source]
    places = [[place for _, place in source] for source in sources]
    block = pieces[0].shape[3]
    vmem, scratch = pl.BlockSpec(memory_space=pltpu.VMEM), [
        pltpu.VMEM((2 * LAGS, AT_ONCE * block), jnp.float32),
        pltpu.VMEM((LAGS, AT_ONCE * block), jnp.bfloat16),
    ]
    if to_output:
        out_spec = pl.BlockSpec(memory_space=pltpu.HBM)
        out_shape = jax.ShapeDtypeStruct((1, 2, F, SUB * groups, block), jnp.bfloat16)
        scratch += [
            pltpu.VMEM((SUB, 2 * F, block), jnp.bfloat16),
            pltpu.VMEM((2 * F, SUB, block), jnp.bfloat16),
            pltpu.SemaphoreType.DMA((PARTS,)),
        ]
    else:
        out_spec = vmem
        out_shape = jax.ShapeDtypeStruct((rows, 2 * F, block), jnp.bfloat16)
    return pl.pallas_call(
        functools.partial(lag_kernel, places, rows, group, len(given), len(before), to_output),
        in_specs=[vmem] * (2 + len(pieces) + len(given)) + [pl.BlockSpec(memory_space=pltpu.HBM)] * len(before),
        out_specs=out_spec,
        out_shape=out_shape,
        scratch_shapes=scratch,
        input_output_aliases={2 + len(pieces) + len(given): 0} if before else {},
        compiler_params=pltpu.CompilerParams(vmem_limit_bytes=VMEM_BYTES),
        cost_estimate=NO_COST,
        name="lag_group",
    )(lag_table, back_table, *pieces, *given, *before)


def shards(spectra, seg_mask):
    tile_count, freq_count = lax.axis_size("tile"), lax.axis_size("freq")
    half_axis = tile_count // 2
    _, seg, band, block = spectra.shape
    half = band // 2
    n_sub = half // SUB
    groups = block // freq_count // SUB
    me = lax.axis_index("freq")
    side = lax.axis_index("tile") // half_axis
    keep_from, send_from = side * half, (1 - side) * half

    across = [(t, (t + half_axis) % tile_count) for t in range(tile_count)]

    def moved(block, d, distance):
        route = []
        for h in range(freq_count):
            for t in range(tile_count):
                route.append((h * tile_count + t, (h + d) % freq_count * tile_count + (t + distance) % tile_count))
        return lax.ppermute(block, ("freq", "tile"), route)

    keep_sub, send_sub = side * n_sub, (1 - side) * n_sub
    *pieces, power = prepare(spectra, seg_mask, send_sub, 1, (SHORT, SUB - SHORT))
    send_power, counts = [power], [2]
    if n_sub > 1:
        piece, power = prepare(spectra, seg_mask, send_sub + 1, 1, (SUB,))
        pieces.append(piece)
        send_power.append(power)
        counts.append(1)
    far = [lax.ppermute(piece, "tile", across) for piece in pieces]
    rest, far[0] = lax.optimization_barrier((spectra, far[0]))
    pieces = []
    for i in range(2, n_sub):
        *both, power = prepare(rest, seg_mask, send_sub + i, 1, (SUB // 2, SUB // 2))
        rest, both = lax.optimization_barrier((rest, both))
        pieces += both
        send_power.append(power)
        counts.append(2)
    own, own_power = prepare(rest, seg_mask, keep_sub, n_sub, (half,))
    send_power = jnp.concatenate(send_power, axis=0)

    total = lax.psum(jnp.sum(own_power, axis=0) + jnp.sum(send_power, axis=0), "freq")
    lift = WATER * (total / F)[None, :]
    own_inv = (1.0 / ((own_power + lift) * seg)).T
    local = jnp.arange(half, dtype=jnp.int32)
    lag_cols = []
    for mine in (True, False):
        for d in range(freq_count):
            freqs = (me - d) % freq_count * band + (keep_from if mine else send_from) + local
            cos_tab, sin_tab = dft_tables(freqs)
            lag_cols.append(jnp.concatenate([cos_tab, sin_tab], axis=0))
            lag_cols.append(jnp.concatenate([-sin_tab, cos_tab], axis=0))
    lag_table = jnp.concatenate(lag_cols, axis=1)
    cos_tab, sin_tab = dft_tables(jnp.arange(F, dtype=jnp.int32))
    back_table = jnp.concatenate([cos_tab, -sin_tab], axis=1).T

    far_total = None
    for i, piece in enumerate(pieces):
        if i == 0:
            shape = piece.shape
            piece, terms, own_inv, lag_table, back_table = lax.optimization_barrier(
                (piece, exact_terms(total), own_inv, lag_table, back_table)
            )
            piece = jnp.concatenate([piece.reshape(-1, block), terms], axis=0)
        if i >= 2:
            piece, far[i - 1] = lax.optimization_barrier((piece, far[i - 1]))
        got = lax.ppermute(piece, "tile", across)
        if i == 0:
            far_total = jnp.sum(got[-SUB:].astype(jnp.float32), axis=0)
            got = got[:-SUB].reshape(shape)
        far.append(got)
    if far_total is None:
        far_total = lax.ppermute(total, "tile", across)
    far_lift = WATER * (far_total / F)[None, :]

    n_split = groups // 2 if n_sub > 1 else 0
    full = groups * SUB
    early_rows = n_split * SUB
    first_parts = [(j * SUB, SUB, "early") for j in range(n_split)]
    late_parts = [(0, early_rows, "late")] if n_split else []
    own_rest = [(early_rows, full - early_rows, "all")]
    halves = [(row, SUB // 2, "all") for row in range(early_rows, full, SUB // 2)] if groups > 1 else own_rest
    places = [first_parts + late_parts + (own_rest if k < freq_count else halves) for k in range(2 * freq_count)]
    slots = [(k, *place) for k in range(2 * freq_count) for place in places[k]]
    me_arr = me.astype(jnp.int32).reshape(1)
    ready = max(sum(counts[:-1]) - 1, 0)
    far[ready], lag_table, back_table, own_inv, far_lift, own = lax.optimization_barrier(
        (far[ready], lag_table, back_table, own_inv, far_lift, own)
    )
    far = [far[sum(counts[:i]) : sum(counts[: i + 1])] for i in range(n_sub)]
    made = {}
    for i in range(n_sub):
        made = cross_piece(i, freq_count, groups, slots, me_arr, own, far[i], own_inv, far_lift, made)

    arrived = {}

    def send(place, wait_for=None):
        kinds = [k for k in range(1, 2 * freq_count) if place in places[k]]
        outgoing = [made[(k, *place)] for k in kinds]
        if wait_for is not None:
            outgoing, arrived[wait_for] = lax.optimization_barrier((outgoing, arrived[wait_for]))
        if wait_for is not None and place == halves[-1]:
            outgoing, state["out"] = lax.optimization_barrier((outgoing, state["out"]))
        moves = [moved(x, k % freq_count, half_axis * (k // freq_count)) for k, x in zip(kinds, outgoing)]
        arrived[place] = dict(zip(kinds, moves))

    def transform(place):
        first_row, rows, _ = place
        sources = []
        for k in range(2 * freq_count):
            holds = [hold for hold in places[k] if hold[0] <= first_row < hold[0] + hold[1]]
            sources.append([(arrived[hold][k] if k else made[(0, *hold)], first_row - hold[0]) for hold in holds])
        group, ends = first_row // SUB, (first_row + rows) % SUB == 0
        before = state["out"] if ends else []
        done = lag_group(rows, group, groups, lag_table, back_table, sources, state["given"], before, to_output=ends)
        state["given" if not ends else "out"] = [done]
        if ends:
            state["given"] = []

    state = {"given": [], "out": []}
    for place in first_parts + late_parts:
        send(place)
    if own_rest != halves:
        send(own_rest[0])
    chain = first_parts + late_parts + halves
    for n, place in enumerate(halves, start=len(chain) - len(halves)):
        if place == halves[-1]:
            for part in first_parts:
                transform(part)
        send(place, chain[n - 2] if n >= 2 else None)
    for place in halves:
        if place in halves[-2:-1]:
            arrived[place], state["out"] = lax.optimization_barrier((arrived[place], state["out"]))
        transform(place)
    out = state["out"]
    return out[0]


def solution(mesh):
    placed = (P(None, None, "freq", "tile"), P(None, "tile"))
    return jax.shard_map(
        shards,
        mesh=mesh,
        in_specs=placed,
        out_specs=P("tile", None, None, "freq", None),
        check_vma=False,
    )
```

```python
import functools
import math

import jax
import jax.numpy as jnp
from jax import lax
from jax.experimental import pallas as pl
from jax.experimental.pallas import tpu as pltpu
from jax.sharding import PartitionSpec as P

F = 256
LAGS = 512
WATER = 0.05
SUB = 16
SHORT = 4
AT_ONCE = 8
PARTS = 4
SLICE = 16
VMEM_BYTES = 28 * 2**20
PREPARE_BYTES = 44 * 2**20
NO_COST = pl.CostEstimate(flops=0, bytes_accessed=0, transcendentals=0)


def dft_tables(freq_index):
    lag_index = jnp.arange(LAGS, dtype=jnp.int32)[:, None]
    phase = (lag_index * freq_index[None, :] % LAGS).astype(jnp.float32) * (2.0 * math.pi / LAGS)
    return jnp.cos(phase).astype(jnp.bfloat16), jnp.sin(phase).astype(jnp.bfloat16)


def rounded(x):
    return x.astype(jnp.bfloat16).astype(jnp.float32)


def interleave():
    row = lax.broadcasted_iota(jnp.int32, (SUB * SUB, SUB * SUB), 0)
    col = lax.broadcasted_iota(jnp.int32, (SUB * SUB, SUB * SUB), 1)
    return jnp.where(col == row % SUB * SUB + row // SUB, 1.0, 0.0).astype(jnp.bfloat16)


def turned_rows(matrix, left, right):
    lanes = left.shape[2]
    both = jnp.concatenate([left.reshape(SUB * SUB, lanes), right.reshape(SUB * SUB, lanes)], axis=1)
    return jnp.dot(matrix, both, preferred_element_type=jnp.float32).reshape(SUB, SUB, 2 * lanes)


def prepare_kernel(at_ref, x_ref, mask_ref, *outs):
    parts, power_ref = outs[:-1], outs[-1]
    seg, lanes = mask_ref.shape
    matrix = interleave()
    total = jnp.zeros((SUB, 8, lanes), jnp.float32)
    for s in range(0, seg, SUB):
        mask = mask_ref[s : s + SUB].astype(jnp.float32)[None]
        turned = turned_rows(matrix, x_ref[0, s : s + SUB], x_ref[1, s : s + SUB])
        for part in range(2):
            val = turned[:, :, part * lanes : (part + 1) * lanes] * mask
            square = val * val
            total += square[:, :8] + square[:, 8:]
            at = 0
            for out in parts:
                count = out.shape[0]
                out[:, part, s : s + SUB] = val[at : at + count].astype(jnp.bfloat16)
                at += count
    power_ref[...] = jnp.sum(total, axis=1) * (1.0 / seg) + 1e-05


def prepare(spectra, seg_mask, first, steps, counts):
    _, seg, _, block = spectra.shape
    assert sum(counts) == steps * SUB and (steps == 1 or len(counts) == 1)
    out_specs = [pl.BlockSpec((min(count, SUB), 2, seg, block), lambda i, at: (i, 0, 0, 0)) for count in counts]
    out_shape = [jax.ShapeDtypeStruct((count, 2, seg, block), jnp.bfloat16) for count in counts]
    return pl.pallas_call(
        prepare_kernel,
        grid_spec=pltpu.PrefetchScalarGridSpec(
            num_scalar_prefetch=1,
            grid=(steps,),
            in_specs=[
                pl.BlockSpec((2, seg, SUB, block), lambda i, at: (0, 0, at[0] + i, 0)),
                pl.BlockSpec((seg, block), lambda i, at: (0, 0)),
            ],
            out_specs=out_specs + [pl.BlockSpec((SUB, block), lambda i, at: (i, 0))],
        ),
        out_shape=out_shape + [jax.ShapeDtypeStruct((steps * SUB, block), jnp.float32)],
        compiler_params=pltpu.CompilerParams(vmem_limit_bytes=PREPARE_BYTES),
        cost_estimate=NO_COST,
        name="prepare",
    )(first.astype(jnp.int32).reshape(1), spectra, seg_mask)


def exact_terms(x):
    terms, rest = [], x
    for _ in range(3):
        terms.append(lax.reduce_precision(rest, 8, 7))
        rest = rest - terms[-1]
    return jnp.pad(jnp.stack(terms).astype(jnp.bfloat16), ((0, SUB - 3), (0, 0)))


def cross_kernel(piece, freq_count, groups, slots, held, n_far, me_ref, own_ref, own_inv_ref, far_lift_ref, *refs):
    far_refs, outs, (own_scr, far_scr) = refs[:n_far], refs[n_far + held : -2], refs[-2:]
    seg = own_ref.shape[2]
    block = own_ref.shape[3]
    far_rows = [(far_ref, k) for far_ref in far_refs for k in range(far_ref.shape[0])]
    for f in range(SUB):
        own = own_ref[f].reshape(2 * seg, block)
        far_ref, k = far_rows[f]
        far_re, far_im = far_ref[k, 0], far_ref[k, 1]
        cols = jnp.concatenate(
            [jnp.concatenate([far_re, far_im], axis=0), jnp.concatenate([far_im, -far_re], axis=0)], axis=1
        )
        cross = lax.dot_general(own, cols, (((0,), (0,)), ((), ())), preferred_element_type=jnp.float32)
        at = piece * SUB + f
        own_inv = own_inv_ref[:, at : at + 1]
        square = jnp.square(far_re.astype(jnp.float32)) + jnp.square(far_im.astype(jnp.float32))
        far_power = jnp.sum(square, axis=0, keepdims=True) * (1.0 / seg) + 1e-05
        far_inv = 1.0 / ((far_power + far_lift_ref[...]) * seg)
        for part in range(2):
            val = cross[:, part * block : (part + 1) * block]
            sym = 0.5 * (rounded(val * own_inv) + rounded(val * far_inv))
            own_scr[part, f] = sym.astype(jnp.bfloat16)
            turned = jnp.transpose(sym if part == 0 else -sym)
            far_scr[part, f] = turned.astype(jnp.bfloat16)
    me = me_ref[0]
    matrix = interleave()
    for k in range(2 * freq_count):
        scr = own_scr if k < freq_count else far_scr
        for j in range(groups):
            first = (lax.rem(me + k % freq_count, freq_count) * groups + j) * SUB
            rows = pl.ds(pl.multiple_of(first, SUB), SUB)
            turned = turned_rows(matrix, scr[0, :, rows, :], scr[1, :, rows, :])
            for out, (kind, first_row, count, _) in zip(outs, slots):
                low, high = max(first_row, j * SUB), min(first_row + count, (j + 1) * SUB)
                if kind != k or low >= high:
                    continue
                for part in range(2):
                    vals = turned[low - j * SUB : high - j * SUB, :, part * block : (part + 1) * block]
                    out[low - first_row : high - first_row, part] = vals.astype(jnp.bfloat16)


def cross_piece(piece, freq_count, groups, slots, me, own, far, own_inv, far_lift, made):
    half, _, seg, block = own.shape
    n_far = len(far)
    last = (piece + 1) * SUB == half
    slots = [slot for slot in slots if slot[3] == "all" or (slot[3] == "late") == last]
    counts = {"all": half, "early": half - SUB, "late": SUB}
    places = [0 if slot[3] == "late" else piece for slot in slots]
    spots = [n for n, slot in enumerate(slots) if slot in made]
    flat = pl.pallas_call(
        functools.partial(cross_kernel, piece, freq_count, groups, slots, len(spots), n_far),
        grid=(1,),
        in_specs=[
            pl.BlockSpec(memory_space=pltpu.SMEM),
            pl.BlockSpec((SUB, 2, seg, block), lambda i: (piece, 0, 0, 0)),
            pl.BlockSpec((block, half), lambda i: (0, 0)),
            pl.BlockSpec((1, block), lambda i: (0, 0)),
        ]
        + [pl.BlockSpec(x.shape, lambda i: (0, 0, 0, 0)) for x in far]
        + [pl.BlockSpec(memory_space=pl.ANY)] * len(spots),
        out_specs=[
            pl.BlockSpec((slot[2], 2, SUB, block), functools.partial(lambda at, i: (0, 0, at, 0), at))
            for slot, at in zip(slots, places)
        ],
        out_shape=[jax.ShapeDtypeStruct((slot[2], 2, counts[slot[3]], block), jnp.bfloat16) for slot in slots],
        scratch_shapes=[pltpu.VMEM((2, SUB, block, block), jnp.bfloat16)] * 2,
        input_output_aliases={4 + n_far + i: n for i, n in enumerate(spots)},
        compiler_params=pltpu.CompilerParams(vmem_limit_bytes=VMEM_BYTES),
        cost_estimate=pl.CostEstimate(
            flops=SUB * 8 * seg * block * block, bytes_accessed=SUB * 16 * seg * block, transcendentals=0
        ),
        name="cross_piece",
    )(me, own, own_inv, far_lift, *far, *[made[slots[n]] for n in spots])
    return {**made, **dict(zip(slots, flat))}


def lag_kernel(sources, rows, group, n_given, n_held, to_output, lag_ref, back_ref, *refs):
    n_pieces = sum(len(places) for places in sources)
    pieces, given = refs[:n_pieces], refs[n_pieces : n_pieces + n_given]
    out_ref, lag_scr, norm_scr, *rest = refs[n_pieces + n_given + n_held :]
    block = pieces[0].shape[3]
    width = AT_ONCE * block
    row_ref = rest[0] if to_output else out_ref
    first = SUB - rows if to_output else 0

    def column(r):
        parts, at = [], 0
        for places in sources:
            for part in range(2):
                parts += [piece[place + r, part] for piece, place in zip(pieces[at:], places)]
            at += len(places)
        return jnp.concatenate(parts, axis=0)

    for r in range(0, rows, AT_ONCE):
        cols = jnp.concatenate([column(r + k) for k in range(AT_ONCE)], axis=1)
        lag_scr[...] = jnp.dot(lag_ref[...], cols, preferred_element_type=jnp.float32)
        total = jnp.zeros((8, width), jnp.float32)
        for at in range(0, LAGS, SLICE):
            lag_re, lag_im = lag_scr[at : at + SLICE], lag_scr[LAGS + at : LAGS + at + SLICE]
            energy = lag_re * lag_re + lag_im * lag_im
            lag_scr[LAGS + at : LAGS + at + SLICE] = energy
            total += jnp.sum(energy.reshape(SLICE // 8, 8, width), axis=0)
        floor = (0.25 / LAGS) * jnp.sum(total, axis=0, keepdims=True) + 1e-05
        for at in range(0, LAGS, SLICE):
            scale = lax.rsqrt(lag_scr[LAGS + at : LAGS + at + SLICE] + floor)
            norm_scr[at : at + SLICE] = (lag_scr[at : at + SLICE] * scale).astype(jnp.bfloat16)
        lag_scr[: 2 * F] = jnp.dot(back_ref[...], norm_scr[...], preferred_element_type=jnp.float32)
        for at in range(0, 2 * F, SLICE):
            back = (lag_scr[at : at + SLICE] * (1.0 / math.sqrt(LAGS))).astype(jnp.bfloat16)
            for k in range(AT_ONCE):
                row_ref[first + r + k, at : at + SLICE] = back[:, k * block : (k + 1) * block]
    if to_output:
        _, bins_ref, sems = rest
        matrix = interleave()
        copies = []
        chunk = 2 * F // PARTS
        for at in range(0, 2 * F, 2 * SUB):
            whole = [x[:, at : at + 2 * SUB] for x in given] + [row_ref[first:, at : at + 2 * SUB]]
            whole = jnp.concatenate(whole, axis=0)
            turned = turned_rows(matrix, whole[:, :SUB], whole[:, SUB:])
            for n in range(2):
                bins = turned[:, :, n * block : (n + 1) * block]
                bins_ref[at + n * SUB : at + (n + 1) * SUB] = bins.astype(jnp.bfloat16)
            if (at + 2 * SUB) % chunk == 0:
                start = at + 2 * SUB - chunk
                there = out_ref.at[0, start // F, pl.ds(start % F, chunk), pl.ds(group * SUB, SUB)]
                copies.append(pltpu.make_async_copy(bins_ref.at[pl.ds(start, chunk)], there, sems.at[start // chunk]))
                copies[-1].start()
        for copy in copies:
            copy.wait()


def lag_group(rows, group, groups, lag_table, back_table, sources, given, before, to_output=True):
    pieces = [piece for source in sources for piece, _ in source]
    places = [[place for _, place in source] for source in sources]
    block = pieces[0].shape[3]
    vmem, scratch = pl.BlockSpec(memory_space=pltpu.VMEM), [
        pltpu.VMEM((2 * LAGS, AT_ONCE * block), jnp.float32),
        pltpu.VMEM((LAGS, AT_ONCE * block), jnp.bfloat16),
    ]
    if to_output:
        out_spec = pl.BlockSpec(memory_space=pltpu.HBM)
        out_shape = jax.ShapeDtypeStruct((1, 2, F, SUB * groups, block), jnp.bfloat16)
        scratch += [
            pltpu.VMEM((SUB, 2 * F, block), jnp.bfloat16),
            pltpu.VMEM((2 * F, SUB, block), jnp.bfloat16),
            pltpu.SemaphoreType.DMA((PARTS,)),
        ]
    else:
        out_spec = vmem
        out_shape = jax.ShapeDtypeStruct((rows, 2 * F, block), jnp.bfloat16)
    return pl.pallas_call(
        functools.partial(lag_kernel, places, rows, group, len(given), len(before), to_output),
        in_specs=[vmem] * (2 + len(pieces) + len(given)) + [pl.BlockSpec(memory_space=pltpu.HBM)] * len(before),
        out_specs=out_spec,
        out_shape=out_shape,
        scratch_shapes=scratch,
        input_output_aliases={2 + len(pieces) + len(given): 0} if before else {},
        compiler_params=pltpu.CompilerParams(vmem_limit_bytes=VMEM_BYTES),
        cost_estimate=NO_COST,
        name="lag_group",
    )(lag_table, back_table, *pieces, *given, *before)


def shards(spectra, seg_mask):
    tile_count, freq_count = lax.axis_size("tile"), lax.axis_size("freq")
    half_axis = tile_count // 2
    _, seg, band, block = spectra.shape
    half = band // 2
    n_sub = half // SUB
    groups = block // freq_count // SUB
    me = lax.axis_index("freq")
    side = lax.axis_index("tile") // half_axis
    keep_from, send_from = side * half, (1 - side) * half

    across = [(t, (t + half_axis) % tile_count) for t in range(tile_count)]

    def moved(block, d, distance):
        route = []
        for h in range(freq_count):
            for t in range(tile_count):
                route.append((h * tile_count + t, (h + d) % freq_count * tile_count + (t + distance) % tile_count))
        return lax.ppermute(block, ("freq", "tile"), route)

    keep_sub, send_sub = side * n_sub, (1 - side) * n_sub
    *pieces, power = prepare(spectra, seg_mask, send_sub, 1, (SHORT, SUB - SHORT))
    send_power, counts = [power], [2]
    if n_sub > 1:
        piece, power = prepare(spectra, seg_mask, send_sub + 1, 1, (SUB,))
        pieces.append(piece)
        send_power.append(power)
        counts.append(1)
    far = [lax.ppermute(piece, "tile", across) for piece in pieces]
    rest, far[0] = lax.optimization_barrier((spectra, far[0]))
    pieces = []
    for i in range(2, n_sub):
        *both, power = prepare(rest, seg_mask, send_sub + i, 1, (SUB // 2, SUB // 2))
        rest, both = lax.optimization_barrier((rest, both))
        pieces += both
        send_power.append(power)
        counts.append(2)
    own, own_power = prepare(rest, seg_mask, keep_sub, n_sub, (half,))
    send_power = jnp.concatenate(send_power, axis=0)

    total = lax.psum(jnp.sum(own_power, axis=0) + jnp.sum(send_power, axis=0), "freq")
    lift = WATER * (total / F)[None, :]
    own_inv = (1.0 / ((own_power + lift) * seg)).T
    local = jnp.arange(half, dtype=jnp.int32)
    lag_cols = []
    for mine in (True, False):
        for d in range(freq_count):
            freqs = (me - d) % freq_count * band + (keep_from if mine else send_from) + local
            cos_tab, sin_tab = dft_tables(freqs)
            lag_cols.append(jnp.concatenate([cos_tab, sin_tab], axis=0))
            lag_cols.append(jnp.concatenate([-sin_tab, cos_tab], axis=0))
    lag_table = jnp.concatenate(lag_cols, axis=1)
    cos_tab, sin_tab = dft_tables(jnp.arange(F, dtype=jnp.int32))
    back_table = jnp.concatenate([cos_tab, -sin_tab], axis=1).T

    far_total = None
    for i, piece in enumerate(pieces):
        if i == 0:
            shape = piece.shape
            piece, terms, own_inv, lag_table, back_table = lax.optimization_barrier(
                (piece, exact_terms(total), own_inv, lag_table, back_table)
            )
            piece = jnp.concatenate([piece.reshape(-1, block), terms], axis=0)
        if i >= 2:
            piece, far[i - 1] = lax.optimization_barrier((piece, far[i - 1]))
        got = lax.ppermute(piece, "tile", across)
        if i == 0:
            far_total = jnp.sum(got[-SUB:].astype(jnp.float32), axis=0)
            got = got[:-SUB].reshape(shape)
        far.append(got)
    if far_total is None:
        far_total = lax.ppermute(total, "tile", across)
    far_lift = WATER * (far_total / F)[None, :]

    n_split = groups // 2 if n_sub > 1 else 0
    full = groups * SUB
    early_rows = n_split * SUB
    first_parts = [(j * SUB, SUB, "early") for j in range(n_split)]
    late_parts = [(0, early_rows, "late")] if n_split else []
    own_rest = [(early_rows, full - early_rows, "all")]
    halves = [(row, SUB // 2, "all") for row in range(early_rows, full, SUB // 2)] if groups > 1 else own_rest
    places = [first_parts + late_parts + (own_rest if k < freq_count else halves) for k in range(2 * freq_count)]
    slots = [(k, *place) for k in range(2 * freq_count) for place in places[k]]
    me_arr = me.astype(jnp.int32).reshape(1)
    ready = max(sum(counts[:-1]) - 1, 0)
    far[ready], lag_table, back_table, own_inv, far_lift, own = lax.optimization_barrier(
        (far[ready], lag_table, back_table, own_inv, far_lift, own)
    )
    far = [far[sum(counts[:i]) : sum(counts[: i + 1])] for i in range(n_sub)]
    made = {}
    for i in range(n_sub):
        made = cross_piece(i, freq_count, groups, slots, me_arr, own, far[i], own_inv, far_lift, made)

    arrived = {}

    def send(place, wait_for=None):
        kinds = [k for k in range(1, 2 * freq_count) if place in places[k]]
        outgoing = [made[(k, *place)] for k in kinds]
        if wait_for is not None:
            outgoing, arrived[wait_for] = lax.optimization_barrier((outgoing, arrived[wait_for]))
        if wait_for is not None and place == halves[-1]:
            outgoing, state["out"] = lax.optimization_barrier((outgoing, state["out"]))
        moves = [moved(x, k % freq_count, half_axis * (k // freq_count)) for k, x in zip(kinds, outgoing)]
        arrived[place] = dict(zip(kinds, moves))

    def transform(place):
        first_row, rows, _ = place
        sources = []
        for k in range(2 * freq_count):
            holds = [hold for hold in places[k] if hold[0] <= first_row < hold[0] + hold[1]]
            sources.append([(arrived[hold][k] if k else made[(0, *hold)], first_row - hold[0]) for hold in holds])
        group, ends = first_row // SUB, (first_row + rows) % SUB == 0
        before = state["out"] if ends else []
        done = lag_group(rows, group, groups, lag_table, back_table, sources, state["given"], before, to_output=ends)
        state["given" if not ends else "out"] = [done]
        if ends:
            state["given"] = []

    state = {"given": [], "out": []}
    for place in first_parts + late_parts:
        send(place)
    if own_rest != halves:
        send(own_rest[0])
    chain = first_parts + late_parts + halves
    for n, place in enumerate(halves, start=len(chain) - len(halves)):
        if place == halves[-1]:
            for part in first_parts:
                transform(part)
        send(place, chain[n - 2] if n >= 2 else None)
    for place in halves:
        if place in halves[-2:-1]:
            arrived[place], state["out"] = lax.optimization_barrier((arrived[place], state["out"]))
        transform(place)
    out = state["out"]
    return out[0]


def solution(mesh):
    placed = (P(None, None, "freq", "tile"), P(None, "tile"))
    return jax.shard_map(
        shards,
        mesh=mesh,
        in_specs=placed,
        out_specs=P("tile", None, None, "freq", None),
        check_vma=False,
    )
```

```python
import functools
import math

import jax
import jax.numpy as jnp
from jax import lax
from jax.experimental import pallas as pl
from jax.experimental.pallas import tpu as pltpu
from jax.sharding import PartitionSpec as P

F = 256
LAGS = 512
WATER = 0.05
SUB = 16
SHORT = 4
AT_ONCE = 8
PARTS = 4
SLICE = 16
VMEM_BYTES = 28 * 2**20
PREPARE_BYTES = 48 * 2**20
NO_COST = pl.CostEstimate(flops=0, bytes_accessed=0, transcendentals=0)


def dft_tables(freq_index):
    lag_index = jnp.arange(LAGS, dtype=jnp.int32)[:, None]
    phase = (lag_index * freq_index[None, :] % LAGS).astype(jnp.float32) * (2.0 * math.pi / LAGS)
    return jnp.cos(phase).astype(jnp.bfloat16), jnp.sin(phase).astype(jnp.bfloat16)


def rounded(x):
    return x.astype(jnp.bfloat16).astype(jnp.float32)


def interleave():
    row = lax.broadcasted_iota(jnp.int32, (SUB * SUB, SUB * SUB), 0)
    col = lax.broadcasted_iota(jnp.int32, (SUB * SUB, SUB * SUB), 1)
    return jnp.where(col == row % SUB * SUB + row // SUB, 1.0, 0.0).astype(jnp.bfloat16)


def turned_rows(matrix, left, right):
    lanes = left.shape[2]
    both = jnp.concatenate([left.reshape(SUB * SUB, lanes), right.reshape(SUB * SUB, lanes)], axis=1)
    return jnp.dot(matrix, both, preferred_element_type=jnp.float32).reshape(SUB, SUB, 2 * lanes)


def prepare_kernel(at_ref, x_ref, mask_ref, *outs):
    parts, power_ref = outs[:-1], outs[-1]
    seg, lanes = mask_ref.shape
    matrix = interleave()
    total = jnp.zeros((SUB, 8, lanes), jnp.float32)
    for s in range(0, seg, SUB):
        mask = mask_ref[s : s + SUB].astype(jnp.float32)[None]
        turned = turned_rows(matrix, x_ref[0, s : s + SUB], x_ref[1, s : s + SUB])
        for part in range(2):
            val = turned[:, :, part * lanes : (part + 1) * lanes] * mask
            square = val * val
            total += square[:, :8] + square[:, 8:]
            at = 0
            for out in parts:
                count = out.shape[0]
                out[:, part, s : s + SUB] = val[at : at + count].astype(jnp.bfloat16)
                at += count
    power_ref[...] = jnp.sum(total, axis=1) * (1.0 / seg) + 1e-05


def prepare(spectra, seg_mask, first, steps, counts):
    _, seg, _, block = spectra.shape
    assert sum(counts) == steps * SUB and (steps == 1 or len(counts) == 1)
    out_specs = [pl.BlockSpec((min(count, SUB), 2, seg, block), lambda i, at: (i, 0, 0, 0)) for count in counts]
    out_shape = [jax.ShapeDtypeStruct((count, 2, seg, block), jnp.bfloat16) for count in counts]
    if steps > 1:
        out_shape = [pltpu.HBM(x.shape, x.dtype) for x in out_shape]
    return pl.pallas_call(
        prepare_kernel,
        grid_spec=pltpu.PrefetchScalarGridSpec(
            num_scalar_prefetch=1,
            grid=(steps,),
            in_specs=[
                pl.BlockSpec((2, seg, SUB, block), lambda i, at: (0, 0, at[0] + i, 0)),
                pl.BlockSpec((seg, block), lambda i, at: (0, 0)),
            ],
            out_specs=out_specs + [pl.BlockSpec((SUB, block), lambda i, at: (i, 0))],
        ),
        out_shape=out_shape + [jax.ShapeDtypeStruct((steps * SUB, block), jnp.float32)],
        compiler_params=pltpu.CompilerParams(vmem_limit_bytes=PREPARE_BYTES),
        cost_estimate=NO_COST,
        name="prepare",
    )(first.astype(jnp.int32).reshape(1), spectra, seg_mask)


def exact_terms(x):
    terms, rest = [], x
    for _ in range(3):
        terms.append(lax.reduce_precision(rest, 8, 7))
        rest = rest - terms[-1]
    return jnp.pad(jnp.stack(terms).astype(jnp.bfloat16), ((0, SUB - 3), (0, 0)))


def cross_kernel(piece, freq_count, groups, slots, held, n_far, me_ref, own_ref, own_inv_ref, far_lift_ref, *refs):
    far_refs, outs, (own_scr, far_scr) = refs[:n_far], refs[n_far + held : -2], refs[-2:]
    seg = own_ref.shape[2]
    block = own_ref.shape[3]
    far_rows = [(far_ref, k) for far_ref in far_refs for k in range(far_ref.shape[0])]
    for f in range(SUB):
        own = own_ref[f].reshape(2 * seg, block)
        far_ref, k = far_rows[f]
        far_re, far_im = far_ref[k, 0], far_ref[k, 1]
        cols = jnp.concatenate(
            [jnp.concatenate([far_re, far_im], axis=0), jnp.concatenate([far_im, -far_re], axis=0)], axis=1
        )
        cross = lax.dot_general(own, cols, (((0,), (0,)), ((), ())), preferred_element_type=jnp.float32)
        at = piece * SUB + f
        own_inv = own_inv_ref[:, at : at + 1]
        square = jnp.square(far_re.astype(jnp.float32)) + jnp.square(far_im.astype(jnp.float32))
        far_power = jnp.sum(square, axis=0, keepdims=True) * (1.0 / seg) + 1e-05
        far_inv = 1.0 / ((far_power + far_lift_ref[...]) * seg)
        for part in range(2):
            val = cross[:, part * block : (part + 1) * block]
            sym = 0.5 * (rounded(val * own_inv) + rounded(val * far_inv))
            own_scr[part, f] = sym.astype(jnp.bfloat16)
            turned = jnp.transpose(sym if part == 0 else -sym)
            far_scr[part, f] = turned.astype(jnp.bfloat16)
    me = me_ref[0]
    matrix = interleave()
    for k in range(2 * freq_count):
        scr = own_scr if k < freq_count else far_scr
        for j in range(groups):
            first = (lax.rem(me + k % freq_count, freq_count) * groups + j) * SUB
            rows = pl.ds(pl.multiple_of(first, SUB), SUB)
            turned = turned_rows(matrix, scr[0, :, rows, :], scr[1, :, rows, :])
            for out, (kind, first_row, count, _) in zip(outs, slots):
                low, high = max(first_row, j * SUB), min(first_row + count, (j + 1) * SUB)
                if kind != k or low >= high:
                    continue
                for part in range(2):
                    vals = turned[low - j * SUB : high - j * SUB, :, part * block : (part + 1) * block]
                    out[low - first_row : high - first_row, part] = vals.astype(jnp.bfloat16)


def cross_piece(piece, freq_count, groups, slots, me, own, far, own_inv, far_lift, made):
    half, _, seg, block = own.shape
    n_far = len(far)
    last = (piece + 1) * SUB == half
    slots = [slot for slot in slots if slot[3] == "all" or (slot[3] == "late") == last]
    counts = {"all": half, "early": half - SUB, "late": SUB}
    places = [0 if slot[3] == "late" else piece for slot in slots]
    spots = [n for n, slot in enumerate(slots) if slot in made]
    flat = pl.pallas_call(
        functools.partial(cross_kernel, piece, freq_count, groups, slots, len(spots), n_far),
        grid=(1,),
        in_specs=[
            pl.BlockSpec(memory_space=pltpu.SMEM),
            pl.BlockSpec((SUB, 2, seg, block), lambda i: (piece, 0, 0, 0)),
            pl.BlockSpec((block, half), lambda i: (0, 0)),
            pl.BlockSpec((1, block), lambda i: (0, 0)),
        ]
        + [pl.BlockSpec(x.shape, lambda i: (0, 0, 0, 0)) for x in far]
        + [pl.BlockSpec(memory_space=pl.ANY)] * len(spots),
        out_specs=[
            pl.BlockSpec((slot[2], 2, SUB, block), functools.partial(lambda at, i: (0, 0, at, 0), at))
            for slot, at in zip(slots, places)
        ],
        out_shape=[jax.ShapeDtypeStruct((slot[2], 2, counts[slot[3]], block), jnp.bfloat16) for slot in slots],
        scratch_shapes=[pltpu.VMEM((2, SUB, block, block), jnp.bfloat16)] * 2,
        input_output_aliases={4 + n_far + i: n for i, n in enumerate(spots)},
        compiler_params=pltpu.CompilerParams(vmem_limit_bytes=VMEM_BYTES),
        cost_estimate=pl.CostEstimate(
            flops=SUB * 8 * seg * block * block, bytes_accessed=SUB * 16 * seg * block, transcendentals=0
        ),
        name="cross_piece",
    )(me, own, own_inv, far_lift, *far, *[made[slots[n]] for n in spots])
    return {**made, **dict(zip(slots, flat))}


def lag_kernel(sources, rows, group, n_given, n_held, to_output, lag_ref, back_ref, *refs):
    n_pieces = sum(len(places) for places in sources)
    pieces, given = refs[:n_pieces], refs[n_pieces : n_pieces + n_given]
    out_ref, lag_scr, norm_scr, *rest = refs[n_pieces + n_given + n_held :]
    block = pieces[0].shape[3]
    width = AT_ONCE * block
    row_ref = rest[0] if to_output else out_ref
    first = SUB - rows if to_output else 0

    def column(r):
        parts, at = [], 0
        for places in sources:
            for part in range(2):
                parts += [piece[place + r, part] for piece, place in zip(pieces[at:], places)]
            at += len(places)
        return jnp.concatenate(parts, axis=0)

    for r in range(0, rows, AT_ONCE):
        cols = jnp.concatenate([column(r + k) for k in range(AT_ONCE)], axis=1)
        lag_scr[...] = jnp.dot(lag_ref[...], cols, preferred_element_type=jnp.float32)
        total = jnp.zeros((8, width), jnp.float32)
        for at in range(0, LAGS, SLICE):
            lag_re, lag_im = lag_scr[at : at + SLICE], lag_scr[LAGS + at : LAGS + at + SLICE]
            energy = lag_re * lag_re + lag_im * lag_im
            lag_scr[LAGS + at : LAGS + at + SLICE] = energy
            total += jnp.sum(energy.reshape(SLICE // 8, 8, width), axis=0)
        floor = (0.25 / LAGS) * jnp.sum(total, axis=0, keepdims=True) + 1e-05
        for at in range(0, LAGS, SLICE):
            scale = lax.rsqrt(lag_scr[LAGS + at : LAGS + at + SLICE] + floor)
            norm_scr[at : at + SLICE] = (lag_scr[at : at + SLICE] * scale).astype(jnp.bfloat16)
        lag_scr[: 2 * F] = jnp.dot(back_ref[...], norm_scr[...], preferred_element_type=jnp.float32)
        for at in range(0, 2 * F, SLICE):
            back = (lag_scr[at : at + SLICE] * (1.0 / math.sqrt(LAGS))).astype(jnp.bfloat16)
            for k in range(AT_ONCE):
                row_ref[first + r + k, at : at + SLICE] = back[:, k * block : (k + 1) * block]
    if to_output:
        _, bins_ref, sems = rest
        matrix = interleave()
        copies = []
        chunk = 2 * F // PARTS
        for at in range(0, 2 * F, 2 * SUB):
            whole = [x[:, at : at + 2 * SUB] for x in given] + [row_ref[first:, at : at + 2 * SUB]]
            whole = jnp.concatenate(whole, axis=0)
            turned = turned_rows(matrix, whole[:, :SUB], whole[:, SUB:])
            for n in range(2):
                bins = turned[:, :, n * block : (n + 1) * block]
                bins_ref[at + n * SUB : at + (n + 1) * SUB] = bins.astype(jnp.bfloat16)
            if (at + 2 * SUB) % chunk == 0:
                start = at + 2 * SUB - chunk
                there = out_ref.at[0, start // F, pl.ds(start % F, chunk), pl.ds(group * SUB, SUB)]
                copies.append(pltpu.make_async_copy(bins_ref.at[pl.ds(start, chunk)], there, sems.at[start // chunk]))
                copies[-1].start()
        for copy in copies:
            copy.wait()


def lag_group(rows, group, groups, lag_table, back_table, sources, given, before, to_output=True):
    pieces = [piece for source in sources for piece, _ in source]
    places = [[place for _, place in source] for source in sources]
    block = pieces[0].shape[3]
    vmem, scratch = pl.BlockSpec(memory_space=pltpu.VMEM), [
        pltpu.VMEM((2 * LAGS, AT_ONCE * block), jnp.float32),
        pltpu.VMEM((LAGS, AT_ONCE * block), jnp.bfloat16),
    ]
    if to_output:
        out_spec = pl.BlockSpec(memory_space=pltpu.HBM)
        out_shape = jax.ShapeDtypeStruct((1, 2, F, SUB * groups, block), jnp.bfloat16)
        scratch += [
            pltpu.VMEM((SUB, 2 * F, block), jnp.bfloat16),
            pltpu.VMEM((2 * F, SUB, block), jnp.bfloat16),
            pltpu.SemaphoreType.DMA((PARTS,)),
        ]
    else:
        out_spec = vmem
        out_shape = jax.ShapeDtypeStruct((rows, 2 * F, block), jnp.bfloat16)
    return pl.pallas_call(
        functools.partial(lag_kernel, places, rows, group, len(given), len(before), to_output),
        in_specs=[vmem] * (2 + len(pieces) + len(given)) + [pl.BlockSpec(memory_space=pltpu.HBM)] * len(before),
        out_specs=out_spec,
        out_shape=out_shape,
        scratch_shapes=scratch,
        input_output_aliases={2 + len(pieces) + len(given): 0} if before else {},
        compiler_params=pltpu.CompilerParams(vmem_limit_bytes=VMEM_BYTES),
        cost_estimate=NO_COST,
        name="lag_group",
    )(lag_table, back_table, *pieces, *given, *before)


def shards(spectra, seg_mask):
    tile_count, freq_count = lax.axis_size("tile"), lax.axis_size("freq")
    half_axis = tile_count // 2
    _, seg, band, block = spectra.shape
    half = band // 2
    n_sub = half // SUB
    groups = block // freq_count // SUB
    me = lax.axis_index("freq")
    side = lax.axis_index("tile") // half_axis
    keep_from, send_from = side * half, (1 - side) * half

    across = [(t, (t + half_axis) % tile_count) for t in range(tile_count)]

    def moved(block, d, distance):
        route = []
        for h in range(freq_count):
            for t in range(tile_count):
                route.append((h * tile_count + t, (h + d) % freq_count * tile_count + (t + distance) % tile_count))
        return lax.ppermute(block, ("freq", "tile"), route)

    keep_sub, send_sub = side * n_sub, (1 - side) * n_sub
    *pieces, power = prepare(spectra, seg_mask, send_sub, 1, (SHORT, SUB - SHORT))
    send_power, counts = [power], [2]
    if n_sub > 1:
        piece, power = prepare(spectra, seg_mask, send_sub + 1, 1, (SUB,))
        pieces.append(piece)
        send_power.append(power)
        counts.append(1)
    far = [lax.ppermute(piece, "tile", across) for piece in pieces]
    rest, far[0] = lax.optimization_barrier((spectra, far[0]))
    pieces = []
    for i in range(2, n_sub):
        *both, power = prepare(rest, seg_mask, send_sub + i, 1, (SUB // 2, SUB // 2))
        rest, both = lax.optimization_barrier((rest, both))
        pieces += both
        send_power.append(power)
        counts.append(2)
    own, own_power = prepare(rest, seg_mask, keep_sub, n_sub, (half,))
    send_power = jnp.concatenate(send_power, axis=0)

    total = lax.psum(jnp.sum(own_power, axis=0) + jnp.sum(send_power, axis=0), "freq")
    lift = WATER * (total / F)[None, :]
    own_inv = (1.0 / ((own_power + lift) * seg)).T
    local = jnp.arange(half, dtype=jnp.int32)
    lag_cols = []
    for mine in (True, False):
        for d in range(freq_count):
            freqs = (me - d) % freq_count * band + (keep_from if mine else send_from) + local
            cos_tab, sin_tab = dft_tables(freqs)
            lag_cols.append(jnp.concatenate([cos_tab, sin_tab], axis=0))
            lag_cols.append(jnp.concatenate([-sin_tab, cos_tab], axis=0))
    lag_table = jnp.concatenate(lag_cols, axis=1)
    cos_tab, sin_tab = dft_tables(jnp.arange(F, dtype=jnp.int32))
    back_table = jnp.concatenate([cos_tab, -sin_tab], axis=1).T

    far_total = None
    for i, piece in enumerate(pieces):
        if i == 0:
            shape = piece.shape
            piece, terms, own_inv, lag_table, back_table = lax.optimization_barrier(
                (piece, exact_terms(total), own_inv, lag_table, back_table)
            )
            piece = jnp.concatenate([piece.reshape(-1, block), terms], axis=0)
        if i >= 2:
            piece, far[i - 1] = lax.optimization_barrier((piece, far[i - 1]))
        got = lax.ppermute(piece, "tile", across)
        if i == 0:
            far_total = jnp.sum(got[-SUB:].astype(jnp.float32), axis=0)
            got = got[:-SUB].reshape(shape)
        far.append(got)
    if far_total is None:
        far_total = lax.ppermute(total, "tile", across)
    far_lift = WATER * (far_total / F)[None, :]

    n_split = groups // 2 if n_sub > 1 else 0
    full = groups * SUB
    early_rows = n_split * SUB
    first_parts = [(j * SUB, SUB, "early") for j in range(n_split)]
    late_parts = [(0, early_rows, "late")] if n_split else []
    own_rest = [(early_rows, full - early_rows, "all")]
    halves = [(row, SUB // 2, "all") for row in range(early_rows, full, SUB // 2)] if groups > 1 else own_rest
    places = [first_parts + late_parts + (own_rest if k < freq_count else halves) for k in range(2 * freq_count)]
    slots = [(k, *place) for k in range(2 * freq_count) for place in places[k]]
    me_arr = me.astype(jnp.int32).reshape(1)
    ready = max(sum(counts[:-1]) - 1, 0)
    far[ready], lag_table, back_table, own_inv, far_lift, own = lax.optimization_barrier(
        (far[ready], lag_table, back_table, own_inv, far_lift, own)
    )
    far = [far[sum(counts[:i]) : sum(counts[: i + 1])] for i in range(n_sub)]
    made = {}
    for i in range(n_sub):
        made = cross_piece(i, freq_count, groups, slots, me_arr, own, far[i], own_inv, far_lift, made)

    arrived = {}

    def send(place, wait_for=None):
        kinds = [k for k in range(1, 2 * freq_count) if place in places[k]]
        outgoing = [made[(k, *place)] for k in kinds]
        if wait_for is not None:
            outgoing, arrived[wait_for] = lax.optimization_barrier((outgoing, arrived[wait_for]))
        if wait_for is not None and place == halves[-1]:
            outgoing, state["out"] = lax.optimization_barrier((outgoing, state["out"]))
        moves = [moved(x, k % freq_count, half_axis * (k // freq_count)) for k, x in zip(kinds, outgoing)]
        arrived[place] = dict(zip(kinds, moves))

    def transform(place):
        first_row, rows, _ = place
        sources = []
        for k in range(2 * freq_count):
            holds = [hold for hold in places[k] if hold[0] <= first_row < hold[0] + hold[1]]
            sources.append([(arrived[hold][k] if k else made[(0, *hold)], first_row - hold[0]) for hold in holds])
        group, ends = first_row // SUB, (first_row + rows) % SUB == 0
        before = state["out"] if ends else []
        done = lag_group(rows, group, groups, lag_table, back_table, sources, state["given"], before, to_output=ends)
        state["given" if not ends else "out"] = [done]
        if ends:
            state["given"] = []

    state = {"given": [], "out": []}
    for place in first_parts + late_parts:
        send(place)
    if own_rest != halves:
        send(own_rest[0])
    chain = first_parts + late_parts + halves
    for n, place in enumerate(halves, start=len(chain) - len(halves)):
        if place == halves[-1]:
            for part in first_parts:
                transform(part)
        send(place, chain[n - 2] if n >= 2 else None)
    for place in halves:
        if place in halves[-2:-1]:
            arrived[place], state["out"] = lax.optimization_barrier((arrived[place], state["out"]))
        transform(place)
    out = state["out"]
    return out[0]


def solution(mesh):
    placed = (P(None, None, "freq", "tile"), P(None, "tile"))
    return jax.shard_map(
        shards,
        mesh=mesh,
        in_specs=placed,
        out_specs=P("tile", None, None, "freq", None),
        check_vma=False,
    )
```

```python
import functools
import math

import jax
import jax.numpy as jnp
from jax import lax
from jax.experimental import pallas as pl
from jax.experimental.pallas import tpu as pltpu
from jax.sharding import PartitionSpec as P

F = 256
LAGS = 512
WATER = 0.05
SUB = 16
SHORT = 4
AT_ONCE = 8
PARTS = 4
SLICE = 16
VMEM_BYTES = 28 * 2**20
PREPARE_BYTES = 48 * 2**20
NO_COST = pl.CostEstimate(flops=0, bytes_accessed=0, transcendentals=0)


def dft_tables(freq_index):
    lag_index = jnp.arange(LAGS, dtype=jnp.int32)[:, None]
    phase = (lag_index * freq_index[None, :] % LAGS).astype(jnp.float32) * (2.0 * math.pi / LAGS)
    return jnp.cos(phase).astype(jnp.bfloat16), jnp.sin(phase).astype(jnp.bfloat16)


def rounded(x):
    return x.astype(jnp.bfloat16).astype(jnp.float32)


def interleave():
    row = lax.broadcasted_iota(jnp.int32, (SUB * SUB, SUB * SUB), 0)
    col = lax.broadcasted_iota(jnp.int32, (SUB * SUB, SUB * SUB), 1)
    return jnp.where(col == row % SUB * SUB + row // SUB, 1.0, 0.0).astype(jnp.bfloat16)


def turned_rows(matrix, left, right):
    lanes = left.shape[2]
    both = jnp.concatenate([left.reshape(SUB * SUB, lanes), right.reshape(SUB * SUB, lanes)], axis=1)
    return jnp.dot(matrix, both, preferred_element_type=jnp.float32).reshape(SUB, SUB, 2 * lanes)


def prepare_kernel(at_ref, x_ref, mask_ref, *outs):
    parts, power_ref = outs[:-1], outs[-1]
    seg, lanes = mask_ref.shape
    matrix = interleave()
    total = jnp.zeros((SUB, 8, lanes), jnp.float32)
    for s in range(0, seg, SUB):
        total += prepare_rows(x_ref, mask_ref, s, matrix, parts)
    power_ref[...] = jnp.sum(total, axis=1) * (1.0 / seg) + 1e-05


def prepare(spectra, seg_mask, first, steps, counts):
    _, seg, _, block = spectra.shape
    assert sum(counts) == steps * SUB and (steps == 1 or len(counts) == 1)
    out_specs = [pl.BlockSpec((min(count, SUB), 2, seg, block), lambda i, at: (i, 0, 0, 0)) for count in counts]
    out_shape = [jax.ShapeDtypeStruct((count, 2, seg, block), jnp.bfloat16) for count in counts]
    if steps > 1:
        out_shape = [pltpu.HBM(x.shape, x.dtype) for x in out_shape]
    return pl.pallas_call(
        prepare_kernel,
        grid_spec=pltpu.PrefetchScalarGridSpec(
            num_scalar_prefetch=1,
            grid=(steps,),
            in_specs=[
                pl.BlockSpec((2, seg, SUB, block), lambda i, at: (0, 0, at[0] + i, 0)),
                pl.BlockSpec((seg, block), lambda i, at: (0, 0)),
            ],
            out_specs=out_specs + [pl.BlockSpec((SUB, block), lambda i, at: (i, 0))],
        ),
        out_shape=out_shape + [jax.ShapeDtypeStruct((steps * SUB, block), jnp.float32)],
        compiler_params=pltpu.CompilerParams(vmem_limit_bytes=PREPARE_BYTES),
        cost_estimate=NO_COST,
        name="prepare",
    )(first.astype(jnp.int32).reshape(1), spectra, seg_mask)


def prepare_rows(x_ref, mask_ref, s, matrix, parts):
    lanes = mask_ref.shape[1]
    mask = mask_ref[s : s + SUB].astype(jnp.float32)[None]
    turned = turned_rows(matrix, x_ref[0, s : s + SUB], x_ref[1, s : s + SUB])
    total = 0.0
    for part in range(2):
        val = turned[:, :, part * lanes : (part + 1) * lanes] * mask
        square = val * val
        total += square[:, :8] + square[:, 8:]
        at = 0
        for out in parts:
            count = out.shape[0]
            out[:, part, s : s + SUB] = val[at : at + count].astype(jnp.bfloat16)
            at += count
    return total


def prepare_piece_kernel(at_ref, x_hbm, mask_hbm, *refs):
    parts, power_ref, x_ref, mask_ref, sems = refs[:-4], refs[-4], refs[-3], refs[-2], refs[-1]
    seg, lanes = mask_ref.shape
    freqs = pl.ds(pl.multiple_of(at_ref[0] * SUB, SUB), SUB)
    chunk = seg // PARTS
    copies = []
    for n in range(PARTS):
        rows = pl.ds(n * chunk, chunk)
        copies.append(
            [
                pltpu.make_async_copy(mask_hbm.at[rows], mask_ref.at[rows], sems.at[2 * n]),
                pltpu.make_async_copy(x_hbm.at[:, rows, freqs], x_ref.at[:, rows], sems.at[2 * n + 1]),
            ]
        )
        for copy in copies[-1]:
            copy.start()
    matrix = interleave()
    total = jnp.zeros((SUB, 8, lanes), jnp.float32)
    for n in range(PARTS):
        for copy in copies[n]:
            copy.wait()
        for s in range(n * chunk, (n + 1) * chunk, SUB):
            total += prepare_rows(x_ref, mask_ref, s, matrix, parts)
    power_ref[...] = jnp.sum(total, axis=1) * (1.0 / seg) + 1e-05


def prepare_first(spectra, seg_mask, first, counts):
    _, seg, _, block = spectra.shape
    vmem = pl.BlockSpec(memory_space=pltpu.VMEM)
    return pl.pallas_call(
        prepare_piece_kernel,
        in_specs=[pl.BlockSpec(memory_space=pltpu.SMEM)] + [pl.BlockSpec(memory_space=pltpu.HBM)] * 2,
        out_specs=[vmem] * (len(counts) + 1),
        out_shape=[jax.ShapeDtypeStruct((count, 2, seg, block), jnp.bfloat16) for count in counts]
        + [jax.ShapeDtypeStruct((SUB, block), jnp.float32)],
        scratch_shapes=[
            pltpu.VMEM((2, seg, SUB, block), jnp.bfloat16),
            pltpu.VMEM((seg, block), jnp.int32),
            pltpu.SemaphoreType.DMA((2 * PARTS,)),
        ],
        compiler_params=pltpu.CompilerParams(vmem_limit_bytes=PREPARE_BYTES),
        cost_estimate=NO_COST,
        name="prepare_first",
    )(first.astype(jnp.int32).reshape(1), spectra, seg_mask)


def exact_terms(x):
    terms, rest = [], x
    for _ in range(3):
        terms.append(lax.reduce_precision(rest, 8, 7))
        rest = rest - terms[-1]
    return jnp.pad(jnp.stack(terms).astype(jnp.bfloat16), ((0, SUB - 3), (0, 0)))


def cross_kernel(piece, freq_count, groups, slots, held, n_far, me_ref, own_ref, own_inv_ref, far_lift_ref, *refs):
    far_refs, outs, (own_scr, far_scr) = refs[:n_far], refs[n_far + held : -2], refs[-2:]
    seg = own_ref.shape[2]
    block = own_ref.shape[3]
    far_rows = [(far_ref, k) for far_ref in far_refs for k in range(far_ref.shape[0])]
    for f in range(SUB):
        own = own_ref[f].reshape(2 * seg, block)
        far_ref, k = far_rows[f]
        far_re, far_im = far_ref[k, 0], far_ref[k, 1]
        cols = jnp.concatenate(
            [jnp.concatenate([far_re, far_im], axis=0), jnp.concatenate([far_im, -far_re], axis=0)], axis=1
        )
        cross = lax.dot_general(own, cols, (((0,), (0,)), ((), ())), preferred_element_type=jnp.float32)
        at = piece * SUB + f
        own_inv = own_inv_ref[:, at : at + 1]
        square = jnp.square(far_re.astype(jnp.float32)) + jnp.square(far_im.astype(jnp.float32))
        far_power = jnp.sum(square, axis=0, keepdims=True) * (1.0 / seg) + 1e-05
        far_inv = 1.0 / ((far_power + far_lift_ref[...]) * seg)
        for part in range(2):
            val = cross[:, part * block : (part + 1) * block]
            sym = 0.5 * (rounded(val * own_inv) + rounded(val * far_inv))
            own_scr[part, f] = sym.astype(jnp.bfloat16)
            turned = jnp.transpose(sym if part == 0 else -sym)
            far_scr[part, f] = turned.astype(jnp.bfloat16)
    me = me_ref[0]
    matrix = interleave()
    for k in range(2 * freq_count):
        scr = own_scr if k < freq_count else far_scr
        for j in range(groups):
            first = (lax.rem(me + k % freq_count, freq_count) * groups + j) * SUB
            rows = pl.ds(pl.multiple_of(first, SUB), SUB)
            turned = turned_rows(matrix, scr[0, :, rows, :], scr[1, :, rows, :])
            for out, (kind, first_row, count, _) in zip(outs, slots):
                low, high = max(first_row, j * SUB), min(first_row + count, (j + 1) * SUB)
                if kind != k or low >= high:
                    continue
                for part in range(2):
                    vals = turned[low - j * SUB : high - j * SUB, :, part * block : (part + 1) * block]
                    out[low - first_row : high - first_row, part] = vals.astype(jnp.bfloat16)


def cross_piece(piece, freq_count, groups, slots, me, own, far, own_inv, far_lift, made):
    half, _, seg, block = own.shape
    n_far = len(far)
    last = (piece + 1) * SUB == half
    slots = [slot for slot in slots if slot[3] == "all" or (slot[3] == "late") == last]
    counts = {"all": half, "early": half - SUB, "late": SUB}
    places = [0 if slot[3] == "late" else piece for slot in slots]
    spots = [n for n, slot in enumerate(slots) if slot in made]
    flat = pl.pallas_call(
        functools.partial(cross_kernel, piece, freq_count, groups, slots, len(spots), n_far),
        grid=(1,),
        in_specs=[
            pl.BlockSpec(memory_space=pltpu.SMEM),
            pl.BlockSpec((SUB, 2, seg, block), lambda i: (piece, 0, 0, 0)),
            pl.BlockSpec((block, half), lambda i: (0, 0)),
            pl.BlockSpec((1, block), lambda i: (0, 0)),
        ]
        + [pl.BlockSpec(x.shape, lambda i: (0, 0, 0, 0)) for x in far]
        + [pl.BlockSpec(memory_space=pl.ANY)] * len(spots),
        out_specs=[
            pl.BlockSpec((slot[2], 2, SUB, block), functools.partial(lambda at, i: (0, 0, at, 0), at))
            for slot, at in zip(slots, places)
        ],
        out_shape=[jax.ShapeDtypeStruct((slot[2], 2, counts[slot[3]], block), jnp.bfloat16) for slot in slots],
        scratch_shapes=[pltpu.VMEM((2, SUB, block, block), jnp.bfloat16)] * 2,
        input_output_aliases={4 + n_far + i: n for i, n in enumerate(spots)},
        compiler_params=pltpu.CompilerParams(vmem_limit_bytes=VMEM_BYTES),
        cost_estimate=pl.CostEstimate(
            flops=SUB * 8 * seg * block * block, bytes_accessed=SUB * 16 * seg * block, transcendentals=0
        ),
        name="cross_piece",
    )(me, own, own_inv, far_lift, *far, *[made[slots[n]] for n in spots])
    return {**made, **dict(zip(slots, flat))}


def lag_kernel(sources, rows, group, n_given, n_held, to_output, lag_ref, back_ref, *refs):
    n_pieces = sum(len(places) for places in sources)
    pieces, given = refs[:n_pieces], refs[n_pieces : n_pieces + n_given]
    out_ref, lag_scr, norm_scr, *rest = refs[n_pieces + n_given + n_held :]
    block = pieces[0].shape[3]
    width = AT_ONCE * block
    row_ref = rest[0] if to_output else out_ref
    first = SUB - rows if to_output else 0

    def column(r):
        parts, at = [], 0
        for places in sources:
            for part in range(2):
                parts += [piece[place + r, part] for piece, place in zip(pieces[at:], places)]
            at += len(places)
        return jnp.concatenate(parts, axis=0)

    for r in range(0, rows, AT_ONCE):
        cols = jnp.concatenate([column(r + k) for k in range(AT_ONCE)], axis=1)
        lag_scr[...] = jnp.dot(lag_ref[...], cols, preferred_element_type=jnp.float32)
        total = jnp.zeros((8, width), jnp.float32)
        for at in range(0, LAGS, SLICE):
            lag_re, lag_im = lag_scr[at : at + SLICE], lag_scr[LAGS + at : LAGS + at + SLICE]
            energy = lag_re * lag_re + lag_im * lag_im
            lag_scr[LAGS + at : LAGS + at + SLICE] = energy
            total += jnp.sum(energy.reshape(SLICE // 8, 8, width), axis=0)
        floor = (0.25 / LAGS) * jnp.sum(total, axis=0, keepdims=True) + 1e-05
        for at in range(0, LAGS, SLICE):
            scale = lax.rsqrt(lag_scr[LAGS + at : LAGS + at + SLICE] + floor)
            norm_scr[at : at + SLICE] = (lag_scr[at : at + SLICE] * scale).astype(jnp.bfloat16)
        lag_scr[: 2 * F] = jnp.dot(back_ref[...], norm_scr[...], preferred_element_type=jnp.float32)
        for at in range(0, 2 * F, SLICE):
            back = (lag_scr[at : at + SLICE] * (1.0 / math.sqrt(LAGS))).astype(jnp.bfloat16)
            for k in range(AT_ONCE):
                row_ref[first + r + k, at : at + SLICE] = back[:, k * block : (k + 1) * block]
    if to_output:
        _, bins_ref, sems = rest
        matrix = interleave()
        copies = []
        chunk = 2 * F // PARTS
        for at in range(0, 2 * F, 2 * SUB):
            whole = [x[:, at : at + 2 * SUB] for x in given] + [row_ref[first:, at : at + 2 * SUB]]
            whole = jnp.concatenate(whole, axis=0)
            turned = turned_rows(matrix, whole[:, :SUB], whole[:, SUB:])
            for n in range(2):
                bins = turned[:, :, n * block : (n + 1) * block]
                bins_ref[at + n * SUB : at + (n + 1) * SUB] = bins.astype(jnp.bfloat16)
            if (at + 2 * SUB) % chunk == 0:
                start = at + 2 * SUB - chunk
                there = out_ref.at[0, start // F, pl.ds(start % F, chunk), pl.ds(group * SUB, SUB)]
                copies.append(pltpu.make_async_copy(bins_ref.at[pl.ds(start, chunk)], there, sems.at[start // chunk]))
                copies[-1].start()
        for copy in copies:
            copy.wait()


def lag_group(rows, group, groups, lag_table, back_table, sources, given, before, to_output=True):
    pieces = [piece for source in sources for piece, _ in source]
    places = [[place for _, place in source] for source in sources]
    block = pieces[0].shape[3]
    vmem, scratch = pl.BlockSpec(memory_space=pltpu.VMEM), [
        pltpu.VMEM((2 * LAGS, AT_ONCE * block), jnp.float32),
        pltpu.VMEM((LAGS, AT_ONCE * block), jnp.bfloat16),
    ]
    if to_output:
        out_spec = pl.BlockSpec(memory_space=pltpu.HBM)
        out_shape = jax.ShapeDtypeStruct((1, 2, F, SUB * groups, block), jnp.bfloat16)
        scratch += [
            pltpu.VMEM((SUB, 2 * F, block), jnp.bfloat16),
            pltpu.VMEM((2 * F, SUB, block), jnp.bfloat16),
            pltpu.SemaphoreType.DMA((PARTS,)),
        ]
    else:
        out_spec = vmem
        out_shape = jax.ShapeDtypeStruct((rows, 2 * F, block), jnp.bfloat16)
    return pl.pallas_call(
        functools.partial(lag_kernel, places, rows, group, len(given), len(before), to_output),
        in_specs=[vmem] * (2 + len(pieces) + len(given)) + [pl.BlockSpec(memory_space=pltpu.HBM)] * len(before),
        out_specs=out_spec,
        out_shape=out_shape,
        scratch_shapes=scratch,
        input_output_aliases={2 + len(pieces) + len(given): 0} if before else {},
        compiler_params=pltpu.CompilerParams(vmem_limit_bytes=VMEM_BYTES),
        cost_estimate=NO_COST,
        name="lag_group",
    )(lag_table, back_table, *pieces, *given, *before)


def shards(spectra, seg_mask):
    tile_count, freq_count = lax.axis_size("tile"), lax.axis_size("freq")
    half_axis = tile_count // 2
    _, seg, band, block = spectra.shape
    half = band // 2
    n_sub = half // SUB
    groups = block // freq_count // SUB
    me = lax.axis_index("freq")
    side = lax.axis_index("tile") // half_axis
    keep_from, send_from = side * half, (1 - side) * half

    across = [(t, (t + half_axis) % tile_count) for t in range(tile_count)]

    def moved(block, d, distance):
        route = []
        for h in range(freq_count):
            for t in range(tile_count):
                route.append((h * tile_count + t, (h + d) % freq_count * tile_count + (t + distance) % tile_count))
        return lax.ppermute(block, ("freq", "tile"), route)

    keep_sub, send_sub = side * n_sub, (1 - side) * n_sub
    *pieces, power = prepare_first(spectra, seg_mask, send_sub, (SHORT, SUB - SHORT))
    send_power, counts = [power], [2]
    if n_sub > 1:
        piece, power = prepare(spectra, seg_mask, send_sub + 1, 1, (SUB,))
        pieces.append(piece)
        send_power.append(power)
        counts.append(1)
    far = [lax.ppermute(piece, "tile", across) for piece in pieces]
    rest, far[0] = lax.optimization_barrier((spectra, far[0]))
    pieces = []
    for i in range(2, n_sub):
        *both, power = prepare(rest, seg_mask, send_sub + i, 1, (SUB // 2, SUB // 2))
        rest, both = lax.optimization_barrier((rest, both))
        pieces += both
        send_power.append(power)
        counts.append(2)
    own, own_power = prepare(rest, seg_mask, keep_sub, n_sub, (half,))
    send_power = jnp.concatenate(send_power, axis=0)

    total = lax.psum(jnp.sum(own_power, axis=0) + jnp.sum(send_power, axis=0), "freq")
    lift = WATER * (total / F)[None, :]
    own_inv = (1.0 / ((own_power + lift) * seg)).T
    local = jnp.arange(half, dtype=jnp.int32)
    lag_cols = []
    for mine in (True, False):
        for d in range(freq_count):
            freqs = (me - d) % freq_count * band + (keep_from if mine else send_from) + local
            cos_tab, sin_tab = dft_tables(freqs)
            lag_cols.append(jnp.concatenate([cos_tab, sin_tab], axis=0))
            lag_cols.append(jnp.concatenate([-sin_tab, cos_tab], axis=0))
    lag_table = jnp.concatenate(lag_cols, axis=1)
    cos_tab, sin_tab = dft_tables(jnp.arange(F, dtype=jnp.int32))
    back_table = jnp.concatenate([cos_tab, -sin_tab], axis=1).T

    far_total = None
    for i, piece in enumerate(pieces):
        if i == 0:
            shape = piece.shape
            piece, terms, own_inv, lag_table, back_table = lax.optimization_barrier(
                (piece, exact_terms(total), own_inv, lag_table, back_table)
            )
            piece = jnp.concatenate([piece.reshape(-1, block), terms], axis=0)
        if i >= 2:
            piece, far[i - 1] = lax.optimization_barrier((piece, far[i - 1]))
        got = lax.ppermute(piece, "tile", across)
        if i == 0:
            far_total = jnp.sum(got[-SUB:].astype(jnp.float32), axis=0)
            got = got[:-SUB].reshape(shape)
        far.append(got)
    if far_total is None:
        far_total = lax.ppermute(total, "tile", across)
    far_lift = WATER * (far_total / F)[None, :]

    n_split = groups // 2 if n_sub > 1 else 0
    full = groups * SUB
    early_rows = n_split * SUB
    first_parts = [(j * SUB, SUB, "early") for j in range(n_split)]
    late_parts = [(0, early_rows, "late")] if n_split else []
    own_rest = [(early_rows, full - early_rows, "all")]
    halves = [(row, SUB // 2, "all") for row in range(early_rows, full, SUB // 2)] if groups > 1 else own_rest
    places = [first_parts + late_parts + (own_rest if k < freq_count else halves) for k in range(2 * freq_count)]
    slots = [(k, *place) for k in range(2 * freq_count) for place in places[k]]
    me_arr = me.astype(jnp.int32).reshape(1)
    ready = max(sum(counts[:-1]) - 1, 0)
    far[ready], lag_table, back_table, own_inv, far_lift, own = lax.optimization_barrier(
        (far[ready], lag_table, back_table, own_inv, far_lift, own)
    )
    far = [far[sum(counts[:i]) : sum(counts[: i + 1])] for i in range(n_sub)]
    made = {}
    for i in range(n_sub):
        made = cross_piece(i, freq_count, groups, slots, me_arr, own, far[i], own_inv, far_lift, made)

    arrived = {}

    def send(place, wait_for=None):
        kinds = [k for k in range(1, 2 * freq_count) if place in places[k]]
        outgoing = [made[(k, *place)] for k in kinds]
        if wait_for is not None:
            outgoing, arrived[wait_for] = lax.optimization_barrier((outgoing, arrived[wait_for]))
        if wait_for is not None and place == halves[-1]:
            outgoing, state["out"] = lax.optimization_barrier((outgoing, state["out"]))
        moves = [moved(x, k % freq_count, half_axis * (k // freq_count)) for k, x in zip(kinds, outgoing)]
        arrived[place] = dict(zip(kinds, moves))

    def transform(place):
        first_row, rows, _ = place
        sources = []
        for k in range(2 * freq_count):
            holds = [hold for hold in places[k] if hold[0] <= first_row < hold[0] + hold[1]]
            sources.append([(arrived[hold][k] if k else made[(0, *hold)], first_row - hold[0]) for hold in holds])
        group, ends = first_row // SUB, (first_row + rows) % SUB == 0
        before = state["out"] if ends else []
        done = lag_group(rows, group, groups, lag_table, back_table, sources, state["given"], before, to_output=ends)
        state["given" if not ends else "out"] = [done]
        if ends:
            state["given"] = []

    state = {"given": [], "out": []}
    for place in first_parts + late_parts:
        send(place)
    if own_rest != halves:
        send(own_rest[0])
    chain = first_parts + late_parts + halves
    for n, place in enumerate(halves, start=len(chain) - len(halves)):
        if place == halves[-1]:
            for part in first_parts:
                transform(part)
        send(place, chain[n - 2] if n >= 2 else None)
    for place in halves:
        if place in halves[-2:-1]:
            arrived[place], state["out"] = lax.optimization_barrier((arrived[place], state["out"]))
        transform(place)
    out = state["out"]
    return out[0]


def solution(mesh):
    placed = (P(None, None, "freq", "tile"), P(None, "tile"))
    return jax.shard_map(
        shards,
        mesh=mesh,
        in_specs=placed,
        out_specs=P("tile", None, None, "freq", None),
        check_vma=False,
    )
```

```python
import functools
import math

import jax
import jax.numpy as jnp
from jax import lax
from jax.experimental import pallas as pl
from jax.experimental.pallas import tpu as pltpu
from jax.sharding import PartitionSpec as P

F = 256
LAGS = 512
WATER = 0.05
SUB = 16
SHORT = 4
AT_ONCE = 8
PARTS = 4
SLICE = 16
VMEM_BYTES = 28 * 2**20
PREPARE_BYTES = 46 * 2**20
NO_COST = pl.CostEstimate(flops=0, bytes_accessed=0, transcendentals=0)


def dft_tables(freq_index):
    lag_index = jnp.arange(LAGS, dtype=jnp.int32)[:, None]
    phase = (lag_index * freq_index[None, :] % LAGS).astype(jnp.float32) * (2.0 * math.pi / LAGS)
    return jnp.cos(phase).astype(jnp.bfloat16), jnp.sin(phase).astype(jnp.bfloat16)


def rounded(x):
    return x.astype(jnp.bfloat16).astype(jnp.float32)


def interleave():
    row = lax.broadcasted_iota(jnp.int32, (SUB * SUB, SUB * SUB), 0)
    col = lax.broadcasted_iota(jnp.int32, (SUB * SUB, SUB * SUB), 1)
    return jnp.where(col == row % SUB * SUB + row // SUB, 1.0, 0.0).astype(jnp.bfloat16)


def turned_rows(matrix, left, right):
    lanes = left.shape[2]
    both = jnp.concatenate([left.reshape(SUB * SUB, lanes), right.reshape(SUB * SUB, lanes)], axis=1)
    return jnp.dot(matrix, both, preferred_element_type=jnp.float32).reshape(SUB, SUB, 2 * lanes)


def prepare_kernel(at_ref, x_ref, mask_ref, *outs):
    parts, power_ref = outs[:-1], outs[-1]
    seg, lanes = mask_ref.shape
    matrix = interleave()
    total = jnp.zeros((SUB, 8, lanes), jnp.float32)
    for s in range(0, seg, SUB):
        mask = mask_ref[s : s + SUB].astype(jnp.float32)[None]
        turned = turned_rows(matrix, x_ref[0, s : s + SUB], x_ref[1, s : s + SUB])
        for part in range(2):
            val = turned[:, :, part * lanes : (part + 1) * lanes] * mask
            square = val * val
            total += square[:, :8] + square[:, 8:]
            at = 0
            for out in parts:
                count = out.shape[0]
                out[:, part, s : s + SUB] = val[at : at + count].astype(jnp.bfloat16)
                at += count
    power_ref[...] = jnp.sum(total, axis=1) * (1.0 / seg) + 1e-05


def prepare(spectra, seg_mask, first, steps, counts):
    _, seg, _, block = spectra.shape
    assert sum(counts) == steps * SUB and (steps == 1 or len(counts) == 1)
    out_specs = [pl.BlockSpec((min(count, SUB), 2, seg, block), lambda i, at: (i, 0, 0, 0)) for count in counts]
    out_shape = [jax.ShapeDtypeStruct((count, 2, seg, block), jnp.bfloat16) for count in counts]
    if steps > 1:
        out_shape = [pltpu.HBM(x.shape, x.dtype) for x in out_shape]
    return pl.pallas_call(
        prepare_kernel,
        grid_spec=pltpu.PrefetchScalarGridSpec(
            num_scalar_prefetch=1,
            grid=(steps,),
            in_specs=[
                pl.BlockSpec((2, seg, SUB, block), lambda i, at: (0, 0, at[0] + i, 0)),
                pl.BlockSpec((seg, block), lambda i, at: (0, 0)),
            ],
            out_specs=out_specs + [pl.BlockSpec((SUB, block), lambda i, at: (i, 0))],
        ),
        out_shape=out_shape + [jax.ShapeDtypeStruct((steps * SUB, block), jnp.float32)],
        compiler_params=pltpu.CompilerParams(vmem_limit_bytes=PREPARE_BYTES),
        cost_estimate=NO_COST,
        name="prepare",
    )(first.astype(jnp.int32).reshape(1), spectra, seg_mask)


def exact_terms(x):
    terms, rest = [], x
    for _ in range(3):
        terms.append(lax.reduce_precision(rest, 8, 7))
        rest = rest - terms[-1]
    return jnp.pad(jnp.stack(terms).astype(jnp.bfloat16), ((0, SUB - 3), (0, 0)))


def cross_kernel(piece, freq_count, groups, slots, held, n_far, me_ref, own_ref, own_inv_ref, far_lift_ref, *refs):
    far_refs, outs, (own_scr, far_scr) = refs[:n_far], refs[n_far + held : -2], refs[-2:]
    seg = own_ref.shape[2]
    block = own_ref.shape[3]
    far_rows = [(far_ref, k) for far_ref in far_refs for k in range(far_ref.shape[0])]
    for f in range(SUB):
        own = own_ref[f].reshape(2 * seg, block)
        far_ref, k = far_rows[f]
        far_re, far_im = far_ref[k, 0], far_ref[k, 1]
        cols = jnp.concatenate(
            [jnp.concatenate([far_re, far_im], axis=0), jnp.concatenate([far_im, -far_re], axis=0)], axis=1
        )
        cross = lax.dot_general(own, cols, (((0,), (0,)), ((), ())), preferred_element_type=jnp.float32)
        at = piece * SUB + f
        own_inv = own_inv_ref[:, at : at + 1]
        square = jnp.square(far_re.astype(jnp.float32)) + jnp.square(far_im.astype(jnp.float32))
        far_power = jnp.sum(square, axis=0, keepdims=True) * (1.0 / seg) + 1e-05
        far_inv = 1.0 / ((far_power + far_lift_ref[...]) * seg)
        for part in range(2):
            val = cross[:, part * block : (part + 1) * block]
            sym = 0.5 * (rounded(val * own_inv) + rounded(val * far_inv))
            own_scr[part, f] = sym.astype(jnp.bfloat16)
            turned = jnp.transpose(sym if part == 0 else -sym)
            far_scr[part, f] = turned.astype(jnp.bfloat16)
    me = me_ref[0]
    matrix = interleave()
    for k in range(2 * freq_count):
        scr = own_scr if k < freq_count else far_scr
        for j in range(groups):
            first = (lax.rem(me + k % freq_count, freq_count) * groups + j) * SUB
            rows = pl.ds(pl.multiple_of(first, SUB), SUB)
            turned = turned_rows(matrix, scr[0, :, rows, :], scr[1, :, rows, :])
            for out, (kind, first_row, count, _) in zip(outs, slots):
                low, high = max(first_row, j * SUB), min(first_row + count, (j + 1) * SUB)
                if kind != k or low >= high:
                    continue
                for part in range(2):
                    vals = turned[low - j * SUB : high - j * SUB, :, part * block : (part + 1) * block]
                    out[low - first_row : high - first_row, part] = vals.astype(jnp.bfloat16)


def cross_piece(piece, freq_count, groups, slots, me, own, far, own_inv, far_lift, made):
    half, _, seg, block = own.shape
    n_far = len(far)
    last = (piece + 1) * SUB == half
    slots = [slot for slot in slots if slot[3] == "all" or (slot[3] == "late") == last]
    counts = {"all": half, "early": half - SUB, "late": SUB}
    places = [0 if slot[3] == "late" else piece for slot in slots]
    spots = [n for n, slot in enumerate(slots) if slot in made]
    flat = pl.pallas_call(
        functools.partial(cross_kernel, piece, freq_count, groups, slots, len(spots), n_far),
        grid=(1,),
        in_specs=[
            pl.BlockSpec(memory_space=pltpu.SMEM),
            pl.BlockSpec((SUB, 2, seg, block), lambda i: (piece, 0, 0, 0)),
            pl.BlockSpec((block, half), lambda i: (0, 0)),
            pl.BlockSpec((1, block), lambda i: (0, 0)),
        ]
        + [pl.BlockSpec(x.shape, lambda i: (0, 0, 0, 0)) for x in far]
        + [pl.BlockSpec(memory_space=pl.ANY)] * len(spots),
        out_specs=[
            pl.BlockSpec((slot[2], 2, SUB, block), functools.partial(lambda at, i: (0, 0, at, 0), at))
            for slot, at in zip(slots, places)
        ],
        out_shape=[jax.ShapeDtypeStruct((slot[2], 2, counts[slot[3]], block), jnp.bfloat16) for slot in slots],
        scratch_shapes=[pltpu.VMEM((2, SUB, block, block), jnp.bfloat16)] * 2,
        input_output_aliases={4 + n_far + i: n for i, n in enumerate(spots)},
        compiler_params=pltpu.CompilerParams(vmem_limit_bytes=VMEM_BYTES),
        cost_estimate=pl.CostEstimate(
            flops=SUB * 8 * seg * block * block, bytes_accessed=SUB * 16 * seg * block, transcendentals=0
        ),
        name="cross_piece",
    )(me, own, own_inv, far_lift, *far, *[made[slots[n]] for n in spots])
    return {**made, **dict(zip(slots, flat))}


def lag_kernel(sources, rows, group, n_given, n_held, to_output, lag_ref, back_ref, *refs):
    n_pieces = sum(len(places) for places in sources)
    pieces, given = refs[:n_pieces], refs[n_pieces : n_pieces + n_given]
    out_ref, lag_scr, norm_scr, *rest = refs[n_pieces + n_given + n_held :]
    block = pieces[0].shape[3]
    width = AT_ONCE * block
    row_ref = rest[0] if to_output else out_ref
    first = SUB - rows if to_output else 0

    def column(r):
        parts, at = [], 0
        for places in sources:
            for part in range(2):
                parts += [piece[place + r, part] for piece, place in zip(pieces[at:], places)]
            at += len(places)
        return jnp.concatenate(parts, axis=0)

    for r in range(0, rows, AT_ONCE):
        cols = jnp.concatenate([column(r + k) for k in range(AT_ONCE)], axis=1)
        lag_scr[...] = jnp.dot(lag_ref[...], cols, preferred_element_type=jnp.float32)
        total = jnp.zeros((8, width), jnp.float32)
        for at in range(0, LAGS, SLICE):
            lag_re, lag_im = lag_scr[at : at + SLICE], lag_scr[LAGS + at : LAGS + at + SLICE]
            energy = lag_re * lag_re + lag_im * lag_im
            lag_scr[LAGS + at : LAGS + at + SLICE] = energy
            total += jnp.sum(energy.reshape(SLICE // 8, 8, width), axis=0)
        floor = (0.25 / LAGS) * jnp.sum(total, axis=0, keepdims=True) + 1e-05
        for at in range(0, LAGS, SLICE):
            scale = lax.rsqrt(lag_scr[LAGS + at : LAGS + at + SLICE] + floor)
            norm_scr[at : at + SLICE] = (lag_scr[at : at + SLICE] * scale).astype(jnp.bfloat16)
        lag_scr[: 2 * F] = jnp.dot(back_ref[...], norm_scr[...], preferred_element_type=jnp.float32)
        for at in range(0, 2 * F, SLICE):
            back = (lag_scr[at : at + SLICE] * (1.0 / math.sqrt(LAGS))).astype(jnp.bfloat16)
            for k in range(AT_ONCE):
                row_ref[first + r + k, at : at + SLICE] = back[:, k * block : (k + 1) * block]
    if to_output:
        _, bins_ref, sems = rest
        matrix = interleave()
        copies = []
        chunk = 2 * F // PARTS
        for at in range(0, 2 * F, 2 * SUB):
            whole = [x[:, at : at + 2 * SUB] for x in given] + [row_ref[first:, at : at + 2 * SUB]]
            whole = jnp.concatenate(whole, axis=0)
            turned = turned_rows(matrix, whole[:, :SUB], whole[:, SUB:])
            for n in range(2):
                bins = turned[:, :, n * block : (n + 1) * block]
                bins_ref[at + n * SUB : at + (n + 1) * SUB] = bins.astype(jnp.bfloat16)
            if (at + 2 * SUB) % chunk == 0:
                start = at + 2 * SUB - chunk
                there = out_ref.at[0, start // F, pl.ds(start % F, chunk), pl.ds(group * SUB, SUB)]
                copies.append(pltpu.make_async_copy(bins_ref.at[pl.ds(start, chunk)], there, sems.at[start // chunk]))
                copies[-1].start()
        for copy in copies:
            copy.wait()


def lag_group(rows, group, groups, lag_table, back_table, sources, given, before, to_output=True):
    pieces = [piece for source in sources for piece, _ in source]
    places = [[place for _, place in source] for source in sources]
    block = pieces[0].shape[3]
    vmem, scratch = pl.BlockSpec(memory_space=pltpu.VMEM), [
        pltpu.VMEM((2 * LAGS, AT_ONCE * block), jnp.float32),
        pltpu.VMEM((LAGS, AT_ONCE * block), jnp.bfloat16),
    ]
    if to_output:
        out_spec = pl.BlockSpec(memory_space=pltpu.HBM)
        out_shape = jax.ShapeDtypeStruct((1, 2, F, SUB * groups, block), jnp.bfloat16)
        scratch += [
            pltpu.VMEM((SUB, 2 * F, block), jnp.bfloat16),
            pltpu.VMEM((2 * F, SUB, block), jnp.bfloat16),
            pltpu.SemaphoreType.DMA((PARTS,)),
        ]
    else:
        out_spec = vmem
        out_shape = jax.ShapeDtypeStruct((rows, 2 * F, block), jnp.bfloat16)
    return pl.pallas_call(
        functools.partial(lag_kernel, places, rows, group, len(given), len(before), to_output),
        in_specs=[vmem] * (2 + len(pieces) + len(given)) + [pl.BlockSpec(memory_space=pltpu.HBM)] * len(before),
        out_specs=out_spec,
        out_shape=out_shape,
        scratch_shapes=scratch,
        input_output_aliases={2 + len(pieces) + len(given): 0} if before else {},
        compiler_params=pltpu.CompilerParams(vmem_limit_bytes=VMEM_BYTES),
        cost_estimate=NO_COST,
        name="lag_group",
    )(lag_table, back_table, *pieces, *given, *before)


def shards(spectra, seg_mask):
    tile_count, freq_count = lax.axis_size("tile"), lax.axis_size("freq")
    half_axis = tile_count // 2
    _, seg, band, block = spectra.shape
    half = band // 2
    n_sub = half // SUB
    groups = block // freq_count // SUB
    me = lax.axis_index("freq")
    side = lax.axis_index("tile") // half_axis
    keep_from, send_from = side * half, (1 - side) * half

    across = [(t, (t + half_axis) % tile_count) for t in range(tile_count)]

    def moved(block, d, distance):
        route = []
        for h in range(freq_count):
            for t in range(tile_count):
                route.append((h * tile_count + t, (h + d) % freq_count * tile_count + (t + distance) % tile_count))
        return lax.ppermute(block, ("freq", "tile"), route)

    keep_sub, send_sub = side * n_sub, (1 - side) * n_sub
    *pieces, power = prepare(spectra, seg_mask, send_sub, 1, (SHORT, SUB - SHORT))
    send_power, counts = [power], [2]
    if n_sub > 1:
        piece, power = prepare(spectra, seg_mask, send_sub + 1, 1, (SUB,))
        pieces.append(piece)
        send_power.append(power)
        counts.append(1)
    far = [lax.ppermute(piece, "tile", across) for piece in pieces]
    rest, far[0] = lax.optimization_barrier((spectra, far[0]))
    pieces = []
    for i in range(2, n_sub):
        *both, power = prepare(rest, seg_mask, send_sub + i, 1, (SUB // 2, SUB // 2))
        rest, both = lax.optimization_barrier((rest, both))
        pieces += both
        send_power.append(power)
        counts.append(2)
    own, own_power = prepare(rest, seg_mask, keep_sub, n_sub, (half,))
    send_power = jnp.concatenate(send_power, axis=0)

    total = lax.psum(jnp.sum(own_power, axis=0) + jnp.sum(send_power, axis=0), "freq")
    lift = WATER * (total / F)[None, :]
    own_inv = (1.0 / ((own_power + lift) * seg)).T
    local = jnp.arange(half, dtype=jnp.int32)
    lag_cols = []
    for mine in (True, False):
        for d in range(freq_count):
            freqs = (me - d) % freq_count * band + (keep_from if mine else send_from) + local
            cos_tab, sin_tab = dft_tables(freqs)
            lag_cols.append(jnp.concatenate([cos_tab, sin_tab], axis=0))
            lag_cols.append(jnp.concatenate([-sin_tab, cos_tab], axis=0))
    lag_table = jnp.concatenate(lag_cols, axis=1)
    cos_tab, sin_tab = dft_tables(jnp.arange(F, dtype=jnp.int32))
    back_table = jnp.concatenate([cos_tab, -sin_tab], axis=1).T

    far_total = None
    for i, piece in enumerate(pieces):
        if i == 0:
            shape = piece.shape
            piece, terms, own_inv, lag_table, back_table = lax.optimization_barrier(
                (piece, exact_terms(total), own_inv, lag_table, back_table)
            )
            piece = jnp.concatenate([piece.reshape(-1, block), terms], axis=0)
        if i >= 2:
            piece, far[i - 1] = lax.optimization_barrier((piece, far[i - 1]))
        got = lax.ppermute(piece, "tile", across)
        if i == 0:
            far_total = jnp.sum(got[-SUB:].astype(jnp.float32), axis=0)
            got = got[:-SUB].reshape(shape)
        far.append(got)
    if far_total is None:
        far_total = lax.ppermute(total, "tile", across)
    far_lift = WATER * (far_total / F)[None, :]

    n_split = groups // 2 if n_sub > 1 else 0
    full = groups * SUB
    early_rows = n_split * SUB
    first_parts = [(j * SUB, SUB, "early") for j in range(n_split)]
    late_parts = [(0, early_rows, "late")] if n_split else []
    own_rest = [(early_rows, full - early_rows, "all")]
    halves = [(row, SUB // 2, "all") for row in range(early_rows, full, SUB // 2)] if groups > 1 else own_rest
    places = [first_parts + late_parts + (own_rest if k < freq_count else halves) for k in range(2 * freq_count)]
    slots = [(k, *place) for k in range(2 * freq_count) for place in places[k]]
    me_arr = me.astype(jnp.int32).reshape(1)
    ready = max(sum(counts[:-1]) - 1, 0)
    far[ready], lag_table, back_table, own_inv, far_lift, own = lax.optimization_barrier(
        (far[ready], lag_table, back_table, own_inv, far_lift, own)
    )
    far = [far[sum(counts[:i]) : sum(counts[: i + 1])] for i in range(n_sub)]
    made = {}
    for i in range(n_sub):
        made = cross_piece(i, freq_count, groups, slots, me_arr, own, far[i], own_inv, far_lift, made)

    arrived = {}

    def send(place, wait_for=None):
        kinds = [k for k in range(1, 2 * freq_count) if place in places[k]]
        outgoing = [made[(k, *place)] for k in kinds]
        if wait_for is not None:
            outgoing, arrived[wait_for] = lax.optimization_barrier((outgoing, arrived[wait_for]))
        if wait_for is not None and place == halves[-1]:
            outgoing, state["out"] = lax.optimization_barrier((outgoing, state["out"]))
        moves = [moved(x, k % freq_count, half_axis * (k // freq_count)) for k, x in zip(kinds, outgoing)]
        arrived[place] = dict(zip(kinds, moves))

    def transform(place):
        first_row, rows, _ = place
        sources = []
        for k in range(2 * freq_count):
            holds = [hold for hold in places[k] if hold[0] <= first_row < hold[0] + hold[1]]
            sources.append([(arrived[hold][k] if k else made[(0, *hold)], first_row - hold[0]) for hold in holds])
        group, ends = first_row // SUB, (first_row + rows) % SUB == 0
        before = state["out"] if ends else []
        done = lag_group(rows, group, groups, lag_table, back_table, sources, state["given"], before, to_output=ends)
        state["given" if not ends else "out"] = [done]
        if ends:
            state["given"] = []

    state = {"given": [], "out": []}
    for place in first_parts + late_parts:
        send(place)
    if own_rest != halves:
        send(own_rest[0])
    chain = first_parts + late_parts + halves
    for n, place in enumerate(halves, start=len(chain) - len(halves)):
        if place == halves[-1]:
            for part in first_parts:
                transform(part)
        send(place, chain[n - 2] if n >= 2 else None)
    for place in halves:
        if place in halves[-2:-1]:
            arrived[place], state["out"] = lax.optimization_barrier((arrived[place], state["out"]))
        transform(place)
    out = state["out"]
    return out[0]


def solution(mesh):
    placed = (P(None, None, "freq", "tile"), P(None, "tile"))
    return jax.shard_map(
        shards,
        mesh=mesh,
        in_specs=placed,
        out_specs=P("tile", None, None, "freq", None),
        check_vma=False,
    )
```

```python
import functools
import math

import jax
import jax.numpy as jnp
from jax import lax
from jax.experimental import pallas as pl
from jax.experimental.pallas import tpu as pltpu
from jax.sharding import PartitionSpec as P

F = 256
LAGS = 512
WATER = 0.05
SUB = 16
SHORT = 4
AT_ONCE = 8
PARTS = 8
SLICE = 16
VMEM_BYTES = 28 * 2**20
PREPARE_BYTES = 46 * 2**20
NO_COST = pl.CostEstimate(flops=0, bytes_accessed=0, transcendentals=0)


def dft_tables(freq_index):
    lag_index = jnp.arange(LAGS, dtype=jnp.int32)[:, None]
    phase = (lag_index * freq_index[None, :] % LAGS).astype(jnp.float32) * (2.0 * math.pi / LAGS)
    return jnp.cos(phase).astype(jnp.bfloat16), jnp.sin(phase).astype(jnp.bfloat16)


def rounded(x):
    return x.astype(jnp.bfloat16).astype(jnp.float32)


def interleave():
    row = lax.broadcasted_iota(jnp.int32, (SUB * SUB, SUB * SUB), 0)
    col = lax.broadcasted_iota(jnp.int32, (SUB * SUB, SUB * SUB), 1)
    return jnp.where(col == row % SUB * SUB + row // SUB, 1.0, 0.0).astype(jnp.bfloat16)


def turned_rows(matrix, left, right):
    lanes = left.shape[2]
    both = jnp.concatenate([left.reshape(SUB * SUB, lanes), right.reshape(SUB * SUB, lanes)], axis=1)
    return jnp.dot(matrix, both, preferred_element_type=jnp.float32).reshape(SUB, SUB, 2 * lanes)


def prepare_kernel(at_ref, x_ref, mask_ref, *outs):
    parts, power_ref = outs[:-1], outs[-1]
    seg, lanes = mask_ref.shape
    matrix = interleave()
    total = jnp.zeros((SUB, 8, lanes), jnp.float32)
    for s in range(0, seg, SUB):
        mask = mask_ref[s : s + SUB].astype(jnp.float32)[None]
        turned = turned_rows(matrix, x_ref[0, s : s + SUB], x_ref[1, s : s + SUB])
        for part in range(2):
            val = turned[:, :, part * lanes : (part + 1) * lanes] * mask
            square = val * val
            total += square[:, :8] + square[:, 8:]
            at = 0
            for out in parts:
                count = out.shape[0]
                out[:, part, s : s + SUB] = val[at : at + count].astype(jnp.bfloat16)
                at += count
    power_ref[...] = jnp.sum(total, axis=1) * (1.0 / seg) + 1e-05


def prepare(spectra, seg_mask, first, steps, counts):
    _, seg, _, block = spectra.shape
    assert sum(counts) == steps * SUB and (steps == 1 or len(counts) == 1)
    out_specs = [pl.BlockSpec((min(count, SUB), 2, seg, block), lambda i, at: (i, 0, 0, 0)) for count in counts]
    out_shape = [jax.ShapeDtypeStruct((count, 2, seg, block), jnp.bfloat16) for count in counts]
    if steps > 1:
        out_shape = [pltpu.HBM(x.shape, x.dtype) for x in out_shape]
    return pl.pallas_call(
        prepare_kernel,
        grid_spec=pltpu.PrefetchScalarGridSpec(
            num_scalar_prefetch=1,
            grid=(steps,),
            in_specs=[
                pl.BlockSpec((2, seg, SUB, block), lambda i, at: (0, 0, at[0] + i, 0)),
                pl.BlockSpec((seg, block), lambda i, at: (0, 0)),
            ],
            out_specs=out_specs + [pl.BlockSpec((SUB, block), lambda i, at: (i, 0))],
        ),
        out_shape=out_shape + [jax.ShapeDtypeStruct((steps * SUB, block), jnp.float32)],
        compiler_params=pltpu.CompilerParams(vmem_limit_bytes=PREPARE_BYTES),
        cost_estimate=NO_COST,
        name="prepare",
    )(first.astype(jnp.int32).reshape(1), spectra, seg_mask)


def exact_terms(x):
    terms, rest = [], x
    for _ in range(3):
        terms.append(lax.reduce_precision(rest, 8, 7))
        rest = rest - terms[-1]
    return jnp.pad(jnp.stack(terms).astype(jnp.bfloat16), ((0, SUB - 3), (0, 0)))


def cross_kernel(piece, freq_count, groups, slots, held, n_far, me_ref, own_ref, own_inv_ref, far_lift_ref, *refs):
    far_refs, outs, (own_scr, far_scr) = refs[:n_far], refs[n_far + held : -2], refs[-2:]
    seg = own_ref.shape[2]
    block = own_ref.shape[3]
    far_rows = [(far_ref, k) for far_ref in far_refs for k in range(far_ref.shape[0])]
    for f in range(SUB):
        own = own_ref[f].reshape(2 * seg, block)
        far_ref, k = far_rows[f]
        far_re, far_im = far_ref[k, 0], far_ref[k, 1]
        cols = jnp.concatenate(
            [jnp.concatenate([far_re, far_im], axis=0), jnp.concatenate([far_im, -far_re], axis=0)], axis=1
        )
        cross = lax.dot_general(own, cols, (((0,), (0,)), ((), ())), preferred_element_type=jnp.float32)
        at = piece * SUB + f
        own_inv = own_inv_ref[:, at : at + 1]
        square = jnp.square(far_re.astype(jnp.float32)) + jnp.square(far_im.astype(jnp.float32))
        far_power = jnp.sum(square, axis=0, keepdims=True) * (1.0 / seg) + 1e-05
        far_inv = 1.0 / ((far_power + far_lift_ref[...]) * seg)
        for part in range(2):
            val = cross[:, part * block : (part + 1) * block]
            sym = 0.5 * (rounded(val * own_inv) + rounded(val * far_inv))
            own_scr[part, f] = sym.astype(jnp.bfloat16)
            turned = jnp.transpose(sym if part == 0 else -sym)
            far_scr[part, f] = turned.astype(jnp.bfloat16)
    me = me_ref[0]
    matrix = interleave()
    for k in range(2 * freq_count):
        scr = own_scr if k < freq_count else far_scr
        for j in range(groups):
            first = (lax.rem(me + k % freq_count, freq_count) * groups + j) * SUB
            rows = pl.ds(pl.multiple_of(first, SUB), SUB)
            turned = turned_rows(matrix, scr[0, :, rows, :], scr[1, :, rows, :])
            for out, (kind, first_row, count, _) in zip(outs, slots):
                low, high = max(first_row, j * SUB), min(first_row + count, (j + 1) * SUB)
                if kind != k or low >= high:
                    continue
                for part in range(2):
                    vals = turned[low - j * SUB : high - j * SUB, :, part * block : (part + 1) * block]
                    out[low - first_row : high - first_row, part] = vals.astype(jnp.bfloat16)


def cross_piece(piece, freq_count, groups, slots, me, own, far, own_inv, far_lift, made):
    half, _, seg, block = own.shape
    n_far = len(far)
    last = (piece + 1) * SUB == half
    slots = [slot for slot in slots if slot[3] == "all" or (slot[3] == "late") == last]
    counts = {"all": half, "early": half - SUB, "late": SUB}
    places = [0 if slot[3] == "late" else piece for slot in slots]
    spots = [n for n, slot in enumerate(slots) if slot in made]
    flat = pl.pallas_call(
        functools.partial(cross_kernel, piece, freq_count, groups, slots, len(spots), n_far),
        grid=(1,),
        in_specs=[
            pl.BlockSpec(memory_space=pltpu.SMEM),
            pl.BlockSpec((SUB, 2, seg, block), lambda i: (piece, 0, 0, 0)),
            pl.BlockSpec((block, half), lambda i: (0, 0)),
            pl.BlockSpec((1, block), lambda i: (0, 0)),
        ]
        + [pl.BlockSpec(x.shape, lambda i: (0, 0, 0, 0)) for x in far]
        + [pl.BlockSpec(memory_space=pl.ANY)] * len(spots),
        out_specs=[
            pl.BlockSpec((slot[2], 2, SUB, block), functools.partial(lambda at, i: (0, 0, at, 0), at))
            for slot, at in zip(slots, places)
        ],
        out_shape=[jax.ShapeDtypeStruct((slot[2], 2, counts[slot[3]], block), jnp.bfloat16) for slot in slots],
        scratch_shapes=[pltpu.VMEM((2, SUB, block, block), jnp.bfloat16)] * 2,
        input_output_aliases={4 + n_far + i: n for i, n in enumerate(spots)},
        compiler_params=pltpu.CompilerParams(vmem_limit_bytes=VMEM_BYTES),
        cost_estimate=pl.CostEstimate(
            flops=SUB * 8 * seg * block * block, bytes_accessed=SUB * 16 * seg * block, transcendentals=0
        ),
        name="cross_piece",
    )(me, own, own_inv, far_lift, *far, *[made[slots[n]] for n in spots])
    return {**made, **dict(zip(slots, flat))}


def lag_kernel(sources, rows, group, n_given, n_held, to_output, lag_ref, back_ref, *refs):
    n_pieces = sum(len(places) for places in sources)
    pieces, given = refs[:n_pieces], refs[n_pieces : n_pieces + n_given]
    out_ref, lag_scr, norm_scr, *rest = refs[n_pieces + n_given + n_held :]
    block = pieces[0].shape[3]
    width = AT_ONCE * block
    row_ref = rest[0] if to_output else out_ref
    first = SUB - rows if to_output else 0

    def column(r):
        parts, at = [], 0
        for places in sources:
            for part in range(2):
                parts += [piece[place + r, part] for piece, place in zip(pieces[at:], places)]
            at += len(places)
        return jnp.concatenate(parts, axis=0)

    for r in range(0, rows, AT_ONCE):
        cols = jnp.concatenate([column(r + k) for k in range(AT_ONCE)], axis=1)
        lag_scr[...] = jnp.dot(lag_ref[...], cols, preferred_element_type=jnp.float32)
        total = jnp.zeros((8, width), jnp.float32)
        for at in range(0, LAGS, SLICE):
            lag_re, lag_im = lag_scr[at : at + SLICE], lag_scr[LAGS + at : LAGS + at + SLICE]
            energy = lag_re * lag_re + lag_im * lag_im
            lag_scr[LAGS + at : LAGS + at + SLICE] = energy
            total += jnp.sum(energy.reshape(SLICE // 8, 8, width), axis=0)
        floor = (0.25 / LAGS) * jnp.sum(total, axis=0, keepdims=True) + 1e-05
        for at in range(0, LAGS, SLICE):
            scale = lax.rsqrt(lag_scr[LAGS + at : LAGS + at + SLICE] + floor)
            norm_scr[at : at + SLICE] = (lag_scr[at : at + SLICE] * scale).astype(jnp.bfloat16)
        lag_scr[: 2 * F] = jnp.dot(back_ref[...], norm_scr[...], preferred_element_type=jnp.float32)
        for at in range(0, 2 * F, SLICE):
            back = (lag_scr[at : at + SLICE] * (1.0 / math.sqrt(LAGS))).astype(jnp.bfloat16)
            for k in range(AT_ONCE):
                row_ref[first + r + k, at : at + SLICE] = back[:, k * block : (k + 1) * block]
    if to_output:
        _, bins_ref, sems = rest
        matrix = interleave()
        copies = []
        chunk = 2 * F // PARTS
        for at in range(0, 2 * F, 2 * SUB):
            whole = [x[:, at : at + 2 * SUB] for x in given] + [row_ref[first:, at : at + 2 * SUB]]
            whole = jnp.concatenate(whole, axis=0)
            turned = turned_rows(matrix, whole[:, :SUB], whole[:, SUB:])
            for n in range(2):
                bins = turned[:, :, n * block : (n + 1) * block]
                bins_ref[at + n * SUB : at + (n + 1) * SUB] = bins.astype(jnp.bfloat16)
            if (at + 2 * SUB) % chunk == 0:
                start = at + 2 * SUB - chunk
                there = out_ref.at[0, start // F, pl.ds(start % F, chunk), pl.ds(group * SUB, SUB)]
                copies.append(pltpu.make_async_copy(bins_ref.at[pl.ds(start, chunk)], there, sems.at[start // chunk]))
                copies[-1].start()
        for copy in copies:
            copy.wait()


def lag_group(rows, group, groups, lag_table, back_table, sources, given, before, to_output=True):
    pieces = [piece for source in sources for piece, _ in source]
    places = [[place for _, place in source] for source in sources]
    block = pieces[0].shape[3]
    vmem, scratch = pl.BlockSpec(memory_space=pltpu.VMEM), [
        pltpu.VMEM((2 * LAGS, AT_ONCE * block), jnp.float32),
        pltpu.VMEM((LAGS, AT_ONCE * block), jnp.bfloat16),
    ]
    if to_output:
        out_spec = pl.BlockSpec(memory_space=pltpu.HBM)
        out_shape = jax.ShapeDtypeStruct((1, 2, F, SUB * groups, block), jnp.bfloat16)
        scratch += [
            pltpu.VMEM((SUB, 2 * F, block), jnp.bfloat16),
            pltpu.VMEM((2 * F, SUB, block), jnp.bfloat16),
            pltpu.SemaphoreType.DMA((PARTS,)),
        ]
    else:
        out_spec = vmem
        out_shape = jax.ShapeDtypeStruct((rows, 2 * F, block), jnp.bfloat16)
    return pl.pallas_call(
        functools.partial(lag_kernel, places, rows, group, len(given), len(before), to_output),
        in_specs=[vmem] * (2 + len(pieces) + len(given)) + [pl.BlockSpec(memory_space=pltpu.HBM)] * len(before),
        out_specs=out_spec,
        out_shape=out_shape,
        scratch_shapes=scratch,
        input_output_aliases={2 + len(pieces) + len(given): 0} if before else {},
        compiler_params=pltpu.CompilerParams(vmem_limit_bytes=VMEM_BYTES),
        cost_estimate=NO_COST,
        name="lag_group",
    )(lag_table, back_table, *pieces, *given, *before)


def shards(spectra, seg_mask):
    tile_count, freq_count = lax.axis_size("tile"), lax.axis_size("freq")
    half_axis = tile_count // 2
    _, seg, band, block = spectra.shape
    half = band // 2
    n_sub = half // SUB
    groups = block // freq_count // SUB
    me = lax.axis_index("freq")
    side = lax.axis_index("tile") // half_axis
    keep_from, send_from = side * half, (1 - side) * half

    across = [(t, (t + half_axis) % tile_count) for t in range(tile_count)]

    def moved(block, d, distance):
        route = []
        for h in range(freq_count):
            for t in range(tile_count):
                route.append((h * tile_count + t, (h + d) % freq_count * tile_count + (t + distance) % tile_count))
        return lax.ppermute(block, ("freq", "tile"), route)

    keep_sub, send_sub = side * n_sub, (1 - side) * n_sub
    *pieces, power = prepare(spectra, seg_mask, send_sub, 1, (SHORT, SUB - SHORT))
    send_power, counts = [power], [2]
    if n_sub > 1:
        piece, power = prepare(spectra, seg_mask, send_sub + 1, 1, (SUB,))
        pieces.append(piece)
        send_power.append(power)
        counts.append(1)
    far = [lax.ppermute(piece, "tile", across) for piece in pieces]
    rest, far[0] = lax.optimization_barrier((spectra, far[0]))
    pieces = []
    for i in range(2, n_sub):
        *both, power = prepare(rest, seg_mask, send_sub + i, 1, (SUB // 2, SUB // 2))
        rest, both = lax.optimization_barrier((rest, both))
        pieces += both
        send_power.append(power)
        counts.append(2)
    own, own_power = prepare(rest, seg_mask, keep_sub, n_sub, (half,))
    send_power = jnp.concatenate(send_power, axis=0)

    total = lax.psum(jnp.sum(own_power, axis=0) + jnp.sum(send_power, axis=0), "freq")
    lift = WATER * (total / F)[None, :]
    own_inv = (1.0 / ((own_power + lift) * seg)).T
    local = jnp.arange(half, dtype=jnp.int32)
    lag_cols = []
    for mine in (True, False):
        for d in range(freq_count):
            freqs = (me - d) % freq_count * band + (keep_from if mine else send_from) + local
            cos_tab, sin_tab = dft_tables(freqs)
            lag_cols.append(jnp.concatenate([cos_tab, sin_tab], axis=0))
            lag_cols.append(jnp.concatenate([-sin_tab, cos_tab], axis=0))
    lag_table = jnp.concatenate(lag_cols, axis=1)
    cos_tab, sin_tab = dft_tables(jnp.arange(F, dtype=jnp.int32))
    back_table = jnp.concatenate([cos_tab, -sin_tab], axis=1).T

    far_total = None
    for i, piece in enumerate(pieces):
        if i == 0:
            shape = piece.shape
            piece, terms, own_inv, lag_table, back_table = lax.optimization_barrier(
                (piece, exact_terms(total), own_inv, lag_table, back_table)
            )
            piece = jnp.concatenate([piece.reshape(-1, block), terms], axis=0)
        if i >= 2:
            piece, far[i - 1] = lax.optimization_barrier((piece, far[i - 1]))
        got = lax.ppermute(piece, "tile", across)
        if i == 0:
            far_total = jnp.sum(got[-SUB:].astype(jnp.float32), axis=0)
            got = got[:-SUB].reshape(shape)
        far.append(got)
    if far_total is None:
        far_total = lax.ppermute(total, "tile", across)
    far_lift = WATER * (far_total / F)[None, :]

    n_split = groups // 2 if n_sub > 1 else 0
    full = groups * SUB
    early_rows = n_split * SUB
    first_parts = [(j * SUB, SUB, "early") for j in range(n_split)]
    late_parts = [(0, early_rows, "late")] if n_split else []
    own_rest = [(early_rows, full - early_rows, "all")]
    halves = [(row, SUB // 2, "all") for row in range(early_rows, full, SUB // 2)] if groups > 1 else own_rest
    places = [first_parts + late_parts + (own_rest if k < freq_count else halves) for k in range(2 * freq_count)]
    slots = [(k, *place) for k in range(2 * freq_count) for place in places[k]]
    me_arr = me.astype(jnp.int32).reshape(1)
    ready = max(sum(counts[:-1]) - 1, 0)
    far[ready], lag_table, back_table, own_inv, far_lift, own = lax.optimization_barrier(
        (far[ready], lag_table, back_table, own_inv, far_lift, own)
    )
    far = [far[sum(counts[:i]) : sum(counts[: i + 1])] for i in range(n_sub)]
    made = {}
    for i in range(n_sub):
        made = cross_piece(i, freq_count, groups, slots, me_arr, own, far[i], own_inv, far_lift, made)

    arrived = {}

    def send(place, wait_for=None):
        kinds = [k for k in range(1, 2 * freq_count) if place in places[k]]
        outgoing = [made[(k, *place)] for k in kinds]
        if wait_for is not None:
            outgoing, arrived[wait_for] = lax.optimization_barrier((outgoing, arrived[wait_for]))
        if wait_for is not None and place == halves[-1]:
            outgoing, state["out"] = lax.optimization_barrier((outgoing, state["out"]))
        moves = [moved(x, k % freq_count, half_axis * (k // freq_count)) for k, x in zip(kinds, outgoing)]
        arrived[place] = dict(zip(kinds, moves))

    def transform(place):
        first_row, rows, _ = place
        sources = []
        for k in range(2 * freq_count):
            holds = [hold for hold in places[k] if hold[0] <= first_row < hold[0] + hold[1]]
            sources.append([(arrived[hold][k] if k else made[(0, *hold)], first_row - hold[0]) for hold in holds])
        group, ends = first_row // SUB, (first_row + rows) % SUB == 0
        before = state["out"] if ends else []
        done = lag_group(rows, group, groups, lag_table, back_table, sources, state["given"], before, to_output=ends)
        state["given" if not ends else "out"] = [done]
        if ends:
            state["given"] = []

    state = {"given": [], "out": []}
    for place in first_parts + late_parts:
        send(place)
    if own_rest != halves:
        send(own_rest[0])
    chain = first_parts + late_parts + halves
    for n, place in enumerate(halves, start=len(chain) - len(halves)):
        if place == halves[-1]:
            for part in first_parts:
                transform(part)
        send(place, chain[n - 2] if n >= 2 else None)
    for place in halves:
        if place in halves[-2:-1]:
            arrived[place], state["out"] = lax.optimization_barrier((arrived[place], state["out"]))
        transform(place)
    out = state["out"]
    return out[0]


def solution(mesh):
    placed = (P(None, None, "freq", "tile"), P(None, "tile"))
    return jax.shard_map(
        shards,
        mesh=mesh,
        in_specs=placed,
        out_specs=P("tile", None, None, "freq", None),
        check_vma=False,
    )
```
